32 devices in a mesh: gx: 2 (over y), gy: 4 (over x, core), gz: 4 (over z).
Axes of the slice: x: 2, y: 2, z: 4, core: 2. Of those that a mesh axis runs over, the one named last changes fastest.
Arguments:
- initial_warmth: float32 [128, 512, 1024], P('gx', 'gy', 'gz'), may hold values from -6 to 6
- heat_supply: float32 [128, 512, 1024], P('gx', 'gy', 'gz'), may hold values from -82944 to 82946
Outputs:
- updated: float32 [128, 512, 1024], P('gx', 'gy', 'gz')
The draws below stay inside these ranges and needn't reach their ends.
All inputs are finite; a program needn't handle non-finite values.
Results may differ from the reference program's by a relative error of at most 0.0009.
Values sent between devices are 32-bit elements; how exact they have to be, the bound alone decides.
No kernel may reach another device: no remote copies, remote signals or barrier semaphores. Data moves between devices by JAX's collectives and lax.ppermute only.
A program may use at most 128 MiB of HBM per device.

```python
import jax
import jax.numpy as jnp
from jax import lax

MESH_COUNT_EAST = 128
MESH_COUNT_NORTH = 512
MESH_COUNT_UPWARD = 1024
RX = 4096
RY = 65536
RZ = 262144


def draw_heat_supply(key, part):
    first_key = jax.random.fold_in(key, 11)
    second_key = jax.random.fold_in(key, 12)
    base_values = jax.random.uniform(first_key, (MESH_COUNT_EAST, MESH_COUNT_NORTH, MESH_COUNT_UPWARD), jnp.float32, -1.0, 1.0)
    spread_values = jax.random.uniform(second_key, (MESH_COUNT_EAST, MESH_COUNT_NORTH, MESH_COUNT_UPWARD), jnp.float32, 0.5, 2.0)
    result = base_values * spread_values * ((RX + RY + RZ) // 8)
    return result


def levels(own_key, shape, split, low, top_value):
    def one(position, blocks):
        draws = jax.random.uniform(jax.random.fold_in(jax.random.fold_in(own_key, 6), position), (blocks,), jnp.float32, low / len(split), top_value / len(split))
        return jnp.repeat(jnp.exp(draws), shape[position] // blocks).reshape((-1,) + (1,) * (len(shape) - position - 1))

    level = one(*split[0])
    for cut in split[1:]:
        level = level * one(*cut)
    return level


def bell_draw(rng, shape, spread, limit, split=(), held_as=jnp.bfloat16):
    array = spread * jax.random.normal(rng, shape, jnp.float32)
    if split:
        array = array * levels(rng, shape, split, -0.22, 0.18)
    return jnp.clip(array, -limit, limit).astype(held_as)


def setup_inputs(seed: int = 0) -> dict:
    splits = jax.random.split(jax.random.key(seed), 3)
    return {
        "initial_warmth": bell_draw(splits[0], (MESH_COUNT_EAST, MESH_COUNT_NORTH, MESH_COUNT_UPWARD), 1.0, 6.0, ((0, 2), (1, 4), (2, 4)), jnp.float32),
        "heat_supply": draw_heat_supply(jax.random.fold_in(splits[2], 71), 0),
    }


def line_solve(values, factor, axis_pos):
    moved_axis = jnp.moveaxis(values, axis_pos, -2)
    length = moved_axis.shape[-2]
    leading = moved_axis.shape[:-2]
    diagonal = jnp.full(leading + (length,), 1.0 + factor, dtype=jnp.float32)
    sideband = jnp.full(leading + (length,), -0.5 * factor, dtype=jnp.float32)
    lower_band = sideband.at[..., 0].set(0.0)
    upper_band = sideband.at[..., length - 1].set(0.0)
    solved = lax.linalg.tridiagonal_solve(lower_band, diagonal, upper_band, moved_axis)
    return jnp.moveaxis(solved, -2, axis_pos)

def reference(initial_warmth, heat_supply):
    bordered_grid = jnp.pad(initial_warmth, 1)
    coefficient_east = RX * 1.0
    coefficient_north = RY * 1.0
    coefficient_upward = RZ * 1.0
    forward_increment = coefficient_east * (bordered_grid[2:, 1:-1, 1:-1] - 2.0 * initial_warmth + bordered_grid[:-2, 1:-1, 1:-1])
    forward_increment = forward_increment + coefficient_north * (bordered_grid[1:-1, 2:, 1:-1] - 2.0 * initial_warmth + bordered_grid[1:-1, :-2, 1:-1])
    forward_increment = forward_increment + coefficient_upward * (bordered_grid[1:-1, 1:-1, 2:] - 2.0 * initial_warmth + bordered_grid[1:-1, 1:-1, :-2])
    forward_increment = forward_increment + heat_supply
    section_one = line_solve(forward_increment, coefficient_east, 0)
    section_two = line_solve(section_one, coefficient_north, 1)
    upward_portion = line_solve(section_two, coefficient_upward, 2)
    return initial_warmth + upward_portion
```

```python
import functools

import jax
import jax.numpy as jnp
import numpy as np
from jax import lax
from jax.experimental import pallas as pl
from jax.experimental.pallas import tpu as pltpu
from jax.sharding import PartitionSpec as P

F32 = jnp.float32
BF16 = jnp.bfloat16
MIB = 1 << 20


def line_tables(length, factor):
    matrix = (1.0 + factor) * np.eye(length)
    matrix -= 0.5 * factor * (np.eye(length, k=1) + np.eye(length, k=-1))
    inverse = np.linalg.inv(matrix)
    inverse = 0.5 * (inverse + inverse.T)
    return inverse, 0.5 * factor * inverse[:, 0], 0.5 * factor * inverse[:, -1]


def interface_table(before, after, members):
    near, far = before[0], before[-1]
    system = np.eye(2 * members)
    for m in range(members):
        if m > 0:
            system[2 * m, 2 * m - 1] -= near
            system[2 * m + 1, 2 * m - 1] -= far
        if m < members - 1:
            system[2 * m, 2 * m + 2] -= far
            system[2 * m + 1, 2 * m + 2] -= near
    solved = np.linalg.inv(system)
    rows = np.zeros((members, 2, 2 * members))
    for m in range(members):
        if m > 0:
            rows[m, 0] = solved[2 * m - 1]
        if m < members - 1:
            rows[m, 1] = solved[2 * m + 2]
    return rows


def sweep_table(length, factor):
    half = 0.5 * factor
    ratio = np.zeros(length)
    scale = np.zeros(length)
    last = 0.0
    for i in range(length):
        scale[i] = 1.0 / (1.0 + factor - half * last)
        ratio[i] = last = half * scale[i]
    head = np.concatenate([[1.0], np.cumprod(ratio)[:-1]])
    return np.stack([scale, ratio, head, np.cumprod(ratio)])


def split(table):
    high = np.asarray(table, np.float32).astype(BF16)
    low = (np.asarray(table, np.float64) - high.astype(np.float64)).astype(BF16)
    return high, low


def parts(values):
    high = values.astype(BF16)
    return high, (values - high.astype(F32)).astype(BF16)


def dot(a, b):
    return jnp.dot(a, b, preferred_element_type=F32)


def exact_dot(a, b):
    return jnp.dot(a, b, precision=lax.Precision.HIGHEST, preferred_element_type=F32)


def local_kernel(
    group,
    sweep_ref, upward_high_ref, upward_low_ref, north_ref, warmth_hbm, supply_hbm,
    swept_ref, rest_ref, upward_ends_ref, north_ends_ref, east_ends_ref,
    warmth_ref, supply_ref, sems,
):
    east, north, upward = warmth_ref.shape
    groups = east // group
    copies = []
    for g in range(groups):
        block = pl.ds(g * group, group)
        copies.append((
            pltpu.make_async_copy(warmth_hbm.at[block], warmth_ref.at[block], sems.at[0, g]),
            pltpu.make_async_copy(supply_hbm.at[block], supply_ref.at[block], sems.at[1, g]),
        ))
    for pair in copies:
        for copy in pair:
            copy.start()
    upward_ends_ref[...] = jnp.zeros_like(upward_ends_ref)
    east_ends_ref[...] = jnp.zeros_like(east_ends_ref)
    lane = lax.broadcasted_iota(jnp.int32, (1, 2 * east), 1)

    def body(g, _):
        block = pl.ds(pl.multiple_of(g * group, group), group)
        for which, (hbm, ref) in enumerate(((warmth_hbm, warmth_ref), (supply_hbm, supply_ref))):
            pltpu.make_async_copy(hbm.at[block], ref.at[block], sems.at[which, g]).wait()
        warmth = warmth_ref[block]
        flat = (group * north, upward)
        heat = jnp.reshape(supply_ref[block] + 6.0 * warmth, flat)
        heat_high, heat_low = parts(heat)
        warm_high, warm_low = parts(jnp.reshape(warmth, flat))
        upward_high, upward_low = upward_high_ref[...], upward_low_ref[...]
        heat_up = dot(heat_high, upward_high) + dot(heat_low, upward_high) + dot(heat_high, upward_low)
        warm_up = dot(warm_high, upward_high) + dot(warm_low, upward_high)
        for k in range(group):
            i = g * group + k
            rows = slice(k * north, (k + 1) * north)
            first, second = heat_up[rows], warm_up[rows]
            warm = warmth[k]
            for field, value in enumerate((first, second)):
                half = upward // 2
                both = jnp.where(lane < east, value[:, : 2 * east], value[:, upward - 2 * east :])
                turned = pltpu.roll(both, 2 * i + 1, 1)
                own = (lane == 2 * i) | (lane == 2 * i + 1)
                upward_ends_ref[field] = jnp.where(own, turned, upward_ends_ref[field])
            first_high, first_low = parts(first - 2.0 * warm)
            second_high, second_low = parts(second)
            north_one = dot(north_ref[...], jnp.concatenate([first_high, first_low], axis=0))
            north_one = north_one[:north] + north_one[north:]
            north_two = dot(north_ref[:north], jnp.concatenate([second_high, second_low], axis=0))
            for field, value in enumerate((north_one, north_two)):
                north_ends_ref[field, 0, pl.ds(i, 1), :] = value[:1]
                north_ends_ref[field, 1, pl.ds(i, 1), :] = value[north - 1 :]
            rest_ref[i] = warm - 2.0 * north_two
            source = sweep_ref[0, i] * (north_one - 2.0 * second)
            swept = source + sweep_ref[1, i] * east_ends_ref[1]
            swept_ref[i] = swept
            east_ends_ref[1] = swept
            east_ends_ref[0] += sweep_ref[2, i] * swept
        return 0

    lax.fori_loop(0, groups, body, 0)


def upward_kernel(
    axis, members,
    table_ref, gathered_ref, north_ends_ref, east_ends_ref, north_inverse_ref, east_twice_ref, spikes_ref, spread_ref,
    columns_ref, north_out_ref, east_out_ref,
):
    me = lax.axis_index(axis)
    north, lanes = columns_ref.shape
    east = lanes // 2
    even = lax.broadcasted_iota(jnp.int32, (1, lanes), 1) % 2 == 0
    fields = []
    for field in range(2):
        same = jnp.zeros((north, lanes), F32)
        cross = jnp.zeros((north, lanes), F32)
        for m in range(members):
            ends = gathered_ref[m, field]
            before_head, before_tail = table_ref[me, 2 * m], table_ref[me, 2 * m + 1]
            after_head = table_ref[me, 2 * members + 2 * m]
            after_tail = table_ref[me, 2 * members + 2 * m + 1]
            same += ends * jnp.where(even, before_tail, after_head)
            cross += ends * jnp.where(even, after_tail, before_head)
        fields.append(same + jnp.where(even, pltpu.roll(cross, lanes - 1, 1), pltpu.roll(cross, 1, 1)))
    heat_side, warm_side = fields
    solved = exact_dot(north_inverse_ref[...], jnp.concatenate(fields, axis=1))
    heat_solved, warm_solved = solved[:, :lanes], solved[:, lanes:]
    swept = exact_dot(heat_solved - 2.0 * warm_side, east_twice_ref[...])
    columns_ref[...] = swept - 2.0 * warm_solved
    place = lax.broadcasted_iota(jnp.int32, (east, lanes), 1) // 2
    own = place == lax.broadcasted_iota(jnp.int32, (east, lanes), 0)
    picked = []
    for value in (heat_solved, warm_solved):
        for row in (value[:1], value[north - 1 :]):
            picked.append(jnp.where(own, row, 0.0))
    added = exact_dot(jnp.concatenate(picked, axis=0), spread_ref[...])
    for k in range(4):
        north_out_ref[k // 2, k % 2] = north_ends_ref[k // 2, k % 2] + added[k * east : (k + 1) * east]
    for end, start in ((0, 0), (1, lanes - 2)):
        east_out_ref[end] = (
            east_ends_ref[end]
            + swept[:, start : start + 1] * spikes_ref[0:1, :]
            + swept[:, start + 1 : start + 2] * spikes_ref[1:2, :]
        )


def north_kernel(
    axis, members, east_axis, pair,
    table_ref, gathered_ref, east_ends_ref, east_inverse_ref, spikes_ref,
    rows_ref, east_out_ref,
):
    me = lax.axis_index(axis)
    east = rows_ref.shape[1]
    sides = []
    for field in range(2):
        for side in range(2):
            total = jnp.zeros(rows_ref.shape[1:], F32)
            for m in range(members):
                for end in range(2):
                    total += gathered_ref[m, field, end] * table_ref[me, side * 2 * members + 2 * m + end]
            sides.append(total)
    swept = [exact_dot(east_inverse_ref[...], sides[0]), exact_dot(east_inverse_ref[...], sides[1])]
    for side in range(2):
        rows_ref[side] = swept[side] - 2.0 * sides[2 + side]
    ends = []
    for end, row in ((0, 0), (1, east - 1)):
        ends.append(
            east_ends_ref[end]
            + spikes_ref[0] * swept[0][row : row + 1]
            + spikes_ref[1] * swept[1][row : row + 1]
        )
    if pair:
        east_out_ref[...] = jnp.where(lax.axis_index(east_axis) == 0, ends[1], ends[0])
    else:
        for end in range(2):
            east_out_ref[end] = ends[end]


def final_kernel(
    axis, members, pair, tile,
    table_ref, sweep_ref, own_ref, other_ref, swept_ref, rest_ref, columns_ref, rows_ref, upward_spikes_ref, north_spikes_ref,
    out_hbm,
    out_ref, sides_ref, sems,
):
    me = lax.axis_index(axis)
    east, north, upward = out_ref.shape
    if pair:
        value = table_ref[0, 0] * other_ref[...] + table_ref[0, 1] * own_ref[...]
        sides_ref[0] = jnp.where(me == 0, 0.0, value)
        sides_ref[1] = jnp.where(me == 0, value, 0.0)
    else:
        for side in range(2):
            total = jnp.zeros(sides_ref.shape[1:], F32)
            for m in range(members):
                for end in range(2):
                    total += other_ref[m, end] * table_ref[me, side * 2 * members + 2 * m + end]
            sides_ref[side] = total

    def send(t):
        block = pl.ds(pl.multiple_of(t * tile, tile), tile)
        return pltpu.make_async_copy(out_ref.at[:, block], out_hbm.at[:, block], sems.at[t])

    def body(t, _):
        block = pl.ds(pl.multiple_of(t * tile, tile), tile)
        before = sides_ref[0, block]
        value = sides_ref[1, block]
        columns = columns_ref[block]
        first_spike, last_spike = north_spikes_ref[0, block], north_spikes_ref[1, block]
        for i in reversed(range(east)):
            value = swept_ref[i, block] + sweep_ref[3, i] * before + sweep_ref[1, i] * value
            added = (
                columns[:, 2 * i : 2 * i + 1] * upward_spikes_ref[0:1, :]
                + columns[:, 2 * i + 1 : 2 * i + 2] * upward_spikes_ref[1:2, :]
            )
            added += first_spike * rows_ref[0, i : i + 1, :] + last_spike * rows_ref[1, i : i + 1, :]
            out_ref[i, block] = rest_ref[i, block] + value + added
        send(t).start()
        return 0

    lax.fori_loop(0, north // tile, body, 0)
    for t in range(north // tile):
        send(t).wait()


def local(initial_warmth, heat_supply):
    shape = east, north, upward = initial_warmth.shape
    members = [lax.axis_size(axis) for axis in ("gx", "gy", "gz")]
    factors = [float((n * m) ** 2 // 4) for n, m in zip(shape, members)]
    lines = [line_tables(n, factor) for n, factor in zip(shape, factors)]
    faces = [interface_table(line[1], line[2], m) for line, m in zip(lines, members)]
    faces = [table.reshape(m, 4 * m).astype(np.float32) for table, m in zip(faces, members)]
    sweep = sweep_table(east, factors[0]).astype(np.float32)
    upward_high, upward_low = split(lines[2][0])
    north_high, north_low = split(lines[1][0])
    north_stack = np.block([[north_high, north_high], [north_low, np.zeros_like(north_low)]])
    east_inverse = lines[0][0].astype(np.float32)
    north_inverse = lines[1][0].astype(np.float32)
    east_twice = np.kron(lines[0][0], np.eye(2)).astype(np.float32)
    upward_spikes = np.stack(lines[2][1:]).astype(np.float32)
    spread = np.tile(upward_spikes, (east, 1))
    north_spikes = np.broadcast_to(np.stack(lines[1][1:])[:, :, None], (2, north, upward)).astype(np.float32)

    vmem = pl.BlockSpec(memory_space=pltpu.VMEM)
    smem = pl.BlockSpec(memory_space=pltpu.SMEM)
    hbm = pl.BlockSpec(memory_space=pl.ANY)
    params = pltpu.CompilerParams(vmem_limit_bytes=40 * MIB)
    small = pltpu.CompilerParams(vmem_limit_bytes=16 * MIB)
    group = 4
    swept, rest, upward_ends, north_ends, east_ends = pl.pallas_call(
        functools.partial(local_kernel, group),
        in_specs=[smem, vmem, vmem, vmem, hbm, hbm],
        out_specs=[vmem] * 5,
        out_shape=[
            pltpu.VMEM(shape, F32),
            pltpu.VMEM(shape, F32),
            jax.ShapeDtypeStruct((2, north, 2 * east), F32),
            jax.ShapeDtypeStruct((2, 2, east, upward), F32),
            jax.ShapeDtypeStruct((2, north, upward), F32),
        ],
        scratch_shapes=[
            pltpu.VMEM(shape, F32),
            pltpu.VMEM(shape, F32),
            pltpu.SemaphoreType.DMA((2, east // group)),
        ],
        compiler_params=params,
    )(sweep, upward_high, upward_low, north_stack, initial_warmth, heat_supply)

    gathered = lax.all_gather(upward_ends, "gz")
    columns, north_ends, east_ends = pl.pallas_call(
        functools.partial(upward_kernel, "gz", members[2]),
        in_specs=[smem] + [vmem] * 7,
        out_specs=[vmem] * 3,
        out_shape=[
            jax.ShapeDtypeStruct((north, 2 * east), F32),
            jax.ShapeDtypeStruct(north_ends.shape, F32),
            jax.ShapeDtypeStruct(east_ends.shape, F32),
        ],
        compiler_params=small,
    )(faces[2], gathered, north_ends, east_ends, north_inverse, east_twice, upward_spikes, spread)

    pair = members[0] == 2
    gathered = lax.all_gather(north_ends, "gy")
    rows, own = pl.pallas_call(
        functools.partial(north_kernel, "gy", members[1], "gx", pair),
        in_specs=[smem] + [vmem] * 4,
        out_specs=[vmem] * 2,
        out_shape=[
            jax.ShapeDtypeStruct((2, east, upward), F32),
            jax.ShapeDtypeStruct((north, upward) if pair else east_ends.shape, F32),
        ],
        compiler_params=small,
    )(faces[1], gathered, east_ends, east_inverse, north_spikes)

    if pair:
        other = lax.ppermute(own, "gx", [(0, 1), (1, 0)])
        near = lines[0][1][0]
        table = np.array([[1.0 / (1.0 - near**2), near / (1.0 - near**2)]], np.float32)
    else:
        other = lax.all_gather(own, "gx")
        table = faces[0]
    tile = 32
    return pl.pallas_call(
        functools.partial(final_kernel, "gx", members[0], pair, tile),
        in_specs=[smem, smem] + [vmem] * 8,
        out_specs=hbm,
        out_shape=jax.ShapeDtypeStruct(shape, F32),
        scratch_shapes=[
            pltpu.VMEM(shape, F32),
            pltpu.VMEM((2, north, upward), F32),
            pltpu.SemaphoreType.DMA((north // tile,)),
        ],
        compiler_params=params,
    )(table, sweep, own, other, swept, rest, columns, rows, upward_spikes, north_spikes)


def solution(mesh):
    return jax.shard_map(
        local,
        mesh=mesh,
        in_specs=(P("gx", "gy", "gz"), P("gx", "gy", "gz")),
        out_specs=P("gx", "gy", "gz"),
        check_vma=False,
    )
```

```python
import functools

import jax
import jax.numpy as jnp
import numpy as np
from jax import lax
from jax.experimental import pallas as pl
from jax.experimental.pallas import tpu as pltpu
from jax.sharding import PartitionSpec as P

F32 = jnp.float32
BF16 = jnp.bfloat16
MIB = 1 << 20


def line_tables(length, factor):
    matrix = (1.0 + factor) * np.eye(length)
    matrix -= 0.5 * factor * (np.eye(length, k=1) + np.eye(length, k=-1))
    inverse = np.linalg.inv(matrix)
    inverse = 0.5 * (inverse + inverse.T)
    return inverse, 0.5 * factor * inverse[:, 0], 0.5 * factor * inverse[:, -1]


def chain_system(near, far, members):
    system = np.eye(2 * members)
    for m in range(members):
        if m > 0:
            system[2 * m, 2 * m - 1] -= near
            system[2 * m + 1, 2 * m - 1] -= far
        if m < members - 1:
            system[2 * m, 2 * m + 2] -= far
            system[2 * m + 1, 2 * m + 2] -= near
    return np.linalg.inv(system)


def interface_table(before, after, members):
    solved = chain_system(before[0], before[-1], members)
    rows = np.zeros((members, 2, 2 * members))
    for m in range(members):
        if m > 0:
            rows[m, 0] = solved[2 * m - 1]
        if m < members - 1:
            rows[m, 1] = solved[2 * m + 2]
    return rows


def peers(member, members, distance):
    if members & (members - 1) == 0:
        return member ^ distance, member ^ distance
    return (member + distance) % members, (member - distance) % members


def exchange_tables(before, after, members):
    near, far = before[0], before[-1]
    sending = np.zeros((members, 2 * (members - 1)))
    taking = np.zeros((members, 8 + 2 * (members - 1)))
    for m in range(members):
        right = chain_system(near, far, members - 1 - m)
        left = chain_system(near, far, m)
        for d in range(1, members):
            k = peers(m, members, d)[1]
            if k > m:
                sending[k, 2 * d - 2 : 2 * d] = right[0, 2 * (k - m - 1) : 2 * (k - m)]
                taking[m, 8 + 2 * d - 1] = 1.0
            else:
                sending[k, 2 * d - 2 : 2 * d] = left[-1, 2 * k : 2 * k + 2]
                taking[m, 8 + 2 * d - 2] = 1.0
        pull_left = answer(near, far, m)
        pull_right = answer(near, far, members - 1 - m)
        system = np.array([
            [1.0, 0.0, -pull_left, 0.0],
            [0.0, 1.0, 0.0, -pull_right],
            [-near, -far, 1.0, 0.0],
            [-far, -near, 0.0, 1.0],
        ])
        taking[m, :8] = np.linalg.inv(system)[:2].reshape(8)
    return sending, taking


def answer(near, far, members):
    if members == 0:
        return 0.0
    push = np.zeros(2 * members)
    push[0], push[1] = near, far
    return chain_system(near, far, members)[0] @ push


def sweep_table(length, factor):
    half = 0.5 * factor
    ratio = np.zeros(length)
    scale = np.zeros(length)
    last = 0.0
    for i in range(length):
        scale[i] = 1.0 / (1.0 + factor - half * last)
        ratio[i] = last = half * scale[i]
    head = np.concatenate([[1.0], np.cumprod(ratio)[:-1]])
    return np.stack([scale, ratio, head, np.cumprod(ratio)])


def split(table, axis):
    rows = np.moveaxis(np.asarray(table, np.float64), axis, 0)
    high = np.zeros(rows.shape, BF16)
    carried = np.zeros(rows.shape[1:])
    for k, row in enumerate(rows):
        high[k] = (row + carried).astype(np.float32).astype(BF16)
        carried = carried + row - high[k].astype(np.float64)
    low = (rows - high.astype(np.float64)).astype(np.float32).astype(BF16)
    return np.moveaxis(high, 0, axis), np.moveaxis(low, 0, axis)


def parts(values):
    high = values.astype(BF16)
    return high, (values - high.astype(F32)).astype(BF16)


def dot(a, b):
    return jnp.dot(a, b, preferred_element_type=F32)


def exact_dot(a, b):
    return jnp.dot(a, b, precision=lax.Precision.HIGHEST, preferred_element_type=F32)


def send_all(ends, table_ref, me, out_refs):
    for d, out_ref in enumerate(out_refs):
        out_ref[...] = table_ref[me, 2 * d] * ends[0] + table_ref[me, 2 * d + 1] * ends[1]


def take_all(ends, table_ref, me, message_refs):
    left = right = 0.0
    for d, message_ref in enumerate(message_refs):
        left += table_ref[me, 8 + 2 * d] * message_ref[...]
        right += table_ref[me, 9 + 2 * d] * message_ref[...]
    known = (left, right) + tuple(ends)
    return [sum(table_ref[me, 4 * side + k] * known[k] for k in range(4)) for side in range(2)]


def ordered(pair, east):
    if not pair:
        return lambda i: i
    flip = lax.axis_index("gx")
    return lambda i: jnp.where(flip == 0, i, east - 1 - i)


def local_kernel(
    pair, group, factor,
    sweep_ref, sending_ref, upward_high_ref, upward_low_ref, north_ref, warmth_hbm, supply_hbm,
    swept_ref, warmth_ref, upward_ends_ref, north_ends_ref, east_ends_ref, *rest,
):
    *message_refs, supply_ref, both_ref, planes_ref, sems = rest
    east, north, upward = warmth_ref.shape
    groups = east // group
    last = east_ends_ref.shape[0] - 1
    place = ordered(pair, east)
    me_up = lax.axis_index("gz")

    def fetch(which, g):
        start = jnp.minimum(place(g * group), place(g * group + group - 1))
        block = pl.ds(start, group)
        source, target = ((warmth_hbm, warmth_ref), (supply_hbm, supply_ref))[which]
        return pltpu.make_async_copy(source.at[block], target.at[block], sems.at[which, g])

    for g in range(groups):
        for which in range(2):
            fetch(which, g).start()
    both_ref[...] = jnp.zeros_like(both_ref)
    east_ends_ref[...] = jnp.zeros_like(east_ends_ref)
    north_ends_ref[:, east:] = jnp.zeros_like(north_ends_ref[:, east:])
    lane = lax.broadcasted_iota(jnp.int32, (1, 2 * east), 1)
    fetch(0, 0).wait()

    def body(g, _):
        fetch(1, g).wait()

        @pl.when(g + 1 < groups)
        def _():
            fetch(0, g + 1).wait()

        flat = (group * north, upward)
        warm_list, heat_list = [], []
        for k in range(group):
            i = g * group + k
            warm = warmth_ref[place(i)]
            low = warmth_ref[place(jnp.maximum(i - 1, 0))]
            high = warmth_ref[place(jnp.minimum(i + 1, east - 1))]
            low_factor = jnp.where(i == 0, 0.0, factor)
            high_factor = jnp.where(i == east - 1, 0.0, factor)
            heat = supply_ref[place(i)] + (4.0 - 2.0 * factor) * warm
            heat_list.append(heat + (low_factor * low + high_factor * high))
            warm_list.append(warm)
        heat_high, heat_low = parts(jnp.reshape(jnp.stack(heat_list), flat))
        warm_high, warm_low = parts(jnp.reshape(jnp.stack(warm_list), flat))
        upward_high, upward_low = upward_high_ref[...], upward_low_ref[...]
        heat_up = dot(heat_high, upward_high) + dot(heat_low, upward_high) + dot(heat_high, upward_low)
        warm_up = dot(warm_high, upward_high) + dot(warm_low, upward_high)
        for k in range(group):
            i = g * group + k
            rows = slice(k * north, (k + 1) * north)
            first, second = heat_up[rows], warm_up[rows]
            for field, value in enumerate((first, second)):
                both = jnp.where(lane < east, value[:, : 2 * east], value[:, upward - 2 * east :])
                turned = pltpu.roll(both, 2 * i + 1, 1)
                own = (lane == 2 * i) | (lane == 2 * i + 1)
                both_ref[field] = jnp.where(own, turned, both_ref[field])
            first_high, first_low = parts(first - 2.0 * warm_list[k])
            solved = dot(north_ref[...], jnp.concatenate([first_high, first_low], axis=0))
            solved = solved[:north] + solved[north:]
            north_ends_ref[0, pl.ds(i, 1), :] = solved[:1]
            north_ends_ref[1, pl.ds(i, 1), :] = solved[north - 1 :]
            source = sweep_ref[0, i] * (solved - 2.0 * second)
            swept = source + sweep_ref[1, i] * east_ends_ref[last]
            swept_ref[i] = swept
            east_ends_ref[last] = swept
            if not pair:
                east_ends_ref[0] += sweep_ref[2, i] * swept

                @pl.when(i == 0)
                def _():
                    planes_ref[0] = second

            if k == group - 1:

                @pl.when(i == east - 1)
                def _():
                    planes_ref[last] = second

        return 0

    lax.fori_loop(0, groups, body, 0)

    count = east_ends_ref.shape[0]
    for p in range(count):
        high, low = parts(planes_ref[p])
        solved = dot(north_ref[...], jnp.concatenate([high, low], axis=0))
        solved = solved[:north] + solved[north:]
        row = east + count - 1 - p
        north_ends_ref[0, row : row + 1] = solved[:1]
        north_ends_ref[1, row : row + 1] = solved[north - 1 :]
        east_ends_ref[p] += 2.0 * solved
    even = lane % 2 == 0
    heat, warm = both_ref[0], both_ref[1]
    heads = jnp.where(even, pltpu.roll(heat, 2 * east - 1, 1), warm)
    tails = jnp.where(even, heat, pltpu.roll(warm, 1, 1))
    upward_ends_ref[0] = heads
    upward_ends_ref[1] = tails
    send_all((heads, tails), sending_ref, me_up, message_refs)


def upward_kernel(
    count, taken, sent,
    taking_ref, sending_ref, ends_ref, north_ends_ref, east_ends_ref, north_inverse_ref, fold_ref, spikes_ref, spread_ref, *rest,
):
    message_refs = rest[:taken]
    columns_ref, north_out_ref, east_out_ref = rest[taken : taken + 3]
    out_refs = rest[taken + 3 :]
    assert len(out_refs) == sent
    north, lanes = columns_ref.shape
    east = lanes // 2
    sides = take_all((ends_ref[0], ends_ref[1]), taking_ref, lax.axis_index("gz"), message_refs)
    sides = jnp.concatenate(sides, axis=1)
    lane = lax.broadcasted_iota(jnp.int32, (1, 2 * lanes), 1) % lanes
    solved = exact_dot(north_inverse_ref[...], sides)
    mixed = jnp.where(lane % 2 == 0, solved, sides)
    swept = [exact_dot(mixed[:, side * lanes : (side + 1) * lanes], fold_ref[...]) for side in range(2)]
    columns_ref[...] = jnp.concatenate(swept, axis=1)
    padded = north_ends_ref.shape[1]
    row = lax.broadcasted_iota(jnp.int32, (padded, 2 * lanes), 0)
    target = jnp.where(row < east, 2 * row, jnp.where(row == east, lanes - 1, jnp.where(row < east + count, 1, -1)))
    own = lax.broadcasted_iota(jnp.int32, (padded, 2 * lanes), 1) % lanes == target
    picked = [jnp.where(own, solved[y : y + 1], 0.0) for y in (0, north - 1)]
    added = exact_dot(jnp.concatenate(picked, axis=0), spread_ref[...])
    ends = [north_ends_ref[0] + added[:padded], north_ends_ref[1] + added[padded:]]
    north_out_ref[0] = ends[0]
    north_out_ref[1] = ends[1]
    send_all(ends, sending_ref, lax.axis_index("gy"), out_refs)
    for p in range(count):
        i = east - 1 if p == count - 1 else 0
        total = east_ends_ref[p]
        for side in range(2):
            odd = side * lanes + 2 * i + 1
            column = swept[side][:, i : i + 1] + 2.0 * solved[:, odd : odd + 1]
            total += column * spikes_ref[side : side + 1, :]
        east_out_ref[p] = total


def north_kernel(
    count, taken,
    taking_ref, ends_ref, east_ends_ref, east_inverse_ref, spikes_ref, *rest,
):
    message_refs = rest[:taken]
    rows_ref, east_out_ref = rest[taken:]
    east = rows_ref.shape[1]
    sides = take_all((ends_ref[0], ends_ref[1]), taking_ref, lax.axis_index("gy"), message_refs)
    swept = [exact_dot(east_inverse_ref[...], side[:east]) for side in sides]
    for side in range(2):
        rows_ref[side] = swept[side]
    for p in range(count):
        i = east - 1 if p == count - 1 else 0
        extra = east + count - 1 - p
        total = east_ends_ref[p]
        for side in range(2):
            total += spikes_ref[side] * (swept[side][i : i + 1] + 2.0 * sides[side][extra : extra + 1])
        east_out_ref[p] = total


def final_kernel(
    pair, members, tile,
    table_ref, sweep_ref, own_ref, other_ref, swept_ref, warmth_ref, columns_ref, rows_ref, upward_spikes_ref, north_spikes_ref,
    out_hbm,
    out_ref, sides_ref, sems,
):
    east, north, upward = out_ref.shape
    place = ordered(pair, east)
    if pair:
        sides_ref[0] = table_ref[0, 0] * other_ref[0] + table_ref[0, 1] * own_ref[0]
    else:
        me = lax.axis_index("gx")
        for side in range(2):
            total = jnp.zeros(sides_ref.shape[1:], F32)
            for m in range(members):
                for end in range(2):
                    total += other_ref[m, end] * table_ref[me, side * 2 * members + 2 * m + end]
            sides_ref[side] = total

    def send(t):
        block = pl.ds(pl.multiple_of(t * tile, tile), tile)
        return pltpu.make_async_copy(out_ref.at[:, block], out_hbm.at[:, block], sems.at[t])

    def body(t, _):
        block = pl.ds(pl.multiple_of(t * tile, tile), tile)
        value = sides_ref[sides_ref.shape[0] - 1, block]
        columns = columns_ref[block]
        first_spike, last_spike = north_spikes_ref[0, block], north_spikes_ref[1, block]
        for i in reversed(range(east)):
            value = swept_ref[i, block] + sweep_ref[1, i] * value
            if not pair:
                value += sweep_ref[3, i] * sides_ref[0, block]
            added = (
                columns[:, i : i + 1] * upward_spikes_ref[0:1, :]
                + columns[:, east + i : east + i + 1] * upward_spikes_ref[1:2, :]
            )
            added += first_spike * rows_ref[0, i : i + 1, :] + last_spike * rows_ref[1, i : i + 1, :]
            x = place(i)
            out_ref[x, block] = warmth_ref[x, block] + value + added
        send(t).start()
        return 0

    lax.fori_loop(0, north // tile, body, 0)
    for t in range(north // tile):
        send(t).wait()


def spread_out(messages, axis):
    members = lax.axis_size(axis)
    return [
        lax.ppermute(message, axis, [(k, peers(k, members, d + 1)[0]) for k in range(members)])
        for d, message in enumerate(messages)
    ]


def local(initial_warmth, heat_supply):
    shape = east, north, upward = initial_warmth.shape
    members = [lax.axis_size(axis) for axis in ("gx", "gy", "gz")]
    factors = [float((n * m) ** 2 // 4) for n, m in zip(shape, members)]
    lines = [line_tables(n, factor) for n, factor in zip(shape, factors)]
    sweep = sweep_table(east, factors[0]).astype(np.float32)
    exchanges = [exchange_tables(line[1], line[2], m) for line, m in zip(lines, members)]
    exchanges = [tuple(table.astype(np.float32) for table in pair_of) for pair_of in exchanges]
    upward_high, upward_low = split(lines[2][0], 0)
    north_high, north_low = split(lines[1][0], 1)
    north_stack = np.block([[north_high, north_high], [north_low, np.zeros_like(north_low)]])
    east_inverse = lines[0][0].astype(np.float32)
    north_inverse = lines[1][0].astype(np.float32)
    fold = np.kron(lines[0][0], np.array([[1.0], [-2.0]])).astype(np.float32)
    upward_spikes = np.stack(lines[2][1:]).astype(np.float32)
    spread = np.repeat(upward_spikes, 2 * east, axis=0)
    north_spikes = np.broadcast_to(np.stack(lines[1][1:])[:, :, None], (2, north, upward)).astype(np.float32)

    pair = members[0] == 2
    count = 1 if pair else 2
    padded = east + 8
    to_up, to_north = members[2] - 1, members[1] - 1
    vmem = pl.BlockSpec(memory_space=pltpu.VMEM)
    smem = pl.BlockSpec(memory_space=pltpu.SMEM)
    hbm = pl.BlockSpec(memory_space=pl.ANY)

    def kept(*sizes):
        return jax.ShapeDtypeStruct(sizes, F32)

    group = 4
    swept, warmth, upward_ends, north_ends, east_ends, *messages = pl.pallas_call(
        functools.partial(local_kernel, pair, group, factors[0]),
        in_specs=[smem, smem, vmem, vmem, vmem, hbm, hbm],
        out_specs=[vmem] * (5 + to_up),
        out_shape=[
            pltpu.VMEM(shape, F32),
            pltpu.VMEM(shape, F32),
            kept(2, north, 2 * east),
            kept(2, padded, upward),
            kept(count, north, upward),
        ]
        + [kept(north, 2 * east)] * to_up,
        scratch_shapes=[
            pltpu.VMEM(shape, F32),
            pltpu.VMEM((2, north, 2 * east), F32),
            pltpu.VMEM((count, north, upward), F32),
            pltpu.SemaphoreType.DMA((2, east // group)),
        ],
        compiler_params=pltpu.CompilerParams(vmem_limit_bytes=32 * MIB),
    )(sweep, exchanges[2][0], upward_high, upward_low, north_stack, initial_warmth, heat_supply)

    messages = spread_out(messages, "gz")
    columns, north_ends, east_ends, *messages = pl.pallas_call(
        functools.partial(upward_kernel, count, to_up, to_north),
        in_specs=[smem, smem] + [vmem] * (7 + to_up),
        out_specs=[vmem] * (3 + to_north),
        out_shape=[kept(north, 2 * east), kept(2, padded, upward), kept(count, north, upward)]
        + [kept(padded, upward)] * to_north,
        compiler_params=pltpu.CompilerParams(vmem_limit_bytes=6 * MIB),
    )(
        exchanges[2][1], exchanges[1][0], upward_ends, north_ends, east_ends, north_inverse, fold, upward_spikes, spread,
        *messages,
    )

    messages = spread_out(messages, "gy")
    rows, own = pl.pallas_call(
        functools.partial(north_kernel, count, to_north),
        in_specs=[smem] + [vmem] * (4 + to_north),
        out_specs=[vmem] * 2,
        out_shape=[kept(2, east, upward), kept(count, north, upward)],
        compiler_params=pltpu.CompilerParams(vmem_limit_bytes=6 * MIB),
    )(exchanges[1][1], north_ends, east_ends, east_inverse, north_spikes, *messages)

    if pair:
        other = lax.ppermute(own, "gx", [(0, 1), (1, 0)])
        near = lines[0][1][0]
        table = np.array([[1.0 / (1.0 - near**2), near / (1.0 - near**2)]], np.float32)
    else:
        other = lax.all_gather(own, "gx")
        table = interface_table(lines[0][1], lines[0][2], members[0]).reshape(members[0], -1).astype(np.float32)
    swept = pltpu.with_memory_space_constraint(swept, pltpu.VMEM)
    warmth = pltpu.with_memory_space_constraint(warmth, pltpu.VMEM)
    tile = 32
    return pl.pallas_call(
        functools.partial(final_kernel, pair, members[0], tile),
        in_specs=[smem, smem] + [vmem] * 8,
        out_specs=hbm,
        out_shape=kept(*shape),
        scratch_shapes=[
            pltpu.VMEM(shape, F32),
            pltpu.VMEM((count, north, upward), F32),
            pltpu.SemaphoreType.DMA((north // tile,)),
        ],
        compiler_params=pltpu.CompilerParams(vmem_limit_bytes=16 * MIB),
    )(table, sweep, own, other, swept, warmth, columns, rows, upward_spikes, north_spikes)


def solution(mesh):
    return jax.shard_map(
        local,
        mesh=mesh,
        in_specs=(P("gx", "gy", "gz"), P("gx", "gy", "gz")),
        out_specs=P("gx", "gy", "gz"),
        check_vma=False,
    )
```

```python
import functools

import jax
import jax.numpy as jnp
import numpy as np
from jax import lax
from jax.experimental import pallas as pl
from jax.experimental.pallas import tpu as pltpu
from jax.sharding import PartitionSpec as P

F32 = jnp.float32
BF16 = jnp.bfloat16
MIB = 1 << 20


def line_tables(length, factor):
    matrix = (1.0 + factor) * np.eye(length)
    matrix -= 0.5 * factor * (np.eye(length, k=1) + np.eye(length, k=-1))
    inverse = np.linalg.inv(matrix)
    inverse = 0.5 * (inverse + inverse.T)
    return inverse, 0.5 * factor * inverse[:, 0], 0.5 * factor * inverse[:, -1]


def chain_system(near, far, members):
    system = np.eye(2 * members)
    for m in range(members):
        if m > 0:
            system[2 * m, 2 * m - 1] -= near
            system[2 * m + 1, 2 * m - 1] -= far
        if m < members - 1:
            system[2 * m, 2 * m + 2] -= far
            system[2 * m + 1, 2 * m + 2] -= near
    return np.linalg.inv(system)


def interface_table(before, after, members):
    solved = chain_system(before[0], before[-1], members)
    rows = np.zeros((members, 2, 2 * members))
    for m in range(members):
        if m > 0:
            rows[m, 0] = solved[2 * m - 1]
        if m < members - 1:
            rows[m, 1] = solved[2 * m + 2]
    return rows


def peers(member, members, distance):
    if members & (members - 1) == 0:
        return member ^ distance, member ^ distance
    return (member + distance) % members, (member - distance) % members


def exchange_tables(before, after, members):
    near, far = before[0], before[-1]
    sending = np.zeros((members, 2 * (members - 1)))
    taking = np.zeros((members, 8 + 2 * (members - 1)))
    for m in range(members):
        right = chain_system(near, far, members - 1 - m)
        left = chain_system(near, far, m)
        for d in range(1, members):
            k = peers(m, members, d)[1]
            if k > m:
                sending[k, 2 * d - 2 : 2 * d] = right[0, 2 * (k - m - 1) : 2 * (k - m)]
                taking[m, 8 + 2 * d - 1] = 1.0
            else:
                sending[k, 2 * d - 2 : 2 * d] = left[-1, 2 * k : 2 * k + 2]
                taking[m, 8 + 2 * d - 2] = 1.0
        pull_left = answer(near, far, m)
        pull_right = answer(near, far, members - 1 - m)
        system = np.array([
            [1.0, 0.0, -pull_left, 0.0],
            [0.0, 1.0, 0.0, -pull_right],
            [-near, -far, 1.0, 0.0],
            [-far, -near, 0.0, 1.0],
        ])
        taking[m, :8] = np.linalg.inv(system)[:2].reshape(8)
    return sending, taking


def answer(near, far, members):
    if members == 0:
        return 0.0
    push = np.zeros(2 * members)
    push[0], push[1] = near, far
    return chain_system(near, far, members)[0] @ push


def sweep_table(length, factor):
    half = 0.5 * factor
    ratio = np.zeros(length)
    scale = np.zeros(length)
    last = 0.0
    for i in range(length):
        scale[i] = 1.0 / (1.0 + factor - half * last)
        ratio[i] = last = half * scale[i]
    head = np.concatenate([[1.0], np.cumprod(ratio)[:-1]])
    return np.stack([scale, ratio, head, np.cumprod(ratio)])


def split(table, axis):
    rows = np.moveaxis(np.asarray(table, np.float64), axis, 0)
    high = np.zeros(rows.shape, BF16)
    carried = np.zeros(rows.shape[1:])
    for k, row in enumerate(rows):
        high[k] = (row + carried).astype(np.float32).astype(BF16)
        carried = carried + row - high[k].astype(np.float64)
    low = (rows - high.astype(np.float64)).astype(np.float32).astype(BF16)
    return np.moveaxis(high, 0, axis), np.moveaxis(low, 0, axis)


def parts(values):
    high = values.astype(BF16)
    return high, (values - high.astype(F32)).astype(BF16)


def dot(a, b):
    return jnp.dot(a, b, preferred_element_type=F32)


def exact_dot(a, b):
    return jnp.dot(a, b, precision=lax.Precision.HIGHEST, preferred_element_type=F32)


def upward_dot(values, table_ref):
    high, low = parts(values)
    return dot(jnp.concatenate([high, low, high], axis=1), table_ref[...])


def north_dot(table_ref, values):
    north = values.shape[0]
    solved = dot(table_ref[...], jnp.concatenate(parts(values), axis=0))
    return solved[:north] + solved[north:]


def pick(column, me):
    value = float(column[0])
    for k in range(1, len(column)):
        value = jnp.where(me == k, float(column[k]), value)
    return value


def send_all(ends, table, me, out_refs):
    for d, out_ref in enumerate(out_refs):
        out_ref[...] = pick(table[:, 2 * d], me) * ends[0] + pick(table[:, 2 * d + 1], me) * ends[1]


def take_all(ends, table, me, messages):
    left = right = 0.0
    for d, message in enumerate(messages):
        left += pick(table[:, 8 + 2 * d], me) * message
        right += pick(table[:, 9 + 2 * d], me) * message
    known = (left, right) + tuple(ends)
    return [sum(pick(table[:, 4 * side + k], me) * known[k] for k in range(4)) for side in range(2)]


def diagonal(size):
    return lax.broadcasted_iota(jnp.int32, (size, size), 0) == lax.broadcasted_iota(jnp.int32, (size, size), 1)


def as_row(column):
    return jnp.sum(jnp.where(diagonal(column.shape[0]), column, 0.0), axis=0, keepdims=True)


def as_column(row):
    return jnp.sum(jnp.where(diagonal(row.shape[1]), row, 0.0), axis=1, keepdims=True)


def stacked(rows, height):
    filler = jnp.zeros((height - sum(row.shape[0] for row in rows), rows[0].shape[1]), F32)
    return jnp.concatenate(list(rows) + [filler], axis=0)


def ordered(pair, east):
    if not pair:
        return lambda i: i
    flip = lax.axis_index("gx")
    return lambda i: jnp.where(flip == 0, i, east - 1 - i)


def end_places(count, east):
    if count == 1:
        return [(east - 1, 0)]
    return [(0, 0), (east - 1, 1)]


def local_kernel(
    pair, group, factors, sending,
    tables_hbm, warmth_hbm, supply_hbm,
    swept_ref, warmth_ref, upward_ends_ref, north_ends_ref, east_ends_ref, *rest,
):
    to_up, to_north = (table.shape[1] // 2 for table in sending)
    up_refs, north_refs = rest[:to_up], rest[to_up : to_up + to_north]
    supply_ref, both_ref, edges_ref, tables_ref, up_ref, north_ref, sems = rest[to_up + to_north :]
    east, north, upward = supply_ref.shape
    groups = east // group
    count = east_ends_ref.shape[0]
    place = ordered(pair, east)

    def fetch(which, g):
        start = jnp.minimum(place(g * group), place(g * group + group - 1))
        block = pl.ds(start, group)
        if which == 0:
            return pltpu.make_async_copy(warmth_hbm.at[block], warmth_ref.at[pl.ds(start + 1, group)], sems.at[0, g])
        return pltpu.make_async_copy(supply_hbm.at[block], supply_ref.at[block], sems.at[1, g])

    tables = pltpu.make_async_copy(tables_hbm, tables_ref, sems.at[0, groups])
    tables.start()
    for g in range(groups):
        for which in range(2):
            fetch(which, g).start()
    warmth_ref[0] = jnp.zeros((north, upward), F32)
    warmth_ref[east + 1] = jnp.zeros((north, upward), F32)
    both_ref[...] = jnp.zeros_like(both_ref)
    east_ends_ref[...] = jnp.zeros_like(east_ends_ref)
    lane = lax.broadcasted_iota(jnp.int32, (1, 2 * east), 1)
    line = lax.broadcasted_iota(jnp.int32, (north, 1), 0)
    tables.wait()
    up_ref[...] = tables_ref[: 3 * upward].astype(BF16)
    north_ref[...] = tables_ref[3 * upward : 3 * upward + 2 * north, : 2 * north].astype(BF16)
    sweep = 3 * upward + 2 * north
    fetch(0, 0).wait()

    def body(g, _):
        fetch(1, g).wait()

        @pl.when(g + 1 < groups)
        def _():
            fetch(0, g + 1).wait()

        warm_list, heat_list = [], []
        for k in range(group):
            i = g * group + k
            x = place(i)
            warm = warmth_ref[x + 1]
            bent = (warmth_ref[x] - warm) + (warmth_ref[x + 2] - warm)
            low = jnp.where(line == 0, 0.0, pltpu.roll(warm, 1, 0))
            high = jnp.where(line == north - 1, 0.0, pltpu.roll(warm, north - 1, 0))
            bent += (factors[1] / factors[0]) * ((low - warm) + (high - warm))
            heat_list.append((supply_ref[x] + 2.0 * warm) + factors[0] * bent)
            warm_list.append(warm)
            edges_ref[pl.ds(i, 1)] = warm[:1]
            edges_ref[pl.ds(east + i, 1)] = warm[north - 1 :]
        solved_up = upward_dot(jnp.concatenate(heat_list, axis=0), up_ref)
        for k in range(group):
            i = g * group + k
            first = solved_up[k * north : (k + 1) * north]
            heads = pltpu.roll(first[:, : 2 * east], i, 1)
            tails = pltpu.roll(first[:, upward - 2 * east :], east + 1 + i, 1)
            both = jnp.where(lane == i, heads, both_ref[...])
            both_ref[...] = jnp.where(lane == east + i, tails, both)
            solved = north_dot(north_ref, first - 2.0 * warm_list[k])
            north_ends_ref[0, pl.ds(i, 1), :] = solved[:1]
            north_ends_ref[1, pl.ds(i, 1), :] = solved[north - 1 :]
            scale, ratio = (tables_ref[pl.ds(sweep + n * east + i, 1), :] for n in range(2))
            swept = scale * solved + ratio * east_ends_ref[count - 1]
            swept_ref[i] = swept
            east_ends_ref[count - 1] = swept
            if not pair:
                east_ends_ref[0] += tables_ref[pl.ds(sweep + 2 * east + i, 1), :] * swept
        return 0

    lax.fori_loop(0, groups, body, 0)

    ends = end_places(count, east)
    planes = [warmth_ref[place(i) + 1] for i, _ in ends]
    solved_up = upward_dot(jnp.concatenate([edges_ref[...]] + planes, axis=0), up_ref)
    height = north_ends_ref.shape[1]
    rows = [[], []]
    for p in range(count):
        solved = north_dot(north_ref, solved_up[2 * east + p * north : 2 * east + (p + 1) * north])
        rows[0].append(solved[:1])
        rows[1].append(solved[north - 1 :])
        east_ends_ref[p] += 2.0 * solved
    north_ends = []
    for end in range(2):
        north_ends_ref[end, :east] += 2.0 * solved_up[end * east : (end + 1) * east]
        north_ends_ref[end, east:] = stacked(rows[end], height - east)
        north_ends.append(north_ends_ref[end])
    send_all(north_ends, sending[1], lax.axis_index("gy"), north_refs)

    half = north // 2
    top, bottom = both_ref[:half], both_ref[half:]
    folded = (
        jnp.where(lane < east, top, pltpu.roll(bottom, east, 1)),
        jnp.where(lane < east, pltpu.roll(top, east, 1), bottom),
    )
    upward_ends = []
    for end, column in enumerate((slice(0, 1), slice(upward - 1, upward))):
        extra = [as_row(solved_up[k * north : (k + 1) * north, column]) for k in range(1 + count)]
        upward_ends.append(stacked([folded[end]] + extra, upward_ends_ref.shape[1]))
        upward_ends_ref[end] = upward_ends[end]
    send_all(upward_ends, sending[0], lax.axis_index("gz"), up_refs)


def upward_kernel(
    count, taking, sending,
    ends_ref, north_inverse_ref, east_twice_ref, *rest,
):
    taken = (taking.shape[1] - 8) // 2
    message_refs = rest[:taken]
    columns_ref, tiny_ref, plane_ref, *out_refs = rest[taken:]
    north, lanes = columns_ref.shape
    east, half = lanes // 2, north // 2
    lane = lax.broadcasted_iota(jnp.int32, (1, lanes), 1)
    before, after = take_all(
        (ends_ref[0], ends_ref[1]), taking, lax.axis_index("gz"), [ref[...] for ref in message_refs]
    )

    def paired(end, rows):
        if end == 0:
            return jnp.where(lane < east, before[rows], pltpu.roll(after[rows], east, 1))
        return jnp.where(lane < east, pltpu.roll(before[rows], east, 1), after[rows])

    solved = exact_dot(north_inverse_ref[...], jnp.concatenate([paired(0, slice(0, half)), paired(1, slice(0, half))], axis=0))
    columns = exact_dot(solved, east_twice_ref[...])
    columns_ref[...] = columns
    planes = []
    for p in range(count):
        row = slice(half + 1 + p, half + 2 + p)
        planes.append([
            jnp.sum(north_inverse_ref[...] * side[row], axis=1, keepdims=True) for side in (before, after)
        ])
    tiny = []
    for end, y in enumerate((0, north - 1)):
        first = solved[y : y + 1] + 2.0 * paired(end, slice(half, half + 1))
        second = jnp.zeros((1, lanes), F32)
        for p in range(count):
            for side in range(2):
                second = jnp.where(lane == side * east + p, planes[p][side][y : y + 1], second)
        tiny.append(stacked([first, second], 8))
        tiny_ref[end] = tiny[end]
    send_all(tiny, sending, lax.axis_index("gy"), out_refs)
    for p, (i, _) in enumerate(end_places(count, east)):
        rows = []
        for side in range(2):
            column = columns[:, side * east + i : side * east + i + 1] + 2.0 * planes[p][side]
            rows.append(as_row(column))
        plane_ref[p] = stacked(rows, 8)


def north_kernel(
    count, taking,
    ends_ref, tiny_ref, plane_ref, east_inverse_ref, spread_ref, *rest,
):
    taken = (taking.shape[1] - 8) // 2
    message_refs, tiny_refs = rest[:taken], rest[taken : 2 * taken]
    rows_ref, small_ref = rest[2 * taken :]
    _, east, upward = rows_ref.shape
    height = ends_ref.shape[1]
    me = lax.axis_index("gy")
    sides = take_all((ends_ref[0], ends_ref[1]), taking, me, [ref[...] for ref in message_refs])
    tiny = take_all((tiny_ref[0], tiny_ref[1]), taking, me, [ref[...] for ref in tiny_refs])
    shape = (height, 2 * east)
    row = lax.broadcasted_iota(jnp.int32, shape, 0)
    lane = lax.broadcasted_iota(jnp.int32, shape, 1) % east
    own = (row < east) & (lane == row)
    behind = (row >= east) & (row < east + count) & (lane == row - east)
    picked = [jnp.where(own, side[:1], 0.0) + jnp.where(behind, side[1:2], 0.0) for side in tiny]
    added = exact_dot(jnp.concatenate(picked, axis=0), spread_ref[...])
    sides = [side + added[n * height : (n + 1) * height] for n, side in enumerate(sides)]
    swept = [exact_dot(east_inverse_ref[...], side[:east]) for side in sides]
    for n in range(2):
        rows_ref[n] = swept[n]
    for p, (i, k) in enumerate(end_places(count, east)):
        rows = [swept[n][i : i + 1] + 2.0 * sides[n][east + k : east + k + 1] for n in range(2)]
        wide = jnp.concatenate([plane_ref[p], jnp.zeros((8, upward - plane_ref.shape[2]), F32)], axis=1)
        small_ref[p] = stacked(rows + [wide[:2]], 8)


def final_kernel(
    pair, table, tile,
    sweep_ref, own_ref, other_ref, own_small_ref, other_small_ref,
    swept_ref, warmth_ref, columns_ref, rows_ref, upward_spikes_ref, north_spikes_ref,
    out_hbm,
    out_ref, sides_ref, sems,
):
    east, north, upward = out_ref.shape
    place = ordered(pair, east)

    def widened(plane, small):
        for side in range(2):
            plane += north_spikes_ref[side] * small[side : side + 1]
            plane += as_column(small[2 + side : 3 + side, :north]) * upward_spikes_ref[side : side + 1, :]
        return plane

    if pair:
        near, far = float(table[0]), float(table[1])
        sides_ref[0] = widened(
            near * other_ref[0] + far * own_ref[0], near * other_small_ref[0] + far * own_small_ref[0]
        )
    else:
        me = lax.axis_index("gx")
        members = table.shape[0]
        for side in range(2):
            plane, small = 0.0, 0.0
            for m in range(members):
                for end in range(2):
                    weight = pick(table[:, side, 2 * m + end], me)
                    plane += weight * other_ref[m, end]
                    small += weight * other_small_ref[m, end]
            sides_ref[side] = widened(plane, small)
    last = sides_ref.shape[0] - 1

    def send(t):
        block = pl.ds(pl.multiple_of(t * tile, tile), tile)
        return pltpu.make_async_copy(out_ref.at[:, block], out_hbm.at[:, block], sems.at[t])

    def body(t, _):
        block = pl.ds(pl.multiple_of(t * tile, tile), tile)
        value = sides_ref[last, block]
        columns = columns_ref[block]
        first_spike, last_spike = north_spikes_ref[0, block], north_spikes_ref[1, block]
        for i in reversed(range(east)):
            value = swept_ref[i, block] + sweep_ref[1, i] * value
            if not pair:
                value += sweep_ref[3, i] * sides_ref[0, block]
            added = (
                columns[:, i : i + 1] * upward_spikes_ref[0:1, :]
                + columns[:, east + i : east + i + 1] * upward_spikes_ref[1:2, :]
            )
            added += first_spike * rows_ref[0, i : i + 1, :] + last_spike * rows_ref[1, i : i + 1, :]
            x = place(i)
            out_ref[x, block] = warmth_ref[x + 1, block] + value + added
        send(t).start()
        return 0

    lax.fori_loop(0, north // tile, body, 0)
    for t in range(north // tile):
        send(t).wait()


def spread_out(messages, axis):
    members = lax.axis_size(axis)
    return [
        lax.ppermute(message, axis, [(k, peers(k, members, d + 1)[0]) for k in range(members)])
        for d, message in enumerate(messages)
    ]


def local(initial_warmth, heat_supply):
    shape = east, north, upward = initial_warmth.shape
    members = [lax.axis_size(axis) for axis in ("gx", "gy", "gz")]
    factors = [float((n * m) ** 2 // 4) for n, m in zip(shape, members)]
    lines = [line_tables(n, factor) for n, factor in zip(shape, factors)]
    sweep = sweep_table(east, factors[0]).astype(np.float32)
    exchanges = [exchange_tables(line[1], line[2], m) for line, m in zip(lines, members)]
    upward_high, upward_low = split(lines[2][0], 0)
    north_high, north_low = split(lines[1][0], 1)
    north_stack = np.block([[north_high, north_high], [north_low, np.zeros_like(north_low)]])
    tables = np.concatenate([
        np.concatenate([upward_high, upward_high, upward_low]).astype(np.float32),
        np.pad(north_stack.astype(np.float32), ((0, 0), (0, max(upward - 2 * north, 0)))),
        np.repeat(sweep.reshape(-1, 1), upward, axis=1),
    ])
    east_inverse = lines[0][0].astype(np.float32)
    north_inverse = lines[1][0].astype(np.float32)
    east_twice = np.kron(np.eye(2), lines[0][0]).astype(np.float32)
    upward_spikes = np.stack(lines[2][1:]).astype(np.float32)
    spread = np.repeat(upward_spikes, east, axis=0)
    north_spikes = np.broadcast_to(np.stack(lines[1][1:])[:, :, None], (2, north, upward)).astype(np.float32)

    pair = members[0] == 2
    count = 1 if pair else 2
    height = east + 8
    to_up, to_north = members[2] - 1, members[1] - 1
    vmem = pl.BlockSpec(memory_space=pltpu.VMEM)
    smem = pl.BlockSpec(memory_space=pltpu.SMEM)
    hbm = pl.BlockSpec(memory_space=pltpu.HBM)

    def kept(*sizes):
        return jax.ShapeDtypeStruct(sizes, F32)

    group = 4
    folded = kept(north // 2 + 8, 2 * east)
    swept, warmth, upward_ends, north_ends, own, *messages = pl.pallas_call(
        functools.partial(local_kernel, pair, group, factors, (exchanges[2][0], exchanges[1][0])),
        in_specs=[hbm] * 3,
        out_specs=[vmem] * (5 + to_up + to_north),
        out_shape=[
            pltpu.VMEM(shape, F32),
            pltpu.VMEM((east + 2, north, upward), F32),
            kept(2, *folded.shape),
            kept(2, height, upward),
            kept(count, north, upward),
        ]
        + [folded] * to_up
        + [kept(height, upward)] * to_north,
        scratch_shapes=[
            pltpu.VMEM(shape, F32),
            pltpu.VMEM((north, 2 * east), F32),
            pltpu.VMEM((2 * east, upward), F32),
            pltpu.VMEM(tables.shape, F32),
            pltpu.VMEM((3 * upward, upward), BF16),
            pltpu.VMEM((2 * north, 2 * north), BF16),
            pltpu.SemaphoreType.DMA((2, east // group + 1)),
        ],
        compiler_params=pltpu.CompilerParams(vmem_limit_bytes=32 * MIB),
    )(tables, initial_warmth, heat_supply)

    up_messages = spread_out(messages[:to_up], "gz")
    north_messages = spread_out(messages[to_up:], "gy")
    if pair:
        other = lax.ppermute(own, "gx", [(0, 1), (1, 0)])
    else:
        other = lax.all_gather(own, "gx")
    columns, tiny, planes, *messages = pl.pallas_call(
        functools.partial(upward_kernel, count, exchanges[2][1], exchanges[1][0]),
        in_specs=[vmem] * (3 + to_up),
        out_specs=[vmem] * (3 + to_north),
        out_shape=[kept(north, 2 * east), kept(2, 8, 2 * east), kept(count, 8, north)]
        + [kept(8, 2 * east)] * to_north,
        compiler_params=pltpu.CompilerParams(vmem_limit_bytes=6 * MIB),
    )(upward_ends, north_inverse, east_twice, *up_messages)

    tiny_messages = spread_out(messages, "gy")
    rows, own_small = pl.pallas_call(
        functools.partial(north_kernel, count, exchanges[1][1]),
        in_specs=[vmem] * (5 + 2 * to_north),
        out_specs=[vmem] * 2,
        out_shape=[kept(2, east, upward), kept(count, 8, upward)],
        compiler_params=pltpu.CompilerParams(vmem_limit_bytes=6 * MIB),
    )(north_ends, tiny, planes, east_inverse, spread, *north_messages, *tiny_messages)

    if pair:
        other_small = lax.ppermute(own_small, "gx", [(0, 1), (1, 0)])
        near = lines[0][1][0]
        table = np.array([1.0, near]) / (1.0 - near**2)
    else:
        other_small = lax.all_gather(own_small, "gx")
        table = interface_table(lines[0][1], lines[0][2], members[0])
    swept = pltpu.with_memory_space_constraint(swept, pltpu.VMEM)
    warmth = pltpu.with_memory_space_constraint(warmth, pltpu.VMEM)
    tile = 32
    return pl.pallas_call(
        functools.partial(final_kernel, pair, table, tile),
        in_specs=[smem] + [vmem] * 10,
        out_specs=hbm,
        out_shape=kept(*shape),
        scratch_shapes=[
            pltpu.VMEM(shape, F32),
            pltpu.VMEM((count, north, upward), F32),
            pltpu.SemaphoreType.DMA((north // tile,)),
        ],
        compiler_params=pltpu.CompilerParams(vmem_limit_bytes=16 * MIB),
    )(sweep, own, other, own_small, other_small, swept, warmth, columns, rows, upward_spikes, north_spikes)


def solution(mesh):
    return jax.shard_map(
        local,
        mesh=mesh,
        in_specs=(P("gx", "gy", "gz"), P("gx", "gy", "gz")),
        out_specs=P("gx", "gy", "gz"),
        check_vma=False,
    )
```

```python
import functools

import jax
import jax.numpy as jnp
import numpy as np
from jax import lax
from jax.experimental import pallas as pl
from jax.experimental.pallas import tpu as pltpu
from jax.sharding import PartitionSpec as P

F32 = jnp.float32
BF16 = jnp.bfloat16
MIB = 1 << 20


def line_tables(length, factor):
    matrix = (1.0 + factor) * np.eye(length)
    matrix -= 0.5 * factor * (np.eye(length, k=1) + np.eye(length, k=-1))
    inverse = np.linalg.inv(matrix)
    inverse = 0.5 * (inverse + inverse.T)
    return inverse, 0.5 * factor * inverse[:, 0], 0.5 * factor * inverse[:, -1]


def chain_system(near, far, members):
    system = np.eye(2 * members)
    for m in range(members):
        if m > 0:
            system[2 * m, 2 * m - 1] -= near
            system[2 * m + 1, 2 * m - 1] -= far
        if m < members - 1:
            system[2 * m, 2 * m + 2] -= far
            system[2 * m + 1, 2 * m + 2] -= near
    return np.linalg.inv(system)


def interface_table(before, after, members):
    solved = chain_system(before[0], before[-1], members)
    rows = np.zeros((members, 2, 2 * members))
    for m in range(members):
        if m > 0:
            rows[m, 0] = solved[2 * m - 1]
        if m < members - 1:
            rows[m, 1] = solved[2 * m + 2]
    return rows


def peers(member, members, distance):
    if members & (members - 1) == 0:
        return member ^ distance, member ^ distance
    return (member + distance) % members, (member - distance) % members


def exchange_tables(before, after, members):
    near, far = before[0], before[-1]
    sending = np.zeros((members, 2 * (members - 1)))
    taking = np.zeros((members, 8 + 2 * (members - 1)))
    for m in range(members):
        right = chain_system(near, far, members - 1 - m)
        left = chain_system(near, far, m)
        for d in range(1, members):
            k = peers(m, members, d)[1]
            if k > m:
                sending[k, 2 * d - 2 : 2 * d] = right[0, 2 * (k - m - 1) : 2 * (k - m)]
                taking[m, 8 + 2 * d - 1] = 1.0
            else:
                sending[k, 2 * d - 2 : 2 * d] = left[-1, 2 * k : 2 * k + 2]
                taking[m, 8 + 2 * d - 2] = 1.0
        pull_left = answer(near, far, m)
        pull_right = answer(near, far, members - 1 - m)
        system = np.array([
            [1.0, 0.0, -pull_left, 0.0],
            [0.0, 1.0, 0.0, -pull_right],
            [-near, -far, 1.0, 0.0],
            [-far, -near, 0.0, 1.0],
        ])
        taking[m, :8] = np.linalg.inv(system)[:2].reshape(8)
    return sending, taking


def answer(near, far, members):
    if members == 0:
        return 0.0
    push = np.zeros(2 * members)
    push[0], push[1] = near, far
    return chain_system(near, far, members)[0] @ push


def sweep_table(length, factor):
    half = 0.5 * factor
    ratio = np.zeros(length)
    scale = np.zeros(length)
    last = 0.0
    for i in range(length):
        scale[i] = 1.0 / (1.0 + factor - half * last)
        ratio[i] = last = half * scale[i]
    head = np.concatenate([[1.0], np.cumprod(ratio)[:-1]])
    return np.stack([scale, ratio, head, np.cumprod(ratio)])


def split(table, axis):
    rows = np.moveaxis(np.asarray(table, np.float64), axis, 0)
    high = np.zeros(rows.shape, BF16)
    carried = np.zeros(rows.shape[1:])
    for k, row in enumerate(rows):
        high[k] = (row + carried).astype(np.float32).astype(BF16)
        carried = carried + row - high[k].astype(np.float64)
    low = (rows - high.astype(np.float64)).astype(np.float32).astype(BF16)
    return np.moveaxis(high, 0, axis), np.moveaxis(low, 0, axis)


def parts(values):
    high = values.astype(BF16)
    return high, (values - high.astype(F32)).astype(BF16)


def dot(a, b):
    return jnp.dot(a, b, preferred_element_type=F32)


def exact_dot(a, b):
    return jnp.dot(a, b, precision=lax.Precision.HIGHEST, preferred_element_type=F32)


def upward_dot(values, table_ref):
    high, low = parts(values)
    return dot(jnp.concatenate([high, low, high], axis=1), table_ref[...])


def north_dot(table_ref, values):
    north = values.shape[0]
    solved = dot(table_ref[...], jnp.concatenate(parts(values), axis=0))
    return solved[:north] + solved[north:]


def pick(column, me):
    value = float(column[0])
    for k in range(1, len(column)):
        value = jnp.where(me == k, float(column[k]), value)
    return value


def send_all(ends, table, me, out_refs):
    for d, out_ref in enumerate(out_refs):
        out_ref[...] = pick(table[:, 2 * d], me) * ends[0] + pick(table[:, 2 * d + 1], me) * ends[1]


def take_all(ends, table, me, messages):
    left = right = 0.0
    for d, message in enumerate(messages):
        left += pick(table[:, 8 + 2 * d], me) * message
        right += pick(table[:, 9 + 2 * d], me) * message
    known = (left, right) + tuple(ends)
    return [sum(pick(table[:, 4 * side + k], me) * known[k] for k in range(4)) for side in range(2)]


def diagonal(size):
    return lax.broadcasted_iota(jnp.int32, (size, size), 0) == lax.broadcasted_iota(jnp.int32, (size, size), 1)


def as_row(column):
    return jnp.sum(jnp.where(diagonal(column.shape[0]), column, 0.0), axis=0, keepdims=True)


def stacked(rows, height):
    filler = jnp.zeros((height - sum(row.shape[0] for row in rows), rows[0].shape[1]), F32)
    return jnp.concatenate(list(rows) + [filler], axis=0)


def ordered(pair, east):
    if not pair:
        return lambda i: i
    flip = lax.axis_index("gx")
    return lambda i: jnp.where(flip == 0, i, east - 1 - i)


def end_places(count, east):
    if count == 1:
        return [(east - 1, 0)]
    return [(0, 0), (east - 1, 1)]


def local_kernel(
    pair, group, factors, sending,
    tables_hbm, warmth_hbm, supply_hbm,
    swept_ref, warmth_ref, upward_ends_ref, north_ends_ref, east_ends_ref, *rest,
):
    to_up = sending.shape[1] // 2
    up_refs = rest[:to_up]
    supply_ref, both_ref, edges_ref, tables_ref, up_ref, north_ref, even_ref, odd_ref, sems = rest[to_up:]
    east, north, upward = supply_ref.shape
    groups = east // group
    count = east_ends_ref.shape[0]
    place = ordered(pair, east)

    def fetch(which, g):
        start = jnp.minimum(place(g * group), place(g * group + group - 1))
        block = pl.ds(start, group)
        if which == 0:
            return pltpu.make_async_copy(warmth_hbm.at[block], warmth_ref.at[pl.ds(start + 1, group)], sems.at[0, g])
        return pltpu.make_async_copy(supply_hbm.at[block], supply_ref.at[block], sems.at[1, g])

    tables = pltpu.make_async_copy(tables_hbm, tables_ref, sems.at[0, groups])
    tables.start()
    for g in range(groups):
        for which in range(2):
            fetch(which, g).start()
    warmth_ref[0] = jnp.zeros((north, upward), F32)
    warmth_ref[east + 1] = jnp.zeros((north, upward), F32)
    both_ref[...] = jnp.zeros_like(both_ref)
    east_ends_ref[...] = jnp.zeros_like(east_ends_ref)
    lane = lax.broadcasted_iota(jnp.int32, (1, 2 * east), 1)
    line = lax.broadcasted_iota(jnp.int32, (north, 1), 0)
    tables.wait()
    up_ref[...] = tables_ref[: 3 * upward].astype(BF16)
    north_ref[...] = tables_ref[3 * upward : 3 * upward + 2 * north, : 2 * north].astype(BF16)
    sweep = 3 * upward + 2 * north
    fetch(0, 0).wait()

    def arrive(g):
        fetch(1, g).wait()

        @pl.when(g + 1 < groups)
        def _():
            fetch(0, g + 1).wait()

    def upward_part(g, slot_ref):
        heat_list = []
        for k in range(group):
            i = g * group + k
            x = place(i)
            warm = warmth_ref[x + 1]
            bent = (warmth_ref[x] - warm) + (warmth_ref[x + 2] - warm)
            low = jnp.where(line == 0, 0.0, pltpu.roll(warm, 1, 0))
            high = jnp.where(line == north - 1, 0.0, pltpu.roll(warm, north - 1, 0))
            bent += (factors[1] / factors[0]) * ((low - warm) + (high - warm))
            heat_list.append((supply_ref[x] + 2.0 * warm) + factors[0] * bent)
            edges_ref[pl.ds(i, 1)] = warm[:1]
            edges_ref[pl.ds(east + i, 1)] = warm[north - 1 :]
        slot_ref[...] = upward_dot(jnp.concatenate(heat_list, axis=0), up_ref)

    def north_part(g, slot_ref):
        for k in range(group):
            i = g * group + k
            first = slot_ref[k * north : (k + 1) * north]
            heads = pltpu.roll(first[:, : 2 * east], i, 1)
            tails = pltpu.roll(first[:, upward - 2 * east :], east + 1 + i, 1)
            both = jnp.where(lane == i, heads, both_ref[...])
            both_ref[...] = jnp.where(lane == east + i, tails, both)
            solved = north_dot(north_ref, first - 2.0 * warmth_ref[place(i) + 1])
            north_ends_ref[0, pl.ds(i, 1), :] = solved[:1]
            north_ends_ref[1, pl.ds(i, 1), :] = solved[north - 1 :]
            scale, ratio = (tables_ref[pl.ds(sweep + n * east + i, 1), :] for n in range(2))
            swept = scale * solved + ratio * east_ends_ref[count - 1]
            swept_ref[i] = swept
            east_ends_ref[count - 1] = swept
            if not pair:
                east_ends_ref[0] += tables_ref[pl.ds(sweep + 2 * east + i, 1), :] * swept

    arrive(0)
    upward_part(0, even_ref)

    def body(j, _):
        g = 2 * j
        arrive(g + 1)
        upward_part(g + 1, odd_ref)
        north_part(g, even_ref)
        later = jnp.minimum(g + 2, groups - 1)

        @pl.when(g + 2 < groups)
        def _():
            arrive(g + 2)

        upward_part(later, even_ref)
        north_part(g + 1, odd_ref)
        return 0

    lax.fori_loop(0, groups // 2, body, 0)

    ends = end_places(count, east)
    planes = [warmth_ref[place(i) + 1] for i, _ in ends]
    solved_up = upward_dot(jnp.concatenate([edges_ref[...]] + planes, axis=0), up_ref)
    height = north_ends_ref.shape[1]
    rows = [[], []]
    for p in range(count):
        solved = north_dot(north_ref, solved_up[2 * east + p * north : 2 * east + (p + 1) * north])
        rows[0].append(solved[:1])
        rows[1].append(solved[north - 1 :])
        east_ends_ref[p] += 2.0 * solved
    for end in range(2):
        north_ends_ref[end, :east] += 2.0 * solved_up[end * east : (end + 1) * east]
        north_ends_ref[end, east:] = stacked(rows[end], height - east)

    half = north // 2
    top, bottom = both_ref[:half], both_ref[half:]
    folded = (
        jnp.where(lane < east, top, pltpu.roll(bottom, east, 1)),
        jnp.where(lane < east, pltpu.roll(top, east, 1), bottom),
    )
    upward_ends = []
    for end, column in enumerate((slice(0, 1), slice(upward - 1, upward))):
        extra = [as_row(solved_up[k * north : (k + 1) * north, column]) for k in range(1 + count)]
        upward_ends.append(stacked([folded[end]] + extra, upward_ends_ref.shape[1]))
        upward_ends_ref[end] = upward_ends[end]
    send_all(upward_ends, sending, lax.axis_index("gz"), up_refs)


def upward_kernel(
    count, taking, sending,
    ends_ref, north_ends_ref, east_ends_ref, north_inverse_ref, east_twice_ref, spikes_ref, spread_ref, *rest,
):
    taken = (taking.shape[1] - 8) // 2
    message_refs = rest[:taken]
    columns_ref, north_out_ref, east_out_ref, *out_refs = rest[taken:]
    north, lanes = columns_ref.shape
    east, half = lanes // 2, north // 2
    lane = lax.broadcasted_iota(jnp.int32, (1, lanes), 1)
    before, after = take_all(
        (ends_ref[0], ends_ref[1]), taking, lax.axis_index("gz"), [ref[...] for ref in message_refs]
    )

    def paired(end, rows):
        if end == 0:
            return jnp.where(lane < east, before[rows], pltpu.roll(after[rows], east, 1))
        return jnp.where(lane < east, pltpu.roll(before[rows], east, 1), after[rows])

    solved = exact_dot(north_inverse_ref[...], jnp.concatenate([paired(0, slice(0, half)), paired(1, slice(0, half))], axis=0))
    columns = exact_dot(solved, east_twice_ref[...])
    columns_ref[...] = columns
    planes = []
    for p in range(count):
        row = slice(half + 1 + p, half + 2 + p)
        planes.append([
            jnp.sum(north_inverse_ref[...] * side[row], axis=1, keepdims=True) for side in (before, after)
        ])
    height = north_ends_ref.shape[1]
    shape = (height, lanes)
    row = lax.broadcasted_iota(jnp.int32, shape, 0)
    short = lax.broadcasted_iota(jnp.int32, shape, 1) % east
    own = (row < east) & (short == row)
    behind = (row >= east) & (row < east + count) & (short == row - east)
    picked = []
    for end, y in enumerate((0, north - 1)):
        first = solved[y : y + 1] + 2.0 * paired(end, slice(half, half + 1))
        second = jnp.zeros((1, lanes), F32)
        for _, k in end_places(count, east):
            for side in range(2):
                second = jnp.where(lane == side * east + k, planes[k][side][y : y + 1], second)
        picked.append(jnp.where(own, first, 0.0) + jnp.where(behind, second, 0.0))
    added = exact_dot(jnp.concatenate(picked, axis=0), spread_ref[...])
    ends = []
    for end in range(2):
        ends.append(north_ends_ref[end] + added[end * height : (end + 1) * height])
        north_out_ref[end] = ends[end]
    send_all(ends, sending, lax.axis_index("gy"), out_refs)
    for i, k in end_places(count, east):
        total = east_ends_ref[k]
        for side in range(2):
            column = columns[:, side * east + i : side * east + i + 1] + 2.0 * planes[k][side]
            total += column * spikes_ref[side : side + 1, :]
        east_out_ref[k] = total


def north_kernel(
    count, taking,
    ends_ref, east_ends_ref, east_inverse_ref, spikes_ref, *rest,
):
    taken = (taking.shape[1] - 8) // 2
    message_refs = rest[:taken]
    rows_ref, east_out_ref = rest[taken:]
    east = rows_ref.shape[1]
    sides = take_all((ends_ref[0], ends_ref[1]), taking, lax.axis_index("gy"), [ref[...] for ref in message_refs])
    swept = [exact_dot(east_inverse_ref[...], side[:east]) for side in sides]
    for n in range(2):
        rows_ref[n] = swept[n]
    for i, k in end_places(count, east):
        total = east_ends_ref[k]
        for n in range(2):
            total += spikes_ref[n] * (swept[n][i : i + 1] + 2.0 * sides[n][east + k : east + k + 1])
        east_out_ref[k] = total


def final_kernel(
    pair, table, tile,
    sweep_ref, own_ref, other_ref,
    swept_ref, warmth_ref, columns_ref, rows_ref, upward_spikes_ref, north_spikes_ref,
    out_hbm,
    out_ref, sides_ref, sems,
):
    east, north, upward = out_ref.shape
    place = ordered(pair, east)

    if pair:
        sides_ref[0] = float(table[0]) * other_ref[0] + float(table[1]) * own_ref[0]
    else:
        me = lax.axis_index("gx")
        for side in range(2):
            plane = 0.0
            for m in range(table.shape[0]):
                for end in range(2):
                    plane += pick(table[:, side, 2 * m + end], me) * other_ref[m, end]
            sides_ref[side] = plane
    last = sides_ref.shape[0] - 1

    def send(t):
        block = pl.ds(pl.multiple_of(t * tile, tile), tile)
        return pltpu.make_async_copy(out_ref.at[:, block], out_hbm.at[:, block], sems.at[t])

    def body(t, _):
        block = pl.ds(pl.multiple_of(t * tile, tile), tile)
        value = sides_ref[last, block]
        columns = columns_ref[block]
        first_spike, last_spike = north_spikes_ref[0, block], north_spikes_ref[1, block]
        for i in reversed(range(east)):
            value = swept_ref[i, block] + sweep_ref[1, i] * value
            if not pair:
                value += sweep_ref[3, i] * sides_ref[0, block]
            added = (
                columns[:, i : i + 1] * upward_spikes_ref[0:1, :]
                + columns[:, east + i : east + i + 1] * upward_spikes_ref[1:2, :]
            )
            added += first_spike * rows_ref[0, i : i + 1, :] + last_spike * rows_ref[1, i : i + 1, :]
            x = place(i)
            out_ref[x, block] = warmth_ref[x + 1, block] + value + added
        send(t).start()
        return 0

    lax.fori_loop(0, north // tile, body, 0)
    for t in range(north // tile):
        send(t).wait()


def spread_out(messages, axis):
    members = lax.axis_size(axis)
    return [
        lax.ppermute(message, axis, [(k, peers(k, members, d + 1)[0]) for k in range(members)])
        for d, message in enumerate(messages)
    ]


def local(initial_warmth, heat_supply):
    shape = east, north, upward = initial_warmth.shape
    members = [lax.axis_size(axis) for axis in ("gx", "gy", "gz")]
    factors = [float((n * m) ** 2 // 4) for n, m in zip(shape, members)]
    lines = [line_tables(n, factor) for n, factor in zip(shape, factors)]
    sweep = sweep_table(east, factors[0]).astype(np.float32)
    exchanges = [exchange_tables(line[1], line[2], m) for line, m in zip(lines, members)]
    upward_high, upward_low = split(lines[2][0], 0)
    north_high, north_low = split(lines[1][0], 1)
    north_stack = np.block([[north_high, north_high], [north_low, np.zeros_like(north_low)]])
    tables = np.concatenate([
        np.concatenate([upward_high, upward_high, upward_low]).astype(np.float32),
        np.pad(north_stack.astype(np.float32), ((0, 0), (0, max(upward - 2 * north, 0)))),
        np.repeat(sweep.reshape(-1, 1), upward, axis=1),
    ])
    east_inverse = lines[0][0].astype(np.float32)
    north_inverse = lines[1][0].astype(np.float32)
    east_twice = np.kron(np.eye(2), lines[0][0]).astype(np.float32)
    upward_spikes = np.stack(lines[2][1:]).astype(np.float32)
    spread = np.repeat(upward_spikes, east, axis=0)
    north_spikes = np.broadcast_to(np.stack(lines[1][1:])[:, :, None], (2, north, upward)).astype(np.float32)

    pair = members[0] == 2
    count = 1 if pair else 2
    height = east + 8
    to_up, to_north = members[2] - 1, members[1] - 1
    vmem = pl.BlockSpec(memory_space=pltpu.VMEM)
    smem = pl.BlockSpec(memory_space=pltpu.SMEM)
    hbm = pl.BlockSpec(memory_space=pltpu.HBM)

    def kept(*sizes):
        return jax.ShapeDtypeStruct(sizes, F32)

    group = 4
    folded = kept(north // 2 + 8, 2 * east)
    swept, warmth, upward_ends, north_ends, east_ends, *messages = pl.pallas_call(
        functools.partial(local_kernel, pair, group, factors, exchanges[2][0]),
        in_specs=[hbm] * 3,
        out_specs=[vmem] * (5 + to_up),
        out_shape=[
            pltpu.VMEM(shape, F32),
            pltpu.VMEM((east + 2, north, upward), F32),
            kept(2, *folded.shape),
            kept(2, height, upward),
            kept(count, north, upward),
        ]
        + [folded] * to_up,
        scratch_shapes=[
            pltpu.VMEM(shape, F32),
            pltpu.VMEM((north, 2 * east), F32),
            pltpu.VMEM((2 * east, upward), F32),
            pltpu.VMEM(tables.shape, F32),
            pltpu.VMEM((3 * upward, upward), BF16),
            pltpu.VMEM((2 * north, 2 * north), BF16),
            pltpu.VMEM((group * north, upward), F32),
            pltpu.VMEM((group * north, upward), F32),
            pltpu.SemaphoreType.DMA((2, east // group + 1)),
        ],
        compiler_params=pltpu.CompilerParams(vmem_limit_bytes=32 * MIB),
    )(pltpu.with_memory_space_constraint(jnp.asarray(tables), pltpu.HBM), initial_warmth, heat_supply)

    messages = spread_out(messages, "gz")
    columns, north_ends, east_ends, *messages = pl.pallas_call(
        functools.partial(upward_kernel, count, exchanges[2][1], exchanges[1][0]),
        in_specs=[vmem] * (7 + to_up),
        out_specs=[vmem] * (3 + to_north),
        out_shape=[kept(north, 2 * east), kept(2, height, upward), kept(count, north, upward)]
        + [kept(height, upward)] * to_north,
        compiler_params=pltpu.CompilerParams(vmem_limit_bytes=6 * MIB),
    )(upward_ends, north_ends, east_ends, north_inverse, east_twice, upward_spikes, spread, *messages)

    messages = spread_out(messages, "gy")
    rows, own = pl.pallas_call(
        functools.partial(north_kernel, count, exchanges[1][1]),
        in_specs=[vmem] * (4 + to_north),
        out_specs=[vmem] * 2,
        out_shape=[kept(2, east, upward), kept(count, north, upward)],
        compiler_params=pltpu.CompilerParams(vmem_limit_bytes=6 * MIB),
    )(north_ends, east_ends, east_inverse, north_spikes, *messages)

    if pair:
        other = lax.ppermute(own, "gx", [(0, 1), (1, 0)])
        near = lines[0][1][0]
        table = np.array([1.0, near]) / (1.0 - near**2)
    else:
        other = lax.all_gather(own, "gx")
        table = interface_table(lines[0][1], lines[0][2], members[0])
    swept = pltpu.with_memory_space_constraint(swept, pltpu.VMEM)
    warmth = pltpu.with_memory_space_constraint(warmth, pltpu.VMEM)
    tile = 32
    return pl.pallas_call(
        functools.partial(final_kernel, pair, table, tile),
        in_specs=[smem] + [vmem] * 8,
        out_specs=hbm,
        out_shape=kept(*shape),
        scratch_shapes=[
            pltpu.VMEM(shape, F32),
            pltpu.VMEM((count, north, upward), F32),
            pltpu.SemaphoreType.DMA((north // tile,)),
        ],
        compiler_params=pltpu.CompilerParams(vmem_limit_bytes=16 * MIB),
    )(sweep, own, other, swept, warmth, columns, rows, upward_spikes, north_spikes)


def solution(mesh):
    return jax.shard_map(
        local,
        mesh=mesh,
        in_specs=(P("gx", "gy", "gz"), P("gx", "gy", "gz")),
        out_specs=P("gx", "gy", "gz"),
        check_vma=False,
    )
```

```python
import functools

import jax
import jax.numpy as jnp
import numpy as np
from jax import lax
from jax.experimental import pallas as pl
from jax.experimental.pallas import tpu as pltpu
from jax.sharding import PartitionSpec as P

F32 = jnp.float32
BF16 = jnp.bfloat16
MIB = 1 << 20


def line_tables(length, factor):
    matrix = (1.0 + factor) * np.eye(length)
    matrix -= 0.5 * factor * (np.eye(length, k=1) + np.eye(length, k=-1))
    inverse = np.linalg.inv(matrix)
    inverse = 0.5 * (inverse + inverse.T)
    return inverse, 0.5 * factor * inverse[:, 0], 0.5 * factor * inverse[:, -1]


def chain_system(near, far, members):
    system = np.eye(2 * members)
    for m in range(members):
        if m > 0:
            system[2 * m, 2 * m - 1] -= near
            system[2 * m + 1, 2 * m - 1] -= far
        if m < members - 1:
            system[2 * m, 2 * m + 2] -= far
            system[2 * m + 1, 2 * m + 2] -= near
    return np.linalg.inv(system)


def interface_table(before, after, members):
    solved = chain_system(before[0], before[-1], members)
    rows = np.zeros((members, 2, 2 * members))
    for m in range(members):
        if m > 0:
            rows[m, 0] = solved[2 * m - 1]
        if m < members - 1:
            rows[m, 1] = solved[2 * m + 2]
    return rows


def peers(member, members, distance):
    if members & (members - 1) == 0:
        return member ^ distance, member ^ distance
    return (member + distance) % members, (member - distance) % members


def exchange_tables(before, after, members):
    near, far = before[0], before[-1]
    sending = np.zeros((members, 2 * (members - 1)))
    taking = np.zeros((members, 8 + 2 * (members - 1)))
    for m in range(members):
        right = chain_system(near, far, members - 1 - m)
        left = chain_system(near, far, m)
        for d in range(1, members):
            k = peers(m, members, d)[1]
            if k > m:
                sending[k, 2 * d - 2 : 2 * d] = right[0, 2 * (k - m - 1) : 2 * (k - m)]
                taking[m, 8 + 2 * d - 1] = 1.0
            else:
                sending[k, 2 * d - 2 : 2 * d] = left[-1, 2 * k : 2 * k + 2]
                taking[m, 8 + 2 * d - 2] = 1.0
        pull_left = answer(near, far, m)
        pull_right = answer(near, far, members - 1 - m)
        system = np.array([
            [1.0, 0.0, -pull_left, 0.0],
            [0.0, 1.0, 0.0, -pull_right],
            [-near, -far, 1.0, 0.0],
            [-far, -near, 0.0, 1.0],
        ])
        taking[m, :8] = np.linalg.inv(system)[:2].reshape(8)
    return sending, taking


def answer(near, far, members):
    if members == 0:
        return 0.0
    push = np.zeros(2 * members)
    push[0], push[1] = near, far
    return chain_system(near, far, members)[0] @ push


def sweep_table(length, factor):
    half = 0.5 * factor
    ratio = np.zeros(length)
    last = 0.0
    for i in range(length):
        ratio[i] = last = half / (1.0 + factor - half * last)
    decay = np.cumprod(ratio)
    return np.stack([ratio, decay, decay])


def split(table, axis):
    rows = np.moveaxis(np.asarray(table, np.float64), axis, 0)
    high = np.zeros(rows.shape, BF16)
    carried = np.zeros(rows.shape[1:])
    for k, row in enumerate(rows):
        high[k] = (row + carried).astype(np.float32).astype(BF16)
        carried = carried + row - high[k].astype(np.float64)
    low = (rows - high.astype(np.float64)).astype(np.float32).astype(BF16)
    return np.moveaxis(high, 0, axis), np.moveaxis(low, 0, axis)


def parts(values):
    high = values.astype(BF16)
    return high, (values - high.astype(F32)).astype(BF16)


def dot(a, b):
    return jnp.dot(a, b, preferred_element_type=F32)


def exact_dot(a, b):
    return jnp.dot(a, b, precision=lax.Precision.HIGHEST, preferred_element_type=F32)


def upward_dot(high, low, table_ref):
    return dot(jnp.concatenate([high, low, high], axis=1), table_ref[...])


def north_dot(table_ref, values):
    north = values.shape[0]
    solved = dot(table_ref[...], jnp.concatenate(parts(values), axis=0))
    return solved[:north] + solved[north:]


def pick(column, me):
    value = float(column[0])
    for k in range(1, len(column)):
        value = jnp.where(me == k, float(column[k]), value)
    return value


def send_all(ends, table, me, out_refs):
    for d, out_ref in enumerate(out_refs):
        out_ref[...] = pick(table[:, 2 * d], me) * ends[0] + pick(table[:, 2 * d + 1], me) * ends[1]


def take_all(ends, table, me, messages):
    left = right = 0.0
    for d, message in enumerate(messages):
        left += pick(table[:, 8 + 2 * d], me) * message
        right += pick(table[:, 9 + 2 * d], me) * message
    known = (left, right) + tuple(ends)
    return [sum(pick(table[:, 4 * side + k], me) * known[k] for k in range(4)) for side in range(2)]


def diagonal(size):
    return lax.broadcasted_iota(jnp.int32, (size, size), 0) == lax.broadcasted_iota(jnp.int32, (size, size), 1)


def as_row(column):
    return jnp.sum(jnp.where(diagonal(column.shape[0]), column, 0.0), axis=0, keepdims=True)


def stacked(rows, height):
    filler = jnp.zeros((height - sum(row.shape[0] for row in rows), rows[0].shape[1]), F32)
    return jnp.concatenate(list(rows) + [filler], axis=0)


def ordered(pair, east):
    if not pair:
        return lambda i: i
    flip = lax.axis_index("gx")
    return lambda i: jnp.where(flip == 0, i, east - 1 - i)


def end_places(count, east):
    if count == 1:
        return [(east - 1, 0)]
    return [(0, 0), (east - 1, 1)]


def local_kernel(
    pair, group, factors, sending,
    tables_hbm, warmth_hbm, supply_hbm,
    swept_ref, warmth_ref, upward_ends_ref, north_ends_ref, east_ends_ref, *rest,
):
    to_up = sending.shape[1] // 2
    up_refs = rest[:to_up]
    supply_ref, both_ref, edges_ref, tables_ref, up_ref, north_ref, halves_ref, even_ref, odd_ref, sems = rest[to_up:]
    east, north, upward = supply_ref.shape
    groups = east // group
    count = east_ends_ref.shape[0]
    place = ordered(pair, east)

    def fetch(which, g):
        start = jnp.minimum(place(g * group), place(g * group + group - 1))
        block = pl.ds(start, group)
        if which == 0:
            return pltpu.make_async_copy(warmth_hbm.at[block], warmth_ref.at[pl.ds(start + 1, group)], sems.at[0, g])
        return pltpu.make_async_copy(supply_hbm.at[block], supply_ref.at[block], sems.at[1, g])

    tables = pltpu.make_async_copy(tables_hbm, tables_ref, sems.at[0, groups])
    tables.start()
    for g in range(groups):
        for which in range(2):
            fetch(which, g).start()
    warmth_ref[0] = jnp.zeros((north, upward), F32)
    warmth_ref[east + 1] = jnp.zeros((north, upward), F32)
    both_ref[...] = jnp.zeros_like(both_ref)
    east_ends_ref[...] = jnp.zeros_like(east_ends_ref)
    lane = lax.broadcasted_iota(jnp.int32, (1, 2 * east), 1)
    line = lax.broadcasted_iota(jnp.int32, (8, 1), 0)
    half_factor = 0.5 * factors[0]
    width = min(upward, 128)
    swept_ref[0] = jnp.zeros((north, upward), F32)
    tables.wait()
    up_ref[...] = tables_ref[: 3 * upward].astype(BF16)
    north_ref[...] = tables_ref[3 * upward : 3 * upward + 2 * north, : 2 * north].astype(BF16)
    sweep = 3 * upward + 2 * north
    fetch(0, 0).wait()

    def arrive(g):
        fetch(1, g).wait()

        @pl.when(g + 1 < groups)
        def _():
            fetch(0, g + 1).wait()

    def shifted(values, step):
        turned = pltpu.roll(values, step % north, 0)
        if step > 0:
            return jnp.concatenate([jnp.where(line == 0, 0.0, turned[:8]), turned[8:]], axis=0)
        return jnp.concatenate([turned[:-8], jnp.where(line == 7, 0.0, turned[-8:])], axis=0)

    def upward_part(g, slot_ref):
        for k in range(group):
            i = g * group + k
            x = place(i)
            rows = slice(k * north, (k + 1) * north)
            edges_ref[pl.ds(i, 1)] = warmth_ref[x + 1, :1]
            edges_ref[pl.ds(east + i, 1)] = warmth_ref[x + 1, north - 1 :]
            for start in range(0, upward, width):
                lanes = slice(start, start + width)
                warm = warmth_ref[x + 1, :, lanes]
                bent = (warmth_ref[x, :, lanes] - warm) + (warmth_ref[x + 2, :, lanes] - warm)
                across = (shifted(warm, 1) - warm) + (shifted(warm, -1) - warm)
                heat = (supply_ref[x, :, lanes] + 2.0 * warm) + (factors[0] * bent + factors[1] * across)
                high, low = parts(heat)
                halves_ref[rows, lanes] = high
                halves_ref[rows, start + upward : start + upward + width] = low
        slot_ref[...] = upward_dot(halves_ref[:, :upward], halves_ref[:, upward:], up_ref)

    def north_part(g, slot_ref):
        for k in range(group):
            i = g * group + k
            x = place(i)
            rows = slice(k * north, (k + 1) * north)
            heads = pltpu.roll(slot_ref[rows, : 2 * east], i, 1)
            tails = pltpu.roll(slot_ref[rows, upward - 2 * east :], east + 1 + i, 1)
            both = jnp.where(lane == i, heads, both_ref[...])
            both_ref[...] = jnp.where(lane == east + i, tails, both)
            pieces = []
            for start in range(0, upward, width):
                lanes = slice(start, start + width)
                pieces.append(jnp.concatenate(parts(slot_ref[rows, lanes] - 2.0 * warmth_ref[x + 1, :, lanes]), axis=0))
            solved = dot(north_ref[...], jnp.concatenate(pieces, axis=1))
            before = jnp.maximum(i - 1, 0)
            north_ends_ref[0, pl.ds(i, 1)] = half_factor * (solved[:1] + solved[north : north + 1])
            north_ends_ref[1, pl.ds(i, 1)] = half_factor * (solved[north - 1 : north] + solved[2 * north - 1 :])
            ratio = tables_ref[pl.ds(sweep + i, 1), :]
            weight = tables_ref[pl.ds(sweep + east + i, 1), :]
            for start in range(0, upward, width):
                lanes = slice(start, start + width)
                whole = solved[:north, lanes] + solved[north:, lanes]
                swept = whole + ratio[:, lanes] * swept_ref[before, :, lanes]
                swept_ref[i, :, lanes] = swept
                if not pair:
                    east_ends_ref[0, :, lanes] += weight[:, lanes] * swept
        return 0

    arrive(0)
    upward_part(0, even_ref)

    def body(j, _):
        g = 2 * j
        arrive(g + 1)
        upward_part(g + 1, odd_ref)
        north_part(g, even_ref)
        later = jnp.minimum(g + 2, groups - 1)

        @pl.when(g + 2 < groups)
        def _():
            arrive(g + 2)

        upward_part(later, even_ref)
        north_part(g + 1, odd_ref)
        return 0

    lax.fori_loop(0, groups // 2, body, 0)

    ends = end_places(count, east)
    planes = [warmth_ref[place(i) + 1] for i, _ in ends]
    solved_up = upward_dot(*parts(jnp.concatenate([edges_ref[...]] + planes, axis=0)), up_ref)
    east_ends_ref[count - 1] = tables_ref[sweep + 2 * east : sweep + 2 * east + 1, :] * swept_ref[east - 1]
    height = north_ends_ref.shape[1]
    rows = [[], []]
    for p in range(count):
        solved = half_factor * north_dot(north_ref, solved_up[2 * east + p * north : 2 * east + (p + 1) * north])
        rows[0].append(solved[:1])
        rows[1].append(solved[north - 1 :])
        east_ends_ref[p] += 2.0 * solved
    for end in range(2):
        north_ends_ref[end, :east] += 2.0 * solved_up[end * east : (end + 1) * east]
        north_ends_ref[end, east:] = stacked(rows[end], height - east)

    half = north // 2
    top, bottom = both_ref[:half], both_ref[half:]
    folded = (
        jnp.where(lane < east, top, pltpu.roll(bottom, east, 1)),
        jnp.where(lane < east, pltpu.roll(top, east, 1), bottom),
    )
    upward_ends = []
    for end, column in enumerate((slice(0, 1), slice(upward - 1, upward))):
        extra = [as_row(solved_up[k * north : (k + 1) * north, column]) for k in range(1 + count)]
        upward_ends.append(stacked([folded[end]] + extra, upward_ends_ref.shape[1]))
        upward_ends_ref[end] = upward_ends[end]
    send_all(upward_ends, sending, lax.axis_index("gz"), up_refs)


def upward_kernel(
    count, taking, sending,
    ends_ref, north_ends_ref, east_ends_ref, north_inverse_ref, east_twice_ref, spikes_ref, spread_ref, *rest,
):
    taken = (taking.shape[1] - 8) // 2
    message_refs = rest[:taken]
    columns_ref, north_out_ref, east_out_ref, *out_refs = rest[taken:]
    north, lanes = columns_ref.shape
    east, half = lanes // 2, north // 2
    lane = lax.broadcasted_iota(jnp.int32, (1, lanes), 1)
    before, after = take_all(
        (ends_ref[0], ends_ref[1]), taking, lax.axis_index("gz"), [ref[...] for ref in message_refs]
    )

    def paired(end, rows):
        if end == 0:
            return jnp.where(lane < east, before[rows], pltpu.roll(after[rows], east, 1))
        return jnp.where(lane < east, pltpu.roll(before[rows], east, 1), after[rows])

    solved = exact_dot(north_inverse_ref[...], jnp.concatenate([paired(0, slice(0, half)), paired(1, slice(0, half))], axis=0))
    columns = exact_dot(solved, east_twice_ref[...])
    columns_ref[...] = columns
    planes = []
    for p in range(count):
        row = slice(half + 1 + p, half + 2 + p)
        planes.append([
            jnp.sum(north_inverse_ref[...] * side[row], axis=1, keepdims=True) for side in (before, after)
        ])
    height = north_ends_ref.shape[1]
    shape = (height, lanes)
    row = lax.broadcasted_iota(jnp.int32, shape, 0)
    short = lax.broadcasted_iota(jnp.int32, shape, 1) % east
    own = (row < east) & (short == row)
    behind = (row >= east) & (row < east + count) & (short == row - east)
    picked = []
    for end, y in enumerate((0, north - 1)):
        first = solved[y : y + 1] + 2.0 * paired(end, slice(half, half + 1))
        second = jnp.zeros((1, lanes), F32)
        for _, k in end_places(count, east):
            for side in range(2):
                second = jnp.where(lane == side * east + k, planes[k][side][y : y + 1], second)
        picked.append(jnp.where(own, first, 0.0) + jnp.where(behind, second, 0.0))
    added = exact_dot(jnp.concatenate(picked, axis=0), spread_ref[...])
    ends = []
    for end in range(2):
        ends.append(north_ends_ref[end] + added[end * height : (end + 1) * height])
        north_out_ref[end] = ends[end]
    send_all(ends, sending, lax.axis_index("gy"), out_refs)
    for i, k in end_places(count, east):
        total = east_ends_ref[k]
        for side in range(2):
            column = columns[:, side * east + i : side * east + i + 1] + 2.0 * planes[k][side]
            total += column * spikes_ref[side : side + 1, :]
        east_out_ref[k] = total


def north_kernel(
    count, taking,
    ends_ref, east_ends_ref, east_inverse_ref, spikes_ref, *rest,
):
    taken = (taking.shape[1] - 8) // 2
    message_refs = rest[:taken]
    rows_ref, east_out_ref = rest[taken:]
    east = rows_ref.shape[1]
    sides = take_all((ends_ref[0], ends_ref[1]), taking, lax.axis_index("gy"), [ref[...] for ref in message_refs])
    swept = [exact_dot(east_inverse_ref[...], side[:east]) for side in sides]
    for n in range(2):
        rows_ref[n] = swept[n]
    for i, k in end_places(count, east):
        total = east_ends_ref[k]
        for n in range(2):
            total += spikes_ref[n] * (swept[n][i : i + 1] + 2.0 * sides[n][east + k : east + k + 1])
        east_out_ref[k] = total


def final_kernel(
    pair, table, tile,
    sweep_ref, own_ref, other_ref,
    swept_ref, warmth_ref, columns_ref, rows_ref, upward_spikes_ref, north_spikes_ref,
    out_hbm,
    out_ref, sides_ref, sems,
):
    east, north, upward = out_ref.shape
    place = ordered(pair, east)

    if pair:
        sides_ref[0] = float(table[0]) * other_ref[0] + float(table[1]) * own_ref[0]
    else:
        me = lax.axis_index("gx")
        for side in range(2):
            plane = 0.0
            for m in range(table.shape[0]):
                for end in range(2):
                    plane += pick(table[:, side, 2 * m + end], me) * other_ref[m, end]
            sides_ref[side] = plane
    last = sides_ref.shape[0] - 1

    def send(t):
        block = pl.ds(pl.multiple_of(t * tile, tile), tile)
        return pltpu.make_async_copy(out_ref.at[:, block], out_hbm.at[:, block], sems.at[t])

    def body(t, _):
        block = pl.ds(pl.multiple_of(t * tile, tile), tile)
        value = sides_ref[last, block]
        columns = columns_ref[block]
        first_spike, last_spike = north_spikes_ref[0, block], north_spikes_ref[1, block]
        for i in reversed(range(east)):
            value = sweep_ref[0, i] * (swept_ref[i, block] + value)
            if not pair:
                value += sweep_ref[2, i] * sides_ref[0, block]
            added = (
                columns[:, i : i + 1] * upward_spikes_ref[0:1, :]
                + columns[:, east + i : east + i + 1] * upward_spikes_ref[1:2, :]
            )
            added += first_spike * rows_ref[0, i : i + 1, :] + last_spike * rows_ref[1, i : i + 1, :]
            x = place(i)
            out_ref[x, block] = warmth_ref[x + 1, block] + value + added
        send(t).start()
        return 0

    lax.fori_loop(0, north // tile, body, 0)
    for t in range(north // tile):
        send(t).wait()


def spread_out(messages, axis):
    members = lax.axis_size(axis)
    return [
        lax.ppermute(message, axis, [(k, peers(k, members, d + 1)[0]) for k in range(members)])
        for d, message in enumerate(messages)
    ]


def local(initial_warmth, heat_supply):
    shape = east, north, upward = initial_warmth.shape
    members = [lax.axis_size(axis) for axis in ("gx", "gy", "gz")]
    factors = [float((n * m) ** 2 // 4) for n, m in zip(shape, members)]
    lines = [line_tables(n, factor) for n, factor in zip(shape, factors)]
    sweep = sweep_table(east, factors[0])
    ratio, weights = sweep[:2]
    sweep = sweep.astype(np.float32)
    exchanges = [exchange_tables(line[1], line[2], m) for line, m in zip(lines, members)]
    upward_high, upward_low = split(lines[2][0], 0)
    north_high, north_low = split(lines[1][0] / (0.5 * factors[0]), 1)
    north_stack = np.block([[north_high, north_high], [north_low, np.zeros_like(north_low)]])
    tables = np.concatenate([
        np.concatenate([upward_high, upward_high, upward_low]).astype(np.float32),
        np.pad(north_stack.astype(np.float32), ((0, 0), (0, max(upward - 2 * north, 0)))),
        np.repeat(np.concatenate([[0.0], ratio[:-1], weights, ratio[-1:], np.zeros(7)])[:, None], upward, axis=1).astype(np.float32),
    ])
    east_inverse = lines[0][0].astype(np.float32)
    north_inverse = lines[1][0].astype(np.float32)
    east_twice = np.kron(np.eye(2), lines[0][0]).astype(np.float32)
    upward_spikes = np.stack(lines[2][1:]).astype(np.float32)
    spread = np.repeat(upward_spikes, east, axis=0)
    north_spikes = np.broadcast_to(np.stack(lines[1][1:])[:, :, None], (2, north, upward)).astype(np.float32)

    pair = members[0] == 2
    count = 1 if pair else 2
    height = east + 8
    to_up, to_north = members[2] - 1, members[1] - 1
    vmem = pl.BlockSpec(memory_space=pltpu.VMEM)
    smem = pl.BlockSpec(memory_space=pltpu.SMEM)
    hbm = pl.BlockSpec(memory_space=pltpu.HBM)

    def kept(*sizes):
        return jax.ShapeDtypeStruct(sizes, F32)

    group = 4
    folded = kept(north // 2 + 8, 2 * east)
    swept, warmth, upward_ends, north_ends, east_ends, *messages = pl.pallas_call(
        functools.partial(local_kernel, pair, group, factors, exchanges[2][0]),
        in_specs=[hbm] * 3,
        out_specs=[vmem] * (5 + to_up),
        out_shape=[
            pltpu.VMEM(shape, F32),
            pltpu.VMEM((east + 2, north, upward), F32),
            kept(2, *folded.shape),
            kept(2, height, upward),
            kept(count, north, upward),
        ]
        + [folded] * to_up,
        scratch_shapes=[
            pltpu.VMEM(shape, F32),
            pltpu.VMEM((north, 2 * east), F32),
            pltpu.VMEM((2 * east, upward), F32),
            pltpu.VMEM(tables.shape, F32),
            pltpu.VMEM((3 * upward, upward), BF16),
            pltpu.VMEM((2 * north, 2 * north), BF16),
            pltpu.VMEM((group * north, 2 * upward), BF16),
            pltpu.VMEM((group * north, upward), F32),
            pltpu.VMEM((group * north, upward), F32),
            pltpu.SemaphoreType.DMA((2, east // group + 1)),
        ],
        compiler_params=pltpu.CompilerParams(vmem_limit_bytes=32 * MIB),
    )(pltpu.with_memory_space_constraint(jnp.asarray(tables), pltpu.HBM), initial_warmth, heat_supply)

    messages = spread_out(messages, "gz")
    columns, north_ends, east_ends, *messages = pl.pallas_call(
        functools.partial(upward_kernel, count, exchanges[2][1], exchanges[1][0]),
        in_specs=[vmem] * (7 + to_up),
        out_specs=[vmem] * (3 + to_north),
        out_shape=[kept(north, 2 * east), kept(2, height, upward), kept(count, north, upward)]
        + [kept(height, upward)] * to_north,
        compiler_params=pltpu.CompilerParams(vmem_limit_bytes=6 * MIB),
    )(upward_ends, north_ends, east_ends, north_inverse, east_twice, upward_spikes, spread, *messages)

    messages = spread_out(messages, "gy")
    rows, own = pl.pallas_call(
        functools.partial(north_kernel, count, exchanges[1][1]),
        in_specs=[vmem] * (4 + to_north),
        out_specs=[vmem] * 2,
        out_shape=[kept(2, east, upward), kept(count, north, upward)],
        compiler_params=pltpu.CompilerParams(vmem_limit_bytes=6 * MIB),
    )(north_ends, east_ends, east_inverse, north_spikes, *messages)

    if pair:
        other = lax.ppermute(own, "gx", [(0, 1), (1, 0)])
        near = lines[0][1][0]
        table = np.array([1.0, near]) / (1.0 - near**2)
    else:
        other = lax.all_gather(own, "gx")
        table = interface_table(lines[0][1], lines[0][2], members[0])
    swept = pltpu.with_memory_space_constraint(swept, pltpu.VMEM)
    warmth = pltpu.with_memory_space_constraint(warmth, pltpu.VMEM)
    tile = 16
    return pl.pallas_call(
        functools.partial(final_kernel, pair, table, tile),
        in_specs=[smem] + [vmem] * 8,
        out_specs=hbm,
        out_shape=kept(*shape),
        scratch_shapes=[
            pltpu.VMEM(shape, F32),
            pltpu.VMEM((count, north, upward), F32),
            pltpu.SemaphoreType.DMA((north // tile,)),
        ],
        compiler_params=pltpu.CompilerParams(vmem_limit_bytes=16 * MIB),
    )(sweep, own, other, swept, warmth, columns, rows, upward_spikes, north_spikes)


def solution(mesh):
    return jax.shard_map(
        local,
        mesh=mesh,
        in_specs=(P("gx", "gy", "gz"), P("gx", "gy", "gz")),
        out_specs=P("gx", "gy", "gz"),
        check_vma=False,
    )
```

```python
import functools

import jax
import jax.numpy as jnp
import numpy as np
from jax import lax
from jax.experimental import pallas as pl
from jax.experimental.pallas import tpu as pltpu
from jax.sharding import PartitionSpec as P

F32 = jnp.float32
BF16 = jnp.bfloat16
MIB = 1 << 20


def line_tables(length, factor):
    matrix = (1.0 + factor) * np.eye(length)
    matrix -= 0.5 * factor * (np.eye(length, k=1) + np.eye(length, k=-1))
    inverse = np.linalg.inv(matrix)
    inverse = 0.5 * (inverse + inverse.T)
    return inverse, 0.5 * factor * inverse[:, 0], 0.5 * factor * inverse[:, -1]


def chain_system(near, far, members):
    system = np.eye(2 * members)
    for m in range(members):
        if m > 0:
            system[2 * m, 2 * m - 1] -= near
            system[2 * m + 1, 2 * m - 1] -= far
        if m < members - 1:
            system[2 * m, 2 * m + 2] -= far
            system[2 * m + 1, 2 * m + 2] -= near
    return np.linalg.inv(system)


def interface_table(before, after, members):
    solved = chain_system(before[0], before[-1], members)
    rows = np.zeros((members, 2, 2 * members))
    for m in range(members):
        if m > 0:
            rows[m, 0] = solved[2 * m - 1]
        if m < members - 1:
            rows[m, 1] = solved[2 * m + 2]
    return rows


def peers(member, members, distance):
    if members & (members - 1) == 0:
        return member ^ distance, member ^ distance
    return (member + distance) % members, (member - distance) % members


def exchange_tables(before, after, members):
    near, far = before[0], before[-1]
    sending = np.zeros((members, 2 * (members - 1)))
    taking = np.zeros((members, 8 + 2 * (members - 1)))
    for m in range(members):
        right = chain_system(near, far, members - 1 - m)
        left = chain_system(near, far, m)
        for d in range(1, members):
            k = peers(m, members, d)[1]
            if k > m:
                sending[k, 2 * d - 2 : 2 * d] = right[0, 2 * (k - m - 1) : 2 * (k - m)]
                taking[m, 8 + 2 * d - 1] = 1.0
            else:
                sending[k, 2 * d - 2 : 2 * d] = left[-1, 2 * k : 2 * k + 2]
                taking[m, 8 + 2 * d - 2] = 1.0
        pull_left = answer(near, far, m)
        pull_right = answer(near, far, members - 1 - m)
        system = np.array([
            [1.0, 0.0, -pull_left, 0.0],
            [0.0, 1.0, 0.0, -pull_right],
            [-near, -far, 1.0, 0.0],
            [-far, -near, 0.0, 1.0],
        ])
        taking[m, :8] = np.linalg.inv(system)[:2].reshape(8)
    return sending, taking


def answer(near, far, members):
    if members == 0:
        return 0.0
    push = np.zeros(2 * members)
    push[0], push[1] = near, far
    return chain_system(near, far, members)[0] @ push


def sweep_table(length, factor):
    half = 0.5 * factor
    ratio = np.zeros(length)
    last = 0.0
    for i in range(length):
        ratio[i] = last = half / (1.0 + factor - half * last)
    decay = np.cumprod(ratio)
    return np.stack([ratio, decay, decay])


def split(table, axis):
    rows = np.moveaxis(np.asarray(table, np.float64), axis, 0)
    high = np.zeros(rows.shape, BF16)
    carried = np.zeros(rows.shape[1:])
    for k, row in enumerate(rows):
        high[k] = (row + carried).astype(np.float32).astype(BF16)
        carried = carried + row - high[k].astype(np.float64)
    low = (rows - high.astype(np.float64)).astype(np.float32).astype(BF16)
    return np.moveaxis(high, 0, axis), np.moveaxis(low, 0, axis)


def parts(values):
    high = values.astype(BF16)
    return high, (values - high.astype(F32)).astype(BF16)


def dot(a, b):
    return jnp.dot(a, b, preferred_element_type=F32)


def exact_dot(a, b):
    return jnp.dot(a, b, precision=lax.Precision.HIGHEST, preferred_element_type=F32)


def upward_dot(values, table_ref):
    high, low = parts(values)
    count, depth = values.shape
    both = dot(jnp.concatenate([high, low], axis=0), table_ref[:depth])
    return both[:count] + both[count:] + dot(high, table_ref[depth:])


def north_dot(table_ref, values):
    north = values.shape[0]
    solved = dot(table_ref[...], jnp.concatenate(parts(values), axis=0))
    return solved[:north] + solved[north:]


def pick(column, me):
    value = float(column[0])
    for k in range(1, len(column)):
        value = jnp.where(me == k, float(column[k]), value)
    return value


def send_all(ends, table, me, out_refs):
    for d, out_ref in enumerate(out_refs):
        out_ref[...] = pick(table[:, 2 * d], me) * ends[0] + pick(table[:, 2 * d + 1], me) * ends[1]


def take_all(ends, table, me, messages):
    left = right = 0.0
    for d, message in enumerate(messages):
        left += pick(table[:, 8 + 2 * d], me) * message
        right += pick(table[:, 9 + 2 * d], me) * message
    known = (left, right) + tuple(ends)
    return [sum(pick(table[:, 4 * side + k], me) * known[k] for k in range(4)) for side in range(2)]


def diagonal(size):
    return lax.broadcasted_iota(jnp.int32, (size, size), 0) == lax.broadcasted_iota(jnp.int32, (size, size), 1)


def as_row(column):
    return jnp.sum(jnp.where(diagonal(column.shape[0]), column, 0.0), axis=0, keepdims=True)


def stacked(rows, height):
    filler = jnp.zeros((height - sum(row.shape[0] for row in rows), rows[0].shape[1]), F32)
    return jnp.concatenate(list(rows) + [filler], axis=0)


def ordered(pair, east):
    if not pair:
        return lambda i: i
    flip = lax.axis_index("gx")
    return lambda i: jnp.where(flip == 0, i, east - 1 - i)


def end_places(count, east):
    if count == 1:
        return [(east - 1, 0)]
    return [(0, 0), (east - 1, 1)]


def local_kernel(
    pair, group, factors, sending,
    tables_hbm, warmth_hbm, supply_hbm,
    swept_ref, warmth_ref, upward_ends_ref, north_ends_ref, east_ends_ref, *rest,
):
    to_up = sending.shape[1] // 2
    up_refs = rest[:to_up]
    supply_ref, both_ref, edges_ref, tables_ref, up_ref, north_ref, even_ref, odd_ref, sems = rest[to_up:]
    east, north, upward = supply_ref.shape
    groups = east // group
    count = east_ends_ref.shape[0]
    place = ordered(pair, east)

    def fetch(which, g):
        start = jnp.minimum(place(g * group), place(g * group + group - 1))
        block = pl.ds(start, group)
        if which == 0:
            return pltpu.make_async_copy(warmth_hbm.at[block], warmth_ref.at[pl.ds(start + 1, group)], sems.at[0, g])
        return pltpu.make_async_copy(supply_hbm.at[block], supply_ref.at[block], sems.at[1, g])

    tables = pltpu.make_async_copy(tables_hbm, tables_ref, sems.at[0, groups])
    tables.start()
    for g in range(groups):
        for which in range(2):
            fetch(which, g).start()
    warmth_ref[0] = jnp.zeros((north, upward), F32)
    warmth_ref[east + 1] = jnp.zeros((north, upward), F32)
    both_ref[...] = jnp.zeros_like(both_ref)
    east_ends_ref[...] = jnp.zeros_like(east_ends_ref)
    lane = lax.broadcasted_iota(jnp.int32, (1, 2 * east), 1)
    line = lax.broadcasted_iota(jnp.int32, (8, 1), 0)
    half_factor = 0.5 * factors[0]
    tables.wait()
    up_ref[...] = tables_ref[: 2 * upward].astype(BF16)
    north_ref[...] = tables_ref[2 * upward : 2 * upward + 2 * north, : 2 * north].astype(BF16)
    sweep = 2 * upward + 2 * north
    fetch(0, 0).wait()

    def arrive(g):
        fetch(1, g).wait()

        @pl.when(g + 1 < groups)
        def _():
            fetch(0, g + 1).wait()

    def shifted(values, step):
        turned = pltpu.roll(values, step % north, 0)
        if step > 0:
            return jnp.concatenate([jnp.where(line == 0, 0.0, turned[:8]), turned[8:]], axis=0)
        return jnp.concatenate([turned[:-8], jnp.where(line == 7, 0.0, turned[-8:])], axis=0)

    def upward_part(g, slot_ref):
        heat_list = []
        for k in range(group):
            i = g * group + k
            x = place(i)
            warm = warmth_ref[x + 1]
            bent = (warmth_ref[x] - warm) + (warmth_ref[x + 2] - warm)
            across = (shifted(warm, 1) - warm) + (shifted(warm, -1) - warm)
            heat_list.append((supply_ref[x] + 2.0 * warm) + (factors[0] * bent + factors[1] * across))
            edges_ref[pl.ds(i, 1)] = warm[:1]
            edges_ref[pl.ds(east + i, 1)] = warm[north - 1 :]
        slot_ref[...] = upward_dot(jnp.concatenate(heat_list, axis=0), up_ref)

    def north_part(g, slot_ref):
        for k in range(group):
            i = g * group + k
            first = slot_ref[k * north : (k + 1) * north]
            heads = pltpu.roll(first[:, : 2 * east], i, 1)
            tails = pltpu.roll(first[:, upward - 2 * east :], east + 1 + i, 1)
            both = jnp.where(lane == i, heads, both_ref[...])
            both_ref[...] = jnp.where(lane == east + i, tails, both)
            solved = north_dot(north_ref, first - 2.0 * warmth_ref[place(i) + 1])
            north_ends_ref[0, pl.ds(i, 1)] = half_factor * solved[:1]
            north_ends_ref[1, pl.ds(i, 1)] = half_factor * solved[north - 1 :]
            swept = solved + tables_ref[pl.ds(sweep + i, 1), :] * east_ends_ref[count - 1]
            swept_ref[i] = swept
            east_ends_ref[count - 1] = swept
            if not pair:
                east_ends_ref[0] += tables_ref[pl.ds(sweep + east + i, 1), :] * swept

    arrive(0)
    upward_part(0, even_ref)

    def body(j, _):
        g = 2 * j
        arrive(g + 1)
        upward_part(g + 1, odd_ref)
        north_part(g, even_ref)
        later = jnp.minimum(g + 2, groups - 1)

        @pl.when(g + 2 < groups)
        def _():
            arrive(g + 2)

        upward_part(later, even_ref)
        north_part(g + 1, odd_ref)
        return 0

    lax.fori_loop(0, groups // 2, body, 0)

    ends = end_places(count, east)
    planes = [warmth_ref[place(i) + 1] for i, _ in ends]
    solved_up = upward_dot(jnp.concatenate([edges_ref[...]] + planes, axis=0), up_ref)
    east_ends_ref[count - 1] = tables_ref[sweep + 2 * east : sweep + 2 * east + 1, :] * east_ends_ref[count - 1]
    height = north_ends_ref.shape[1]
    rows = [[], []]
    for p in range(count):
        solved = half_factor * north_dot(north_ref, solved_up[2 * east + p * north : 2 * east + (p + 1) * north])
        rows[0].append(solved[:1])
        rows[1].append(solved[north - 1 :])
        east_ends_ref[p] += 2.0 * solved
    for end in range(2):
        north_ends_ref[end, :east] += 2.0 * solved_up[end * east : (end + 1) * east]
        north_ends_ref[end, east:] = stacked(rows[end], height - east)

    half = north // 2
    top, bottom = both_ref[:half], both_ref[half:]
    folded = (
        jnp.where(lane < east, top, pltpu.roll(bottom, east, 1)),
        jnp.where(lane < east, pltpu.roll(top, east, 1), bottom),
    )
    upward_ends = []
    for end, column in enumerate((slice(0, 1), slice(upward - 1, upward))):
        extra = [as_row(solved_up[k * north : (k + 1) * north, column]) for k in range(1 + count)]
        upward_ends.append(stacked([folded[end]] + extra, upward_ends_ref.shape[1]))
        upward_ends_ref[end] = upward_ends[end]
    send_all(upward_ends, sending, lax.axis_index("gz"), up_refs)


def upward_kernel(
    count, taking, sending,
    ends_ref, north_ends_ref, east_ends_ref, north_inverse_ref, east_twice_ref, spikes_ref, spread_ref, *rest,
):
    taken = (taking.shape[1] - 8) // 2
    message_refs = rest[:taken]
    columns_ref, north_out_ref, east_out_ref, *out_refs = rest[taken:]
    north, lanes = columns_ref.shape
    east, half = lanes // 2, north // 2
    lane = lax.broadcasted_iota(jnp.int32, (1, lanes), 1)
    before, after = take_all(
        (ends_ref[0], ends_ref[1]), taking, lax.axis_index("gz"), [ref[...] for ref in message_refs]
    )

    def paired(end, rows):
        if end == 0:
            return jnp.where(lane < east, before[rows], pltpu.roll(after[rows], east, 1))
        return jnp.where(lane < east, pltpu.roll(before[rows], east, 1), after[rows])

    solved = exact_dot(north_inverse_ref[...], jnp.concatenate([paired(0, slice(0, half)), paired(1, slice(0, half))], axis=0))
    columns = exact_dot(solved, east_twice_ref[...])
    columns_ref[...] = columns
    planes = []
    for p in range(count):
        row = slice(half + 1 + p, half + 2 + p)
        planes.append([
            jnp.sum(north_inverse_ref[...] * side[row], axis=1, keepdims=True) for side in (before, after)
        ])
    height = north_ends_ref.shape[1]
    shape = (height, lanes)
    row = lax.broadcasted_iota(jnp.int32, shape, 0)
    short = lax.broadcasted_iota(jnp.int32, shape, 1) % east
    own = (row < east) & (short == row)
    behind = (row >= east) & (row < east + count) & (short == row - east)
    picked = []
    for end, y in enumerate((0, north - 1)):
        first = solved[y : y + 1] + 2.0 * paired(end, slice(half, half + 1))
        second = jnp.zeros((1, lanes), F32)
        for _, k in end_places(count, east):
            for side in range(2):
                second = jnp.where(lane == side * east + k, planes[k][side][y : y + 1], second)
        picked.append(jnp.where(own, first, 0.0) + jnp.where(behind, second, 0.0))
    added = exact_dot(jnp.concatenate(picked, axis=0), spread_ref[...])
    ends = []
    for end in range(2):
        ends.append(north_ends_ref[end] + added[end * height : (end + 1) * height])
        north_out_ref[end] = ends[end]
    send_all(ends, sending, lax.axis_index("gy"), out_refs)
    for i, k in end_places(count, east):
        total = east_ends_ref[k]
        for side in range(2):
            column = columns[:, side * east + i : side * east + i + 1] + 2.0 * planes[k][side]
            total += column * spikes_ref[side : side + 1, :]
        east_out_ref[k] = total


def north_kernel(
    count, taking,
    ends_ref, east_ends_ref, east_inverse_ref, spikes_ref, *rest,
):
    taken = (taking.shape[1] - 8) // 2
    message_refs = rest[:taken]
    rows_ref, east_out_ref = rest[taken:]
    east = rows_ref.shape[1]
    sides = take_all((ends_ref[0], ends_ref[1]), taking, lax.axis_index("gy"), [ref[...] for ref in message_refs])
    swept = [exact_dot(east_inverse_ref[...], side[:east]) for side in sides]
    for n in range(2):
        rows_ref[n] = swept[n]
    for i, k in end_places(count, east):
        total = east_ends_ref[k]
        for n in range(2):
            total += spikes_ref[n] * (swept[n][i : i + 1] + 2.0 * sides[n][east + k : east + k + 1])
        east_out_ref[k] = total


def final_kernel(
    pair, table, tile,
    sweep_ref, own_ref, other_ref,
    swept_ref, warmth_ref, columns_ref, rows_ref, upward_spikes_ref, north_spikes_ref,
    out_hbm,
    out_ref, sides_ref, sems,
):
    east, north, upward = out_ref.shape
    place = ordered(pair, east)

    if pair:
        sides_ref[0] = float(table[0]) * other_ref[0] + float(table[1]) * own_ref[0]
    else:
        me = lax.axis_index("gx")
        for side in range(2):
            plane = 0.0
            for m in range(table.shape[0]):
                for end in range(2):
                    plane += pick(table[:, side, 2 * m + end], me) * other_ref[m, end]
            sides_ref[side] = plane
    last = sides_ref.shape[0] - 1

    def send(t):
        block = pl.ds(pl.multiple_of(t * tile, tile), tile)
        return pltpu.make_async_copy(out_ref.at[:, block], out_hbm.at[:, block], sems.at[t])

    def body(t, _):
        block = pl.ds(pl.multiple_of(t * tile, tile), tile)
        value = sides_ref[last, block]
        columns = columns_ref[block]
        first_spike, last_spike = north_spikes_ref[0, block], north_spikes_ref[1, block]
        for i in reversed(range(east)):
            value = sweep_ref[0, i] * (swept_ref[i, block] + value)
            if not pair:
                value += sweep_ref[2, i] * sides_ref[0, block]
            added = (
                columns[:, i : i + 1] * upward_spikes_ref[0:1, :]
                + columns[:, east + i : east + i + 1] * upward_spikes_ref[1:2, :]
            )
            added += first_spike * rows_ref[0, i : i + 1, :] + last_spike * rows_ref[1, i : i + 1, :]
            x = place(i)
            out_ref[x, block] = warmth_ref[x + 1, block] + value + added
        send(t).start()
        return 0

    lax.fori_loop(0, north // tile, body, 0)
    for t in range(north // tile):
        send(t).wait()


def spread_out(messages, axis):
    members = lax.axis_size(axis)
    taken = [
        lax.ppermute(messages[d], axis, [(k, peers(k, members, d + 1)[0]) for k in range(members)])
        for d in reversed(range(len(messages)))
    ]
    return taken[::-1]


def local(initial_warmth, heat_supply):
    shape = east, north, upward = initial_warmth.shape
    members = [lax.axis_size(axis) for axis in ("gx", "gy", "gz")]
    factors = [float((n * m) ** 2 // 4) for n, m in zip(shape, members)]
    lines = [line_tables(n, factor) for n, factor in zip(shape, factors)]
    sweep = sweep_table(east, factors[0])
    ratio, weights = sweep[:2]
    sweep = sweep.astype(np.float32)
    exchanges = [exchange_tables(line[1], line[2], m) for line, m in zip(lines, members)]
    upward_high, upward_low = split(lines[2][0], 0)
    north_high, north_low = split(lines[1][0] / (0.5 * factors[0]), 1)
    north_stack = np.block([[north_high, north_high], [north_low, np.zeros_like(north_low)]])
    tables = np.concatenate([
        np.concatenate([upward_high, upward_low]).astype(np.float32),
        np.pad(north_stack.astype(np.float32), ((0, 0), (0, max(upward - 2 * north, 0)))),
        np.repeat(np.concatenate([[0.0], ratio[:-1], weights, ratio[-1:], np.zeros(7)])[:, None], upward, axis=1).astype(np.float32),
    ])
    east_inverse = lines[0][0].astype(np.float32)
    north_inverse = lines[1][0].astype(np.float32)
    east_twice = np.kron(np.eye(2), lines[0][0]).astype(np.float32)
    upward_spikes = np.stack(lines[2][1:]).astype(np.float32)
    spread = np.repeat(upward_spikes, east, axis=0)
    north_spikes = np.broadcast_to(np.stack(lines[1][1:])[:, :, None], (2, north, upward)).astype(np.float32)

    pair = members[0] == 2
    count = 1 if pair else 2
    height = east + 8
    to_up, to_north = members[2] - 1, members[1] - 1
    vmem = pl.BlockSpec(memory_space=pltpu.VMEM)
    smem = pl.BlockSpec(memory_space=pltpu.SMEM)
    hbm = pl.BlockSpec(memory_space=pltpu.HBM)

    def kept(*sizes):
        return jax.ShapeDtypeStruct(sizes, F32)

    group = 4
    folded = kept(north // 2 + 8, 2 * east)
    swept, warmth, upward_ends, north_ends, east_ends, *messages = pl.pallas_call(
        functools.partial(local_kernel, pair, group, factors, exchanges[2][0]),
        in_specs=[hbm] * 3,
        out_specs=[vmem] * (5 + to_up),
        out_shape=[
            pltpu.VMEM(shape, F32),
            pltpu.VMEM((east + 2, north, upward), F32),
            kept(2, *folded.shape),
            kept(2, height, upward),
            kept(count, north, upward),
        ]
        + [folded] * to_up,
        scratch_shapes=[
            pltpu.VMEM(shape, F32),
            pltpu.VMEM((north, 2 * east), F32),
            pltpu.VMEM((2 * east, upward), F32),
            pltpu.VMEM(tables.shape, F32),
            pltpu.VMEM((2 * upward, upward), BF16),
            pltpu.VMEM((2 * north, 2 * north), BF16),
            pltpu.VMEM((group * north, upward), F32),
            pltpu.VMEM((group * north, upward), F32),
            pltpu.SemaphoreType.DMA((2, east // group + 1)),
        ],
        compiler_params=pltpu.CompilerParams(vmem_limit_bytes=32 * MIB),
    )(pltpu.with_memory_space_constraint(jnp.asarray(tables), pltpu.HBM), initial_warmth, heat_supply)

    messages = spread_out(messages, "gz")
    columns, north_ends, east_ends, *messages = pl.pallas_call(
        functools.partial(upward_kernel, count, exchanges[2][1], exchanges[1][0]),
        in_specs=[vmem] * (7 + to_up),
        out_specs=[vmem] * (3 + to_north),
        out_shape=[kept(north, 2 * east), kept(2, height, upward), kept(count, north, upward)]
        + [kept(height, upward)] * to_north,
        compiler_params=pltpu.CompilerParams(vmem_limit_bytes=6 * MIB),
    )(upward_ends, north_ends, east_ends, north_inverse, east_twice, upward_spikes, spread, *messages)

    messages = spread_out(messages, "gy")
    rows, own = pl.pallas_call(
        functools.partial(north_kernel, count, exchanges[1][1]),
        in_specs=[vmem] * (4 + to_north),
        out_specs=[vmem] * 2,
        out_shape=[kept(2, east, upward), kept(count, north, upward)],
        compiler_params=pltpu.CompilerParams(vmem_limit_bytes=6 * MIB),
    )(north_ends, east_ends, east_inverse, north_spikes, *messages)

    if pair:
        other = lax.ppermute(own, "gx", [(0, 1), (1, 0)])
        near = lines[0][1][0]
        table = np.array([1.0, near]) / (1.0 - near**2)
    else:
        other = lax.all_gather(own, "gx")
        table = interface_table(lines[0][1], lines[0][2], members[0])
    swept = pltpu.with_memory_space_constraint(swept, pltpu.VMEM)
    warmth = pltpu.with_memory_space_constraint(warmth, pltpu.VMEM)
    tile = 32
    return pl.pallas_call(
        functools.partial(final_kernel, pair, table, tile),
        in_specs=[smem] + [vmem] * 8,
        out_specs=hbm,
        out_shape=kept(*shape),
        scratch_shapes=[
            pltpu.VMEM(shape, F32),
            pltpu.VMEM((count, north, upward), F32),
            pltpu.SemaphoreType.DMA((north // tile,)),
        ],
        compiler_params=pltpu.CompilerParams(vmem_limit_bytes=16 * MIB),
    )(sweep, own, other, swept, warmth, columns, rows, upward_spikes, north_spikes)


def solution(mesh):
    return jax.shard_map(
        local,
        mesh=mesh,
        in_specs=(P("gx", "gy", "gz"), P("gx", "gy", "gz")),
        out_specs=P("gx", "gy", "gz"),
        check_vma=False,
    )
```

```python
import functools

import jax
import jax.numpy as jnp
import numpy as np
from jax import lax
from jax.experimental import pallas as pl
from jax.experimental.pallas import tpu as pltpu
from jax.sharding import PartitionSpec as P

F32 = jnp.float32
BF16 = jnp.bfloat16
MIB = 1 << 20


def line_tables(length, factor):
    matrix = (1.0 + factor) * np.eye(length)
    matrix -= 0.5 * factor * (np.eye(length, k=1) + np.eye(length, k=-1))
    inverse = np.linalg.inv(matrix)
    inverse = 0.5 * (inverse + inverse.T)
    return inverse, 0.5 * factor * inverse[:, 0], 0.5 * factor * inverse[:, -1]


def chain_system(near, far, members):
    system = np.eye(2 * members)
    for m in range(members):
        if m > 0:
            system[2 * m, 2 * m - 1] -= near
            system[2 * m + 1, 2 * m - 1] -= far
        if m < members - 1:
            system[2 * m, 2 * m + 2] -= far
            system[2 * m + 1, 2 * m + 2] -= near
    return np.linalg.inv(system)


def interface_table(before, after, members):
    solved = chain_system(before[0], before[-1], members)
    rows = np.zeros((members, 2, 2 * members))
    for m in range(members):
        if m > 0:
            rows[m, 0] = solved[2 * m - 1]
        if m < members - 1:
            rows[m, 1] = solved[2 * m + 2]
    return rows


def peers(member, members, distance):
    if members & (members - 1) == 0:
        return member ^ distance, member ^ distance
    return (member + distance) % members, (member - distance) % members


def exchange_tables(before, after, members):
    near, far = before[0], before[-1]
    sending = np.zeros((members, 2 * (members - 1)))
    taking = np.zeros((members, 8 + 2 * (members - 1)))
    for m in range(members):
        right = chain_system(near, far, members - 1 - m)
        left = chain_system(near, far, m)
        for d in range(1, members):
            k = peers(m, members, d)[1]
            if k > m:
                sending[k, 2 * d - 2 : 2 * d] = right[0, 2 * (k - m - 1) : 2 * (k - m)]
                taking[m, 8 + 2 * d - 1] = 1.0
            else:
                sending[k, 2 * d - 2 : 2 * d] = left[-1, 2 * k : 2 * k + 2]
                taking[m, 8 + 2 * d - 2] = 1.0
        pull_left = answer(near, far, m)
        pull_right = answer(near, far, members - 1 - m)
        system = np.array([
            [1.0, 0.0, -pull_left, 0.0],
            [0.0, 1.0, 0.0, -pull_right],
            [-near, -far, 1.0, 0.0],
            [-far, -near, 0.0, 1.0],
        ])
        taking[m, :8] = np.linalg.inv(system)[:2].reshape(8)
    return sending, taking


def answer(near, far, members):
    if members == 0:
        return 0.0
    push = np.zeros(2 * members)
    push[0], push[1] = near, far
    return chain_system(near, far, members)[0] @ push


def sweep_table(length, factor):
    half = 0.5 * factor
    ratio = np.zeros(length)
    last = 0.0
    for i in range(length):
        ratio[i] = last = half / (1.0 + factor - half * last)
    decay = np.cumprod(ratio)
    return np.stack([ratio, decay, decay])


def split(table, axis):
    rows = np.moveaxis(np.asarray(table, np.float64), axis, 0)
    high = np.zeros(rows.shape, BF16)
    carried = np.zeros(rows.shape[1:])
    for k, row in enumerate(rows):
        high[k] = (row + carried).astype(np.float32).astype(BF16)
        carried = carried + row - high[k].astype(np.float64)
    low = (rows - high.astype(np.float64)).astype(np.float32).astype(BF16)
    return np.moveaxis(high, 0, axis), np.moveaxis(low, 0, axis)


def parts(values):
    high = values.astype(BF16)
    return high, (values - high.astype(F32)).astype(BF16)


def dot(a, b):
    return jnp.dot(a, b, preferred_element_type=F32)


def exact_dot(a, b):
    return jnp.dot(a, b, precision=lax.Precision.HIGHEST, preferred_element_type=F32)


def upward_dot(values, table_ref):
    high, low = parts(values)
    count, depth = values.shape
    both = dot(jnp.concatenate([high, low], axis=0), table_ref[:depth])
    return both[:count] + both[count:] + dot(high, table_ref[depth:])


def north_dot(table_ref, values):
    north = values.shape[0]
    solved = dot(table_ref[...], jnp.concatenate(parts(values), axis=0))
    return solved[:north] + solved[north:]


def pick(column, me):
    value = float(column[0])
    for k in range(1, len(column)):
        value = jnp.where(me == k, float(column[k]), value)
    return value


def send_all(ends, table, me, out_refs):
    for d, out_ref in enumerate(out_refs):
        out_ref[...] = pick(table[:, 2 * d], me) * ends[0] + pick(table[:, 2 * d + 1], me) * ends[1]


def take_all(ends, table, me, messages):
    left = right = 0.0
    for d, message in enumerate(messages):
        left += pick(table[:, 8 + 2 * d], me) * message
        right += pick(table[:, 9 + 2 * d], me) * message
    known = (left, right) + tuple(ends)
    return [sum(pick(table[:, 4 * side + k], me) * known[k] for k in range(4)) for side in range(2)]


def diagonal(size):
    return lax.broadcasted_iota(jnp.int32, (size, size), 0) == lax.broadcasted_iota(jnp.int32, (size, size), 1)


def as_row(column):
    return jnp.sum(jnp.where(diagonal(column.shape[0]), column, 0.0), axis=0, keepdims=True)


def as_column(row):
    return jnp.sum(jnp.where(diagonal(row.shape[1]), row, 0.0), axis=1, keepdims=True)


def stacked(rows, height):
    filler = jnp.zeros((height - sum(row.shape[0] for row in rows), rows[0].shape[1]), F32)
    return jnp.concatenate(list(rows) + [filler], axis=0)


def ordered(pair, east):
    if not pair:
        return lambda i: i
    flip = lax.axis_index("gx")
    return lambda i: jnp.where(flip == 0, i, east - 1 - i)


def end_places(count, east):
    if count == 1:
        return [(east - 1, 0)]
    return [(0, 0), (east - 1, 1)]


def local_kernel(
    pair, group, factors, sending,
    tables_hbm, warmth_hbm, supply_hbm,
    swept_ref, warmth_ref, upward_ends_ref, north_ends_ref, east_ends_ref, *rest,
):
    to_up = sending.shape[1] // 2
    up_refs = rest[:to_up]
    supply_ref, both_ref, edges_ref, tables_ref, up_ref, north_ref, even_ref, odd_ref, sems = rest[to_up:]
    east, north, upward = supply_ref.shape
    groups = east // group
    count = east_ends_ref.shape[0]
    place = ordered(pair, east)

    def fetch(which, g):
        start = jnp.minimum(place(g * group), place(g * group + group - 1))
        block = pl.ds(start, group)
        if which == 0:
            return pltpu.make_async_copy(warmth_hbm.at[block], warmth_ref.at[pl.ds(start + 1, group)], sems.at[0, g])
        return pltpu.make_async_copy(supply_hbm.at[block], supply_ref.at[block], sems.at[1, g])

    tables = pltpu.make_async_copy(tables_hbm, tables_ref, sems.at[0, groups])
    tables.start()
    for g in range(groups):
        for which in range(2):
            fetch(which, g).start()
    warmth_ref[0] = jnp.zeros((north, upward), F32)
    warmth_ref[east + 1] = jnp.zeros((north, upward), F32)
    both_ref[...] = jnp.zeros_like(both_ref)
    east_ends_ref[...] = jnp.zeros_like(east_ends_ref)
    lane = lax.broadcasted_iota(jnp.int32, (1, 2 * east), 1)
    line = lax.broadcasted_iota(jnp.int32, (8, 1), 0)
    half_factor = 0.5 * factors[0]
    tables.wait()
    up_ref[...] = tables_ref[: 2 * upward].astype(BF16)
    north_ref[...] = tables_ref[2 * upward : 2 * upward + 2 * north, : 2 * north].astype(BF16)
    sweep = 2 * upward + 2 * north
    fetch(0, 0).wait()

    def arrive(g):
        fetch(1, g).wait()

        @pl.when(g + 1 < groups)
        def _():
            fetch(0, g + 1).wait()

    def shifted(values, step):
        turned = pltpu.roll(values, step % north, 0)
        if step > 0:
            return jnp.concatenate([jnp.where(line == 0, 0.0, turned[:8]), turned[8:]], axis=0)
        return jnp.concatenate([turned[:-8], jnp.where(line == 7, 0.0, turned[-8:])], axis=0)

    def upward_part(g, slot_ref):
        heat_list = []
        for k in range(group):
            i = g * group + k
            x = place(i)
            warm = warmth_ref[x + 1]
            bent = (warmth_ref[x] - warm) + (warmth_ref[x + 2] - warm)
            across = (shifted(warm, 1) - warm) + (shifted(warm, -1) - warm)
            heat_list.append((supply_ref[x] + 2.0 * warm) + (factors[0] * bent + factors[1] * across))
            edges_ref[pl.ds(i, 1)] = warm[:1]
            edges_ref[pl.ds(east + i, 1)] = warm[north - 1 :]
        slot_ref[...] = upward_dot(jnp.concatenate(heat_list, axis=0), up_ref)

    def north_part(g, slot_ref):
        for k in range(group):
            i = g * group + k
            first = slot_ref[k * north : (k + 1) * north]
            both = jnp.where(lane < east, first[:, : 2 * east], first[:, upward - 2 * east :])
            both = pltpu.roll(both, i, 1)
            both_ref[0] = jnp.where(lane == i, both, both_ref[0])
            both_ref[1] = jnp.where(lane == lax.rem(i + 2 * east - 1, 2 * east), both, both_ref[1])
            solved = north_dot(north_ref, first - 2.0 * warmth_ref[place(i) + 1])
            north_ends_ref[0, pl.ds(i, 1)] = half_factor * solved[:1]
            north_ends_ref[1, pl.ds(i, 1)] = half_factor * solved[north - 1 :]
            swept = solved + tables_ref[pl.ds(sweep + i, 1), :] * east_ends_ref[count - 1]
            swept_ref[i] = swept
            east_ends_ref[count - 1] = swept
            if not pair:
                east_ends_ref[0] += tables_ref[pl.ds(sweep + east + i, 1), :] * swept

    arrive(0)
    upward_part(0, even_ref)

    def body(j, _):
        g = 2 * j
        arrive(g + 1)
        upward_part(g + 1, odd_ref)
        north_part(g, even_ref)
        later = jnp.minimum(g + 2, groups - 1)

        @pl.when(g + 2 < groups)
        def _():
            arrive(g + 2)

        upward_part(later, even_ref)
        north_part(g + 1, odd_ref)
        return 0

    lax.fori_loop(0, groups // 2, body, 0)

    ends = end_places(count, east)
    planes = [warmth_ref[place(i) + 1] for i, _ in ends]
    solved_up = upward_dot(jnp.concatenate([edges_ref[...]] + planes, axis=0), up_ref)
    east_ends_ref[count - 1] = tables_ref[sweep + 2 * east : sweep + 2 * east + 1, :] * east_ends_ref[count - 1]
    height = north_ends_ref.shape[1]
    rows = [[], []]
    for p in range(count):
        solved = half_factor * north_dot(north_ref, solved_up[2 * east + p * north : 2 * east + (p + 1) * north])
        rows[0].append(solved[:1])
        rows[1].append(solved[north - 1 :])
        east_ends_ref[p] += 2.0 * solved
    for end in range(2):
        north_ends_ref[end, :east] += 2.0 * solved_up[end * east : (end + 1) * east]
        north_ends_ref[end, east:] = stacked(rows[end], height - east)

    half = north // 2
    folded = []
    for end in range(2):
        top, bottom = both_ref[end, :half], both_ref[end, half:]
        top, bottom = pltpu.roll(top, end, 1), pltpu.roll(bottom, east + end, 1)
        folded.append(jnp.where(lane < east, top, bottom))
    upward_ends = []
    for end, column in enumerate((slice(0, 1), slice(upward - 1, upward))):
        extra = [as_row(solved_up[k * north : (k + 1) * north, column]) for k in range(1 + count)]
        upward_ends.append(stacked([folded[end]] + extra, upward_ends_ref.shape[1]))
        upward_ends_ref[end] = upward_ends[end]
    send_all(upward_ends, sending, lax.axis_index("gz"), up_refs)


def upward_kernel(
    count, taking, sending,
    ends_ref, north_ends_ref, north_inverse_ref, east_twice_ref, spread_ref, *rest,
):
    taken = (taking.shape[1] - 8) // 2
    message_refs = rest[:taken]
    columns_ref, north_out_ref, plane_ref, *out_refs = rest[taken:]
    north, lanes = columns_ref.shape
    east, half = lanes // 2, north // 2
    lane = lax.broadcasted_iota(jnp.int32, (1, lanes), 1)
    before, after = take_all(
        (ends_ref[0], ends_ref[1]), taking, lax.axis_index("gz"), [ref[...] for ref in message_refs]
    )

    def paired(end, rows):
        if end == 0:
            return jnp.where(lane < east, before[rows], pltpu.roll(after[rows], east, 1))
        return jnp.where(lane < east, pltpu.roll(before[rows], east, 1), after[rows])

    solved = exact_dot(north_inverse_ref[...], jnp.concatenate([paired(0, slice(0, half)), paired(1, slice(0, half))], axis=0))
    columns = exact_dot(solved, east_twice_ref[...])
    columns_ref[...] = columns
    planes = []
    for p in range(count):
        row = slice(half + 1 + p, half + 2 + p)
        planes.append([
            jnp.sum(north_inverse_ref[...] * side[row], axis=1, keepdims=True) for side in (before, after)
        ])
    height = north_ends_ref.shape[1]
    shape = (height, lanes)
    row = lax.broadcasted_iota(jnp.int32, shape, 0)
    short = lax.broadcasted_iota(jnp.int32, shape, 1) % east
    own = (row < east) & (short == row)
    behind = (row >= east) & (row < east + count) & (short == row - east)
    picked = []
    for end, y in enumerate((0, north - 1)):
        first = solved[y : y + 1] + 2.0 * paired(end, slice(half, half + 1))
        second = jnp.zeros((1, lanes), F32)
        for _, k in end_places(count, east):
            for side in range(2):
                second = jnp.where(lane == side * east + k, planes[k][side][y : y + 1], second)
        picked.append(jnp.where(own, first, 0.0) + jnp.where(behind, second, 0.0))
    added = exact_dot(jnp.concatenate(picked, axis=0), spread_ref[...])
    ends = []
    for end in range(2):
        ends.append(north_ends_ref[end] + added[end * height : (end + 1) * height])
        north_out_ref[end] = ends[end]
    send_all(ends, sending, lax.axis_index("gy"), out_refs)
    for i, k in end_places(count, east):
        rows = []
        for side in range(2):
            rows.append(as_row(columns[:, side * east + i : side * east + i + 1] + 2.0 * planes[k][side]))
        plane_ref[k] = stacked(rows, 8)


def north_kernel(
    count, taking,
    ends_ref, plane_ref, east_inverse_ref, *rest,
):
    taken = (taking.shape[1] - 8) // 2
    message_refs = rest[:taken]
    rows_ref, small_ref = rest[taken:]
    _, east, upward = rows_ref.shape
    sides = take_all((ends_ref[0], ends_ref[1]), taking, lax.axis_index("gy"), [ref[...] for ref in message_refs])
    swept = [exact_dot(east_inverse_ref[...], side[:east]) for side in sides]
    for n in range(2):
        rows_ref[n] = swept[n]
    for i, k in end_places(count, east):
        rows = [swept[n][i : i + 1] + 2.0 * sides[n][east + k : east + k + 1] for n in range(2)]
        wide = jnp.concatenate([plane_ref[k], jnp.zeros((8, upward - plane_ref.shape[2]), F32)], axis=1)
        small_ref[k] = stacked(rows + [wide[:2]], 8)


def final_kernel(
    pair, table, tile,
    sweep_ref, own_ref, other_ref, own_small_ref, other_small_ref,
    swept_ref, warmth_ref, columns_ref, rows_ref, upward_spikes_ref, north_spikes_ref,
    out_hbm,
    out_ref, sides_ref, sems,
):
    east, north, upward = out_ref.shape
    place = ordered(pair, east)

    def widened(plane, small):
        for side in range(2):
            plane += north_spikes_ref[side] * small[side : side + 1]
            plane += as_column(small[2 + side : 3 + side, :north]) * upward_spikes_ref[side : side + 1, :]
        return plane

    if pair:
        near, far = float(table[0]), float(table[1])
        sides_ref[0] = widened(
            near * other_ref[0] + far * own_ref[0], near * other_small_ref[0] + far * own_small_ref[0]
        )
    else:
        me = lax.axis_index("gx")
        members = table.shape[0]
        for side in range(2):
            plane, small = 0.0, 0.0
            for m in range(members):
                for end in range(2):
                    weight = pick(table[:, side, 2 * m + end], me)
                    plane += weight * other_ref[m, end]
                    small += weight * other_small_ref[m, end]
            sides_ref[side] = widened(plane, small)
    last = sides_ref.shape[0] - 1

    def send(t):
        block = pl.ds(pl.multiple_of(t * tile, tile), tile)
        return pltpu.make_async_copy(out_ref.at[:, block], out_hbm.at[:, block], sems.at[t])

    def body(t, _):
        block = pl.ds(pl.multiple_of(t * tile, tile), tile)
        value = sides_ref[last, block]
        columns = columns_ref[block]
        first_spike, last_spike = north_spikes_ref[0, block], north_spikes_ref[1, block]
        for i in reversed(range(east)):
            value = sweep_ref[0, i] * (swept_ref[i, block] + value)
            if not pair:
                value += sweep_ref[2, i] * sides_ref[0, block]
            added = (
                columns[:, i : i + 1] * upward_spikes_ref[0:1, :]
                + columns[:, east + i : east + i + 1] * upward_spikes_ref[1:2, :]
            )
            added += first_spike * rows_ref[0, i : i + 1, :] + last_spike * rows_ref[1, i : i + 1, :]
            x = place(i)
            out_ref[x, block] = warmth_ref[x + 1, block] + value + added
        send(t).start()
        return 0

    lax.fori_loop(0, north // tile, body, 0)
    for t in range(north // tile):
        send(t).wait()


def spread_out(messages, axis):
    members = lax.axis_size(axis)
    taken = [
        lax.ppermute(messages[d], axis, [(k, peers(k, members, d + 1)[0]) for k in range(members)])
        for d in reversed(range(len(messages)))
    ]
    return taken[::-1]


def local(initial_warmth, heat_supply):
    shape = east, north, upward = initial_warmth.shape
    members = [lax.axis_size(axis) for axis in ("gx", "gy", "gz")]
    factors = [float((n * m) ** 2 // 4) for n, m in zip(shape, members)]
    lines = [line_tables(n, factor) for n, factor in zip(shape, factors)]
    sweep = sweep_table(east, factors[0])
    ratio, weights = sweep[:2]
    sweep = sweep.astype(np.float32)
    exchanges = [exchange_tables(line[1], line[2], m) for line, m in zip(lines, members)]
    upward_high, upward_low = split(lines[2][0], 0)
    north_high, north_low = split(lines[1][0] / (0.5 * factors[0]), 1)
    north_stack = np.block([[north_high, north_high], [north_low, np.zeros_like(north_low)]])
    tables = np.concatenate([
        np.concatenate([upward_high, upward_low]).astype(np.float32),
        np.pad(north_stack.astype(np.float32), ((0, 0), (0, max(upward - 2 * north, 0)))),
        np.repeat(np.concatenate([[0.0], ratio[:-1], weights, ratio[-1:], np.zeros(7)])[:, None], upward, axis=1).astype(np.float32),
    ])
    east_inverse = lines[0][0].astype(np.float32)
    north_inverse = lines[1][0].astype(np.float32)
    east_twice = np.kron(np.eye(2), lines[0][0]).astype(np.float32)
    upward_spikes = np.stack(lines[2][1:]).astype(np.float32)
    spread = np.repeat(upward_spikes, east, axis=0)
    north_spikes = np.broadcast_to(np.stack(lines[1][1:])[:, :, None], (2, north, upward)).astype(np.float32)

    pair = members[0] == 2
    count = 1 if pair else 2
    height = east + 8
    to_up, to_north = members[2] - 1, members[1] - 1
    vmem = pl.BlockSpec(memory_space=pltpu.VMEM)
    smem = pl.BlockSpec(memory_space=pltpu.SMEM)
    hbm = pl.BlockSpec(memory_space=pltpu.HBM)

    def kept(*sizes):
        return jax.ShapeDtypeStruct(sizes, F32)

    group = 4
    folded = kept(north // 2 + 8, 2 * east)
    swept, warmth, upward_ends, north_ends, own, *messages = pl.pallas_call(
        functools.partial(local_kernel, pair, group, factors, exchanges[2][0]),
        in_specs=[hbm] * 3,
        out_specs=[vmem] * (5 + to_up),
        out_shape=[
            pltpu.VMEM(shape, F32),
            pltpu.VMEM((east + 2, north, upward), F32),
            kept(2, *folded.shape),
            kept(2, height, upward),
            kept(count, north, upward),
        ]
        + [folded] * to_up,
        scratch_shapes=[
            pltpu.VMEM(shape, F32),
            pltpu.VMEM((2, north, 2 * east), F32),
            pltpu.VMEM((2 * east, upward), F32),
            pltpu.VMEM(tables.shape, F32),
            pltpu.VMEM((2 * upward, upward), BF16),
            pltpu.VMEM((2 * north, 2 * north), BF16),
            pltpu.VMEM((group * north, upward), F32),
            pltpu.VMEM((group * north, upward), F32),
            pltpu.SemaphoreType.DMA((2, east // group + 1)),
        ],
        compiler_params=pltpu.CompilerParams(vmem_limit_bytes=32 * MIB),
    )(pltpu.with_memory_space_constraint(jnp.asarray(tables), pltpu.HBM), initial_warmth, heat_supply)

    messages = spread_out(messages, "gz")
    if pair:
        other = lax.ppermute(own, "gx", [(0, 1), (1, 0)])
    else:
        other = lax.all_gather(own, "gx")
    columns, north_ends, planes, *messages = pl.pallas_call(
        functools.partial(upward_kernel, count, exchanges[2][1], exchanges[1][0]),
        in_specs=[vmem] * (5 + to_up),
        out_specs=[vmem] * (3 + to_north),
        out_shape=[kept(north, 2 * east), kept(2, height, upward), kept(count, 8, north)]
        + [kept(height, upward)] * to_north,
        compiler_params=pltpu.CompilerParams(vmem_limit_bytes=6 * MIB),
    )(upward_ends, north_ends, north_inverse, east_twice, spread, *messages)

    messages = spread_out(messages, "gy")
    rows, own_small = pl.pallas_call(
        functools.partial(north_kernel, count, exchanges[1][1]),
        in_specs=[vmem] * (3 + to_north),
        out_specs=[vmem] * 2,
        out_shape=[kept(2, east, upward), kept(count, 8, upward)],
        compiler_params=pltpu.CompilerParams(vmem_limit_bytes=6 * MIB),
    )(north_ends, planes, east_inverse, *messages)

    if pair:
        other_small = lax.ppermute(own_small, "gx", [(0, 1), (1, 0)])
        near = lines[0][1][0]
        table = np.array([1.0, near]) / (1.0 - near**2)
    else:
        other_small = lax.all_gather(own_small, "gx")
        table = interface_table(lines[0][1], lines[0][2], members[0])
    swept = pltpu.with_memory_space_constraint(swept, pltpu.VMEM)
    warmth = pltpu.with_memory_space_constraint(warmth, pltpu.VMEM)
    tile = 32
    return pl.pallas_call(
        functools.partial(final_kernel, pair, table, tile),
        in_specs=[smem] + [vmem] * 10,
        out_specs=hbm,
        out_shape=kept(*shape),
        scratch_shapes=[
            pltpu.VMEM(shape, F32),
            pltpu.VMEM((count, north, upward), F32),
            pltpu.SemaphoreType.DMA((north // tile,)),
        ],
        compiler_params=pltpu.CompilerParams(vmem_limit_bytes=16 * MIB),
    )(sweep, own, other, own_small, other_small, swept, warmth, columns, rows, upward_spikes, north_spikes)


def solution(mesh):
    return jax.shard_map(
        local,
        mesh=mesh,
        in_specs=(P("gx", "gy", "gz"), P("gx", "gy", "gz")),
        out_specs=P("gx", "gy", "gz"),
        check_vma=False,
    )
```

```python
import functools

import jax
import jax.numpy as jnp
import numpy as np
from jax import lax
from jax.experimental import pallas as pl
from jax.experimental.pallas import tpu as pltpu
from jax.sharding import PartitionSpec as P

F32 = jnp.float32
BF16 = jnp.bfloat16
MIB = 1 << 20


def line_tables(length, factor):
    matrix = (1.0 + factor) * np.eye(length)
    matrix -= 0.5 * factor * (np.eye(length, k=1) + np.eye(length, k=-1))
    inverse = np.linalg.inv(matrix)
    inverse = 0.5 * (inverse + inverse.T)
    return inverse, 0.5 * factor * inverse[:, 0], 0.5 * factor * inverse[:, -1]


def chain_system(near, far, members):
    system = np.eye(2 * members)
    for m in range(members):
        if m > 0:
            system[2 * m, 2 * m - 1] -= near
            system[2 * m + 1, 2 * m - 1] -= far
        if m < members - 1:
            system[2 * m, 2 * m + 2] -= far
            system[2 * m + 1, 2 * m + 2] -= near
    return np.linalg.inv(system)


def interface_table(before, after, members):
    solved = chain_system(before[0], before[-1], members)
    rows = np.zeros((members, 2, 2 * members))
    for m in range(members):
        if m > 0:
            rows[m, 0] = solved[2 * m - 1]
        if m < members - 1:
            rows[m, 1] = solved[2 * m + 2]
    return rows


def peers(member, members, distance):
    if members & (members - 1) == 0:
        return member ^ distance, member ^ distance
    return (member + distance) % members, (member - distance) % members


def exchange_tables(before, after, members):
    near, far = before[0], before[-1]
    sending = np.zeros((members, 2 * (members - 1)))
    taking = np.zeros((members, 8 + 2 * (members - 1)))
    for m in range(members):
        right = chain_system(near, far, members - 1 - m)
        left = chain_system(near, far, m)
        for d in range(1, members):
            k = peers(m, members, d)[1]
            if k > m:
                sending[k, 2 * d - 2 : 2 * d] = right[0, 2 * (k - m - 1) : 2 * (k - m)]
                taking[m, 8 + 2 * d - 1] = 1.0
            else:
                sending[k, 2 * d - 2 : 2 * d] = left[-1, 2 * k : 2 * k + 2]
                taking[m, 8 + 2 * d - 2] = 1.0
        pull_left = answer(near, far, m)
        pull_right = answer(near, far, members - 1 - m)
        system = np.array([
            [1.0, 0.0, -pull_left, 0.0],
            [0.0, 1.0, 0.0, -pull_right],
            [-near, -far, 1.0, 0.0],
            [-far, -near, 0.0, 1.0],
        ])
        taking[m, :8] = np.linalg.inv(system)[:2].reshape(8)
    return sending, taking


def answer(near, far, members):
    if members == 0:
        return 0.0
    push = np.zeros(2 * members)
    push[0], push[1] = near, far
    return chain_system(near, far, members)[0] @ push


def sweep_table(length, factor):
    half = 0.5 * factor
    ratio = np.zeros(length)
    last = 0.0
    for i in range(length):
        ratio[i] = last = half / (1.0 + factor - half * last)
    decay = np.cumprod(ratio)
    return np.stack([ratio, decay, decay])


def split(table, axis):
    rows = np.moveaxis(np.asarray(table, np.float64), axis, 0)
    high = np.zeros(rows.shape, BF16)
    carried = np.zeros(rows.shape[1:])
    for k, row in enumerate(rows):
        high[k] = (row + carried).astype(np.float32).astype(BF16)
        carried = carried + row - high[k].astype(np.float64)
    low = (rows - high.astype(np.float64)).astype(np.float32).astype(BF16)
    return np.moveaxis(high, 0, axis), np.moveaxis(low, 0, axis)


def parts(values):
    high = values.astype(BF16)
    return high, (values - high.astype(F32)).astype(BF16)


def dot(a, b):
    return jnp.dot(a, b, preferred_element_type=F32)


def exact_dot(a, b):
    return jnp.dot(a, b, precision=lax.Precision.HIGHEST, preferred_element_type=F32)


def upward_dot(high, low, table_ref):
    count, depth = high.shape
    both = dot(jnp.concatenate([high, low], axis=0), table_ref[:depth])
    return both[:count] + both[count:] + dot(high, table_ref[depth:])


def north_dot(table_ref, values):
    north = values.shape[0]
    solved = dot(table_ref[...], jnp.concatenate(parts(values), axis=0))
    return solved[:north] + solved[north:]


def pick(column, me):
    value = float(column[0])
    for k in range(1, len(column)):
        value = jnp.where(me == k, float(column[k]), value)
    return value


def send_all(ends, table, me, out_refs):
    for d, out_ref in enumerate(out_refs):
        out_ref[...] = pick(table[:, 2 * d], me) * ends[0] + pick(table[:, 2 * d + 1], me) * ends[1]


def take_all(ends, table, me, messages):
    left = right = 0.0
    for d, message in enumerate(messages):
        left += pick(table[:, 8 + 2 * d], me) * message
        right += pick(table[:, 9 + 2 * d], me) * message
    known = (left, right) + tuple(ends)
    return [sum(pick(table[:, 4 * side + k], me) * known[k] for k in range(4)) for side in range(2)]


def diagonal(size):
    return lax.broadcasted_iota(jnp.int32, (size, size), 0) == lax.broadcasted_iota(jnp.int32, (size, size), 1)


def as_row(column):
    return jnp.sum(jnp.where(diagonal(column.shape[0]), column, 0.0), axis=0, keepdims=True)


def as_column(row):
    return jnp.sum(jnp.where(diagonal(row.shape[1]), row, 0.0), axis=1, keepdims=True)


def stacked(rows, height):
    filler = jnp.zeros((height - sum(row.shape[0] for row in rows), rows[0].shape[1]), F32)
    return jnp.concatenate(list(rows) + [filler], axis=0)


def ordered(pair, east):
    if not pair:
        return lambda i: i
    flip = lax.axis_index("gx")
    return lambda i: jnp.where(flip == 0, i, east - 1 - i)


def end_places(count, east):
    if count == 1:
        return [(east - 1, 0)]
    return [(0, 0), (east - 1, 1)]


def local_kernel(
    pair, group, factors, sending,
    tables_hbm, warmth_hbm, supply_hbm,
    swept_ref, warmth_ref, upward_ends_ref, north_ends_ref, east_ends_ref, *rest,
):
    to_up = sending.shape[1] // 2
    up_refs = rest[:to_up]
    supply_ref, both_ref, edges_ref, tables_ref, up_ref, north_ref, even_ref, odd_ref, sems = rest[to_up:]
    east, north, upward = supply_ref.shape
    groups = east // group
    count = east_ends_ref.shape[0]
    place = ordered(pair, east)

    def fetch(which, g):
        start = jnp.minimum(place(g * group), place(g * group + group - 1))
        block = pl.ds(start, group)
        if which == 0:
            return pltpu.make_async_copy(warmth_hbm.at[block], warmth_ref.at[pl.ds(start + 1, group)], sems.at[0, g])
        return pltpu.make_async_copy(supply_hbm.at[block], supply_ref.at[block], sems.at[1, g])

    tables = pltpu.make_async_copy(tables_hbm, tables_ref, sems.at[0, groups])
    tables.start()
    for g in range(groups):
        for which in range(2):
            fetch(which, g).start()
    warmth_ref[0] = jnp.zeros((north, upward), F32)
    warmth_ref[east + 1] = jnp.zeros((north, upward), F32)
    both_ref[...] = jnp.zeros_like(both_ref)
    east_ends_ref[...] = jnp.zeros_like(east_ends_ref)
    lane = lax.broadcasted_iota(jnp.int32, (1, 2 * east), 1)
    line = lax.broadcasted_iota(jnp.int32, (8, 1), 0)
    half_factor = 0.5 * factors[0]
    tables.wait()
    up_ref[...] = tables_ref[: 2 * upward].astype(BF16)
    north_ref[...] = tables_ref[2 * upward : 2 * upward + 2 * north, : 2 * north].astype(BF16)
    sweep = 2 * upward + 2 * north
    fetch(0, 0).wait()

    def arrive(g):
        fetch(1, g).wait()

        @pl.when(g + 1 < groups)
        def _():
            fetch(0, g + 1).wait()

    def shifted(values, step):
        turned = pltpu.roll(values, step % north, 0)
        if step > 0:
            return jnp.concatenate([jnp.where(line == 0, 0.0, turned[:8]), turned[8:]], axis=0)
        return jnp.concatenate([turned[:-8], jnp.where(line == 7, 0.0, turned[-8:])], axis=0)

    def bent_plane(g, k):
        i = g * group + k
        x = place(i)
        warm = warmth_ref[x + 1]
        bent = (warmth_ref[x] - warm) + (warmth_ref[x + 2] - warm)
        across = (shifted(warm, 1) - warm) + (shifted(warm, -1) - warm)
        edges_ref[pl.ds(i, 1)] = warm[:1]
        edges_ref[pl.ds(east + i, 1)] = warm[north - 1 :]
        return parts((supply_ref[x] + 2.0 * warm) + (factors[0] * bent + factors[1] * across))

    def solve_up(planes, slot_ref):
        high, low = (jnp.concatenate(half, axis=0) for half in zip(*planes))
        slot_ref[...] = upward_dot(high, low, up_ref)

    def north_plane(g, k, slot_ref):
        i = g * group + k
        first = slot_ref[k * north : (k + 1) * north]
        both = jnp.where(lane < east, first[:, : 2 * east], first[:, upward - 2 * east :])
        both = pltpu.roll(both, i, 1)
        both_ref[0] = jnp.where(lane == i, both, both_ref[0])
        both_ref[1] = jnp.where(lane == lax.rem(i + 2 * east - 1, 2 * east), both, both_ref[1])
        solved = north_dot(north_ref, first - 2.0 * warmth_ref[place(i) + 1])
        north_ends_ref[0, pl.ds(i, 1)] = half_factor * solved[:1]
        north_ends_ref[1, pl.ds(i, 1)] = half_factor * solved[north - 1 :]
        swept = solved + tables_ref[pl.ds(sweep + i, 1), :] * east_ends_ref[count - 1]
        swept_ref[i] = swept
        east_ends_ref[count - 1] = swept
        if not pair:
            east_ends_ref[0] += tables_ref[pl.ds(sweep + east + i, 1), :] * swept

    def step(g, slot_ref, last_ref):
        arrive(g)
        planes = []
        for k in range(group):
            planes.append(bent_plane(g, k))
            north_plane(g - 1, k, last_ref)
        solve_up(planes, slot_ref)

    arrive(0)
    solve_up([bent_plane(0, k) for k in range(group)], even_ref)

    def body(j, _):
        step(2 * j + 1, odd_ref, even_ref)
        step(2 * j + 2, even_ref, odd_ref)
        return 0

    lax.fori_loop(0, groups // 2 - 1, body, 0)
    step(groups - 1, odd_ref, even_ref)
    for k in range(group):
        north_plane(groups - 1, k, odd_ref)

    ends = end_places(count, east)
    planes = [warmth_ref[place(i) + 1] for i, _ in ends]
    solved_up = upward_dot(*parts(jnp.concatenate([edges_ref[...]] + planes, axis=0)), up_ref)
    east_ends_ref[count - 1] = tables_ref[sweep + 2 * east : sweep + 2 * east + 1, :] * east_ends_ref[count - 1]
    height = north_ends_ref.shape[1]
    rows = [[], []]
    for p in range(count):
        solved = half_factor * north_dot(north_ref, solved_up[2 * east + p * north : 2 * east + (p + 1) * north])
        rows[0].append(solved[:1])
        rows[1].append(solved[north - 1 :])
        east_ends_ref[p] += 2.0 * solved
    for end in range(2):
        north_ends_ref[end, :east] += 2.0 * solved_up[end * east : (end + 1) * east]
        north_ends_ref[end, east:] = stacked(rows[end], height - east)

    half = north // 2
    folded = []
    for end in range(2):
        top, bottom = both_ref[end, :half], both_ref[end, half:]
        top, bottom = pltpu.roll(top, end, 1), pltpu.roll(bottom, east + end, 1)
        folded.append(jnp.where(lane < east, top, bottom))
    upward_ends = []
    for end, column in enumerate((slice(0, 1), slice(upward - 1, upward))):
        extra = [as_row(solved_up[k * north : (k + 1) * north, column]) for k in range(1 + count)]
        upward_ends.append(stacked([folded[end]] + extra, upward_ends_ref.shape[1]))
        upward_ends_ref[end] = upward_ends[end]
    send_all(upward_ends, sending, lax.axis_index("gz"), up_refs)


def upward_kernel(
    count, taking, sending,
    ends_ref, north_ends_ref, north_inverse_ref, east_twice_ref, spread_ref, *rest,
):
    taken = (taking.shape[1] - 8) // 2
    message_refs = rest[:taken]
    columns_ref, north_out_ref, plane_ref, *out_refs = rest[taken:]
    north, lanes = columns_ref.shape
    east, half = lanes // 2, north // 2
    lane = lax.broadcasted_iota(jnp.int32, (1, lanes), 1)
    before, after = take_all(
        (ends_ref[0], ends_ref[1]), taking, lax.axis_index("gz"), [ref[...] for ref in message_refs]
    )

    def paired(end, rows):
        if end == 0:
            return jnp.where(lane < east, before[rows], pltpu.roll(after[rows], east, 1))
        return jnp.where(lane < east, pltpu.roll(before[rows], east, 1), after[rows])

    solved = exact_dot(north_inverse_ref[...], jnp.concatenate([paired(0, slice(0, half)), paired(1, slice(0, half))], axis=0))
    columns = exact_dot(solved, east_twice_ref[...])
    columns_ref[...] = columns
    planes = []
    for p in range(count):
        row = slice(half + 1 + p, half + 2 + p)
        planes.append([
            jnp.sum(north_inverse_ref[...] * side[row], axis=1, keepdims=True) for side in (before, after)
        ])
    height = north_ends_ref.shape[1]
    shape = (height, lanes)
    row = lax.broadcasted_iota(jnp.int32, shape, 0)
    short = lax.broadcasted_iota(jnp.int32, shape, 1) % east
    own = (row < east) & (short == row)
    behind = (row >= east) & (row < east + count) & (short == row - east)
    picked = []
    for end, y in enumerate((0, north - 1)):
        first = solved[y : y + 1] + 2.0 * paired(end, slice(half, half + 1))
        second = jnp.zeros((1, lanes), F32)
        for _, k in end_places(count, east):
            for side in range(2):
                second = jnp.where(lane == side * east + k, planes[k][side][y : y + 1], second)
        picked.append(jnp.where(own, first, 0.0) + jnp.where(behind, second, 0.0))
    added = exact_dot(jnp.concatenate(picked, axis=0), spread_ref[...])
    ends = []
    for end in range(2):
        ends.append(north_ends_ref[end] + added[end * height : (end + 1) * height])
        north_out_ref[end] = ends[end]
    send_all(ends, sending, lax.axis_index("gy"), out_refs)
    for i, k in end_places(count, east):
        rows = []
        for side in range(2):
            rows.append(as_row(columns[:, side * east + i : side * east + i + 1] + 2.0 * planes[k][side]))
        plane_ref[k] = stacked(rows, 8)


def north_kernel(
    count, taking,
    ends_ref, plane_ref, east_inverse_ref, *rest,
):
    taken = (taking.shape[1] - 8) // 2
    message_refs = rest[:taken]
    rows_ref, small_ref = rest[taken:]
    _, east, upward = rows_ref.shape
    sides = take_all((ends_ref[0], ends_ref[1]), taking, lax.axis_index("gy"), [ref[...] for ref in message_refs])
    swept = [exact_dot(east_inverse_ref[...], side[:east]) for side in sides]
    for n in range(2):
        rows_ref[n] = swept[n]
    for i, k in end_places(count, east):
        rows = [swept[n][i : i + 1] + 2.0 * sides[n][east + k : east + k + 1] for n in range(2)]
        wide = jnp.concatenate([plane_ref[k], jnp.zeros((8, upward - plane_ref.shape[2]), F32)], axis=1)
        small_ref[k] = stacked(rows + [wide[:2]], 8)


def final_kernel(
    pair, table, tile,
    sweep_ref, own_ref, other_ref, own_small_ref, other_small_ref,
    swept_ref, warmth_ref, columns_ref, rows_ref, upward_spikes_ref, north_spikes_ref,
    out_hbm,
    out_ref, sides_ref, sems,
):
    east, north, upward = out_ref.shape
    place = ordered(pair, east)

    def widened(plane, small):
        for side in range(2):
            plane += north_spikes_ref[side] * small[side : side + 1]
            plane += as_column(small[2 + side : 3 + side, :north]) * upward_spikes_ref[side : side + 1, :]
        return plane

    if pair:
        near, far = float(table[0]), float(table[1])
        sides_ref[0] = widened(
            near * other_ref[0] + far * own_ref[0], near * other_small_ref[0] + far * own_small_ref[0]
        )
    else:
        me = lax.axis_index("gx")
        members = table.shape[0]
        for side in range(2):
            plane, small = 0.0, 0.0
            for m in range(members):
                for end in range(2):
                    weight = pick(table[:, side, 2 * m + end], me)
                    plane += weight * other_ref[m, end]
                    small += weight * other_small_ref[m, end]
            sides_ref[side] = widened(plane, small)
    last = sides_ref.shape[0] - 1

    def send(t):
        block = pl.ds(pl.multiple_of(t * tile, tile), tile)
        return pltpu.make_async_copy(out_ref.at[:, block], out_hbm.at[:, block], sems.at[t])

    def body(t, _):
        block = pl.ds(pl.multiple_of(t * tile, tile), tile)
        value = sides_ref[last, block]
        columns = columns_ref[block]
        first_spike, last_spike = north_spikes_ref[0, block], north_spikes_ref[1, block]
        for i in reversed(range(east)):
            value = sweep_ref[0, i] * (swept_ref[i, block] + value)
            if not pair:
                value += sweep_ref[2, i] * sides_ref[0, block]
            added = (
                columns[:, i : i + 1] * upward_spikes_ref[0:1, :]
                + columns[:, east + i : east + i + 1] * upward_spikes_ref[1:2, :]
            )
            added += first_spike * rows_ref[0, i : i + 1, :] + last_spike * rows_ref[1, i : i + 1, :]
            x = place(i)
            out_ref[x, block] = warmth_ref[x + 1, block] + value + added
        send(t).start()
        return 0

    lax.fori_loop(0, north // tile, body, 0)
    for t in range(north // tile):
        send(t).wait()


def spread_out(messages, axis):
    members = lax.axis_size(axis)
    taken = [
        lax.ppermute(messages[d], axis, [(k, peers(k, members, d + 1)[0]) for k in range(members)])
        for d in reversed(range(len(messages)))
    ]
    return taken[::-1]


def local(initial_warmth, heat_supply):
    shape = east, north, upward = initial_warmth.shape
    members = [lax.axis_size(axis) for axis in ("gx", "gy", "gz")]
    factors = [float((n * m) ** 2 // 4) for n, m in zip(shape, members)]
    lines = [line_tables(n, factor) for n, factor in zip(shape, factors)]
    sweep = sweep_table(east, factors[0])
    ratio, weights = sweep[:2]
    sweep = sweep.astype(np.float32)
    exchanges = [exchange_tables(line[1], line[2], m) for line, m in zip(lines, members)]
    upward_high, upward_low = split(lines[2][0], 0)
    north_high, north_low = split(lines[1][0] / (0.5 * factors[0]), 1)
    north_stack = np.block([[north_high, north_high], [north_low, np.zeros_like(north_low)]])
    tables = np.concatenate([
        np.concatenate([upward_high, upward_low]).astype(np.float32),
        np.pad(north_stack.astype(np.float32), ((0, 0), (0, max(upward - 2 * north, 0)))),
        np.repeat(np.concatenate([[0.0], ratio[:-1], weights, ratio[-1:], np.zeros(7)])[:, None], upward, axis=1).astype(np.float32),
    ])
    east_inverse = lines[0][0].astype(np.float32)
    north_inverse = lines[1][0].astype(np.float32)
    east_twice = np.kron(np.eye(2), lines[0][0]).astype(np.float32)
    upward_spikes = np.stack(lines[2][1:]).astype(np.float32)
    spread = np.repeat(upward_spikes, east, axis=0)
    north_spikes = np.broadcast_to(np.stack(lines[1][1:])[:, :, None], (2, north, upward)).astype(np.float32)

    pair = members[0] == 2
    count = 1 if pair else 2
    height = east + 8
    to_up, to_north = members[2] - 1, members[1] - 1
    vmem = pl.BlockSpec(memory_space=pltpu.VMEM)
    smem = pl.BlockSpec(memory_space=pltpu.SMEM)
    hbm = pl.BlockSpec(memory_space=pltpu.HBM)

    def kept(*sizes):
        return jax.ShapeDtypeStruct(sizes, F32)

    group = 4
    folded = kept(north // 2 + 8, 2 * east)
    swept, warmth, upward_ends, north_ends, own, *messages = pl.pallas_call(
        functools.partial(local_kernel, pair, group, factors, exchanges[2][0]),
        in_specs=[hbm] * 3,
        out_specs=[vmem] * (5 + to_up),
        out_shape=[
            pltpu.VMEM(shape, F32),
            pltpu.VMEM((east + 2, north, upward), F32),
            kept(2, *folded.shape),
            kept(2, height, upward),
            kept(count, north, upward),
        ]
        + [folded] * to_up,
        scratch_shapes=[
            pltpu.VMEM(shape, F32),
            pltpu.VMEM((2, north, 2 * east), F32),
            pltpu.VMEM((2 * east, upward), F32),
            pltpu.VMEM(tables.shape, F32),
            pltpu.VMEM((2 * upward, upward), BF16),
            pltpu.VMEM((2 * north, 2 * north), BF16),
            pltpu.VMEM((group * north, upward), F32),
            pltpu.VMEM((group * north, upward), F32),
            pltpu.SemaphoreType.DMA((2, east // group + 1)),
        ],
        compiler_params=pltpu.CompilerParams(vmem_limit_bytes=32 * MIB),
    )(pltpu.with_memory_space_constraint(jnp.asarray(tables), pltpu.HBM), initial_warmth, heat_supply)

    messages = spread_out(messages, "gz")
    if pair:
        other = lax.ppermute(own, "gx", [(0, 1), (1, 0)])
    else:
        other = lax.all_gather(own, "gx")
    columns, north_ends, planes, *messages = pl.pallas_call(
        functools.partial(upward_kernel, count, exchanges[2][1], exchanges[1][0]),
        in_specs=[vmem] * (5 + to_up),
        out_specs=[vmem] * (3 + to_north),
        out_shape=[kept(north, 2 * east), kept(2, height, upward), kept(count, 8, north)]
        + [kept(height, upward)] * to_north,
        compiler_params=pltpu.CompilerParams(vmem_limit_bytes=6 * MIB),
    )(upward_ends, north_ends, north_inverse, east_twice, spread, *messages)

    messages = spread_out(messages, "gy")
    rows, own_small = pl.pallas_call(
        functools.partial(north_kernel, count, exchanges[1][1]),
        in_specs=[vmem] * (3 + to_north),
        out_specs=[vmem] * 2,
        out_shape=[kept(2, east, upward), kept(count, 8, upward)],
        compiler_params=pltpu.CompilerParams(vmem_limit_bytes=6 * MIB),
    )(north_ends, planes, east_inverse, *messages)

    if pair:
        other_small = lax.ppermute(own_small, "gx", [(0, 1), (1, 0)])
        near = lines[0][1][0]
        table = np.array([1.0, near]) / (1.0 - near**2)
    else:
        other_small = lax.all_gather(own_small, "gx")
        table = interface_table(lines[0][1], lines[0][2], members[0])
    swept = pltpu.with_memory_space_constraint(swept, pltpu.VMEM)
    warmth = pltpu.with_memory_space_constraint(warmth, pltpu.VMEM)
    tile = 32
    return pl.pallas_call(
        functools.partial(final_kernel, pair, table, tile),
        in_specs=[smem] + [vmem] * 10,
        out_specs=hbm,
        out_shape=kept(*shape),
        scratch_shapes=[
            pltpu.VMEM(shape, F32),
            pltpu.VMEM((count, north, upward), F32),
            pltpu.SemaphoreType.DMA((north // tile,)),
        ],
        compiler_params=pltpu.CompilerParams(vmem_limit_bytes=16 * MIB),
    )(sweep, own, other, own_small, other_small, swept, warmth, columns, rows, upward_spikes, north_spikes)


def solution(mesh):
    return jax.shard_map(
        local,
        mesh=mesh,
        in_specs=(P("gx", "gy", "gz"), P("gx", "gy", "gz")),
        out_specs=P("gx", "gy", "gz"),
        check_vma=False,
    )
```

```python
import functools

import jax
import jax.numpy as jnp
import numpy as np
from jax import lax
from jax.experimental import pallas as pl
from jax.experimental.pallas import tpu as pltpu
from jax.sharding import PartitionSpec as P

F32 = jnp.float32
BF16 = jnp.bfloat16
MIB = 1 << 20


def line_tables(length, factor):
    matrix = (1.0 + factor) * np.eye(length)
    matrix -= 0.5 * factor * (np.eye(length, k=1) + np.eye(length, k=-1))
    inverse = np.linalg.inv(matrix)
    inverse = 0.5 * (inverse + inverse.T)
    return inverse, 0.5 * factor * inverse[:, 0], 0.5 * factor * inverse[:, -1]


def chain_system(near, far, members):
    system = np.eye(2 * members)
    for m in range(members):
        if m > 0:
            system[2 * m, 2 * m - 1] -= near
            system[2 * m + 1, 2 * m - 1] -= far
        if m < members - 1:
            system[2 * m, 2 * m + 2] -= far
            system[2 * m + 1, 2 * m + 2] -= near
    return np.linalg.inv(system)


def interface_table(before, after, members):
    solved = chain_system(before[0], before[-1], members)
    rows = np.zeros((members, 2, 2 * members))
    for m in range(members):
        if m > 0:
            rows[m, 0] = solved[2 * m - 1]
        if m < members - 1:
            rows[m, 1] = solved[2 * m + 2]
    return rows


def peers(member, members, distance):
    if members & (members - 1) == 0:
        return member ^ distance, member ^ distance
    return (member + distance) % members, (member - distance) % members


def exchange_tables(before, after, members):
    near, far = before[0], before[-1]
    sending = np.zeros((members, 2 * (members - 1)))
    taking = np.zeros((members, 8 + 2 * (members - 1)))
    for m in range(members):
        right = chain_system(near, far, members - 1 - m)
        left = chain_system(near, far, m)
        for d in range(1, members):
            k = peers(m, members, d)[1]
            if k > m:
                sending[k, 2 * d - 2 : 2 * d] = right[0, 2 * (k - m - 1) : 2 * (k - m)]
                taking[m, 8 + 2 * d - 1] = 1.0
            else:
                sending[k, 2 * d - 2 : 2 * d] = left[-1, 2 * k : 2 * k + 2]
                taking[m, 8 + 2 * d - 2] = 1.0
        pull_left = answer(near, far, m)
        pull_right = answer(near, far, members - 1 - m)
        system = np.array([
            [1.0, 0.0, -pull_left, 0.0],
            [0.0, 1.0, 0.0, -pull_right],
            [-near, -far, 1.0, 0.0],
            [-far, -near, 0.0, 1.0],
        ])
        taking[m, :8] = np.linalg.inv(system)[:2].reshape(8)
    return sending, taking


def answer(near, far, members):
    if members == 0:
        return 0.0
    push = np.zeros(2 * members)
    push[0], push[1] = near, far
    return chain_system(near, far, members)[0] @ push


def sweep_table(length, factor):
    half = 0.5 * factor
    ratio = np.zeros(length)
    last = 0.0
    for i in range(length):
        ratio[i] = last = half / (1.0 + factor - half * last)
    decay = np.cumprod(ratio)
    return np.stack([ratio, decay, decay])


def split(table, axis):
    rows = np.moveaxis(np.asarray(table, np.float64), axis, 0)
    high = np.zeros(rows.shape, BF16)
    carried = np.zeros(rows.shape[1:])
    for k, row in enumerate(rows):
        high[k] = (row + carried).astype(np.float32).astype(BF16)
        carried = carried + row - high[k].astype(np.float64)
    low = (rows - high.astype(np.float64)).astype(np.float32).astype(BF16)
    return np.moveaxis(high, 0, axis), np.moveaxis(low, 0, axis)


def parts(values):
    high = values.astype(BF16)
    return high, (values - high.astype(F32)).astype(BF16)


def dot(a, b):
    return jnp.dot(a, b, preferred_element_type=F32)


def exact_dot(a, b):
    return jnp.dot(a, b, precision=lax.Precision.HIGHEST, preferred_element_type=F32)


def upward_dot(values, table_ref):
    high, low = parts(values)
    count, depth = values.shape
    both = dot(jnp.concatenate([high, low], axis=0), table_ref[:depth])
    return both[:count] + both[count:] + dot(high, table_ref[depth:])


def north_dot(table_ref, values):
    north = values.shape[0]
    solved = dot(table_ref[...], jnp.concatenate(parts(values), axis=0))
    return solved[:north] + solved[north:]


def pick(column, me):
    value = float(column[0])
    for k in range(1, len(column)):
        value = jnp.where(me == k, float(column[k]), value)
    return value


def send_all(ends, table, me, out_refs):
    for d, out_ref in enumerate(out_refs):
        out_ref[...] = pick(table[:, 2 * d], me) * ends[0] + pick(table[:, 2 * d + 1], me) * ends[1]


def take_all(ends, table, me, messages):
    left = right = 0.0
    for d, message in enumerate(messages):
        left += pick(table[:, 8 + 2 * d], me) * message
        right += pick(table[:, 9 + 2 * d], me) * message
    known = (left, right) + tuple(ends)
    return [sum(pick(table[:, 4 * side + k], me) * known[k] for k in range(4)) for side in range(2)]


def diagonal(size):
    return lax.broadcasted_iota(jnp.int32, (size, size), 0) == lax.broadcasted_iota(jnp.int32, (size, size), 1)


def as_row(column):
    return jnp.sum(jnp.where(diagonal(column.shape[0]), column, 0.0), axis=0, keepdims=True)


def as_column(row):
    return jnp.sum(jnp.where(diagonal(row.shape[1]), row, 0.0), axis=1, keepdims=True)


def stacked(rows, height):
    filler = jnp.zeros((height - sum(row.shape[0] for row in rows), rows[0].shape[1]), F32)
    return jnp.concatenate(list(rows) + [filler], axis=0)


def ordered(pair, east):
    if not pair:
        return lambda i: i
    flip = lax.axis_index("gx")
    return lambda i: jnp.where(flip == 0, i, east - 1 - i)


def end_places(count, east):
    if count == 1:
        return [(east - 1, 0)]
    return [(0, 0), (east - 1, 1)]


def local_kernel(
    pair, group, factors, sending,
    tables_hbm, warmth_hbm, supply_hbm,
    swept_ref, warmth_ref, upward_ends_ref, north_ends_ref, east_ends_ref, *rest,
):
    to_up = sending.shape[1] // 2
    up_refs = rest[:to_up]
    supply_ref, both_ref, edges_ref, tables_ref, up_ref, north_ref, even_ref, odd_ref, sems = rest[to_up:]
    east, north, upward = supply_ref.shape
    groups = east // group
    count = east_ends_ref.shape[0]
    place = ordered(pair, east)

    def fetch(which, g):
        start = jnp.minimum(place(g * group), place(g * group + group - 1))
        block = pl.ds(start, group)
        if which == 0:
            return pltpu.make_async_copy(warmth_hbm.at[block], warmth_ref.at[pl.ds(start + 1, group)], sems.at[0, g])
        return pltpu.make_async_copy(supply_hbm.at[block], supply_ref.at[block], sems.at[1, g])

    def begin(g):
        for which in range(2):
            fetch(which, g).start()

    ahead = 3
    tables = pltpu.make_async_copy(tables_hbm, tables_ref, sems.at[0, groups])
    tables.start()
    for g in range(min(ahead, groups)):
        begin(g)
    warmth_ref[0] = jnp.zeros((north, upward), F32)
    warmth_ref[east + 1] = jnp.zeros((north, upward), F32)
    both_ref[...] = jnp.zeros_like(both_ref)
    east_ends_ref[...] = jnp.zeros_like(east_ends_ref)
    lane = lax.broadcasted_iota(jnp.int32, (1, 2 * east), 1)
    line = lax.broadcasted_iota(jnp.int32, (8, 1), 0)
    half_factor = 0.5 * factors[0]
    tables.wait()
    up_ref[...] = tables_ref[: 2 * upward].astype(BF16)
    north_ref[...] = tables_ref[2 * upward : 2 * upward + 2 * north, : 2 * north].astype(BF16)
    sweep = 2 * upward + 2 * north
    fetch(0, 0).wait()

    def arrive(g):
        fetch(1, g).wait()

        @pl.when(g + 1 < groups)
        def _():
            fetch(0, g + 1).wait()

        @pl.when(g + ahead < groups)
        def _():
            begin(g + ahead)

    def shifted(values, step):
        turned = pltpu.roll(values, step % north, 0)
        if step > 0:
            return jnp.concatenate([jnp.where(line == 0, 0.0, turned[:8]), turned[8:]], axis=0)
        return jnp.concatenate([turned[:-8], jnp.where(line == 7, 0.0, turned[-8:])], axis=0)

    def upward_part(g, slot_ref):
        heat_list = []
        for k in range(group):
            i = g * group + k
            x = place(i)
            warm = warmth_ref[x + 1]
            bent = (warmth_ref[x] - warm) + (warmth_ref[x + 2] - warm)
            across = (shifted(warm, 1) - warm) + (shifted(warm, -1) - warm)
            heat_list.append((supply_ref[x] + 2.0 * warm) + (factors[0] * bent + factors[1] * across))
            edges_ref[pl.ds(i, 1)] = warm[:1]
            edges_ref[pl.ds(east + i, 1)] = warm[north - 1 :]
        slot_ref[...] = upward_dot(jnp.concatenate(heat_list, axis=0), up_ref)

    def north_part(g, slot_ref):
        for k in range(group):
            i = g * group + k
            first = slot_ref[k * north : (k + 1) * north]
            both = jnp.where(lane < east, first[:, : 2 * east], first[:, upward - 2 * east :])
            both = pltpu.roll(both, i, 1)
            both_ref[0] = jnp.where(lane == i, both, both_ref[0])
            both_ref[1] = jnp.where(lane == lax.rem(i + 2 * east - 1, 2 * east), both, both_ref[1])
            solved = north_dot(north_ref, first - 2.0 * warmth_ref[place(i) + 1])
            north_ends_ref[0, pl.ds(i, 1)] = half_factor * solved[:1]
            north_ends_ref[1, pl.ds(i, 1)] = half_factor * solved[north - 1 :]
            swept = solved + tables_ref[pl.ds(sweep + i, 1), :] * east_ends_ref[count - 1]
            swept_ref[i] = swept
            east_ends_ref[count - 1] = swept
            if not pair:
                east_ends_ref[0] += tables_ref[pl.ds(sweep + east + i, 1), :] * swept

    arrive(0)
    upward_part(0, even_ref)

    def body(j, _):
        g = 2 * j
        arrive(g + 1)
        upward_part(g + 1, odd_ref)
        north_part(g, even_ref)
        later = jnp.minimum(g + 2, groups - 1)

        @pl.when(g + 2 < groups)
        def _():
            arrive(g + 2)

        upward_part(later, even_ref)
        north_part(g + 1, odd_ref)
        return 0

    lax.fori_loop(0, groups // 2, body, 0)

    ends = end_places(count, east)
    planes = [warmth_ref[place(i) + 1] for i, _ in ends]
    solved_up = upward_dot(jnp.concatenate([edges_ref[...]] + planes, axis=0), up_ref)
    east_ends_ref[count - 1] = tables_ref[sweep + 2 * east : sweep + 2 * east + 1, :] * east_ends_ref[count - 1]
    height = north_ends_ref.shape[1]
    rows = [[], []]
    for p in range(count):
        solved = half_factor * north_dot(north_ref, solved_up[2 * east + p * north : 2 * east + (p + 1) * north])
        rows[0].append(solved[:1])
        rows[1].append(solved[north - 1 :])
        east_ends_ref[p] += 2.0 * solved
    for end in range(2):
        north_ends_ref[end, :east] += 2.0 * solved_up[end * east : (end + 1) * east]
        north_ends_ref[end, east:] = stacked(rows[end], height - east)

    half = north // 2
    folded = []
    for end in range(2):
        top, bottom = both_ref[end, :half], both_ref[end, half:]
        top, bottom = pltpu.roll(top, end, 1), pltpu.roll(bottom, east + end, 1)
        folded.append(jnp.where(lane < east, top, bottom))
    upward_ends = []
    for end, column in enumerate((slice(0, 1), slice(upward - 1, upward))):
        extra = [as_row(solved_up[k * north : (k + 1) * north, column]) for k in range(1 + count)]
        upward_ends.append(stacked([folded[end]] + extra, upward_ends_ref.shape[1]))
        upward_ends_ref[end] = upward_ends[end]
    send_all(upward_ends, sending, lax.axis_index("gz"), up_refs)


def upward_kernel(
    count, taking, sending,
    ends_ref, north_ends_ref, north_inverse_ref, east_twice_ref, spread_ref, *rest,
):
    taken = (taking.shape[1] - 8) // 2
    message_refs = rest[:taken]
    columns_ref, north_out_ref, plane_ref, *out_refs = rest[taken:]
    north, lanes = columns_ref.shape
    east, half = lanes // 2, north // 2
    lane = lax.broadcasted_iota(jnp.int32, (1, lanes), 1)
    before, after = take_all(
        (ends_ref[0], ends_ref[1]), taking, lax.axis_index("gz"), [ref[...] for ref in message_refs]
    )

    def paired(end, rows):
        if end == 0:
            return jnp.where(lane < east, before[rows], pltpu.roll(after[rows], east, 1))
        return jnp.where(lane < east, pltpu.roll(before[rows], east, 1), after[rows])

    solved = exact_dot(north_inverse_ref[...], jnp.concatenate([paired(0, slice(0, half)), paired(1, slice(0, half))], axis=0))
    columns = exact_dot(solved, east_twice_ref[...])
    columns_ref[...] = columns
    planes = []
    for p in range(count):
        row = slice(half + 1 + p, half + 2 + p)
        planes.append([
            jnp.sum(north_inverse_ref[...] * side[row], axis=1, keepdims=True) for side in (before, after)
        ])
    height = north_ends_ref.shape[1]
    shape = (height, lanes)
    row = lax.broadcasted_iota(jnp.int32, shape, 0)
    short = lax.broadcasted_iota(jnp.int32, shape, 1) % east
    own = (row < east) & (short == row)
    behind = (row >= east) & (row < east + count) & (short == row - east)
    picked = []
    for end, y in enumerate((0, north - 1)):
        first = solved[y : y + 1] + 2.0 * paired(end, slice(half, half + 1))
        second = jnp.zeros((1, lanes), F32)
        for _, k in end_places(count, east):
            for side in range(2):
                second = jnp.where(lane == side * east + k, planes[k][side][y : y + 1], second)
        picked.append(jnp.where(own, first, 0.0) + jnp.where(behind, second, 0.0))
    added = exact_dot(jnp.concatenate(picked, axis=0), spread_ref[...])
    ends = []
    for end in range(2):
        ends.append(north_ends_ref[end] + added[end * height : (end + 1) * height])
        north_out_ref[end] = ends[end]
    send_all(ends, sending, lax.axis_index("gy"), out_refs)
    for i, k in end_places(count, east):
        rows = []
        for side in range(2):
            rows.append(as_row(columns[:, side * east + i : side * east + i + 1] + 2.0 * planes[k][side]))
        plane_ref[k] = stacked(rows, 8)


def north_kernel(
    count, taking,
    ends_ref, plane_ref, east_inverse_ref, *rest,
):
    taken = (taking.shape[1] - 8) // 2
    message_refs = rest[:taken]
    rows_ref, small_ref = rest[taken:]
    _, east, upward = rows_ref.shape
    sides = take_all((ends_ref[0], ends_ref[1]), taking, lax.axis_index("gy"), [ref[...] for ref in message_refs])
    swept = [exact_dot(east_inverse_ref[...], side[:east]) for side in sides]
    for n in range(2):
        rows_ref[n] = swept[n]
    for i, k in end_places(count, east):
        rows = [swept[n][i : i + 1] + 2.0 * sides[n][east + k : east + k + 1] for n in range(2)]
        wide = jnp.concatenate([plane_ref[k], jnp.zeros((8, upward - plane_ref.shape[2]), F32)], axis=1)
        small_ref[k] = stacked(rows + [wide[:2]], 8)


def final_kernel(
    pair, table, tile,
    sweep_ref, own_ref, other_ref, own_small_ref, other_small_ref,
    swept_ref, warmth_ref, columns_ref, rows_ref, upward_spikes_ref, north_spikes_ref,
    out_hbm,
    out_ref, sides_ref, sems,
):
    east, north, upward = out_ref.shape
    place = ordered(pair, east)

    def widened(plane, small):
        for side in range(2):
            plane += north_spikes_ref[side] * small[side : side + 1]
            plane += as_column(small[2 + side : 3 + side, :north]) * upward_spikes_ref[side : side + 1, :]
        return plane

    if pair:
        near, far = float(table[0]), float(table[1])
        sides_ref[0] = widened(
            near * other_ref[0] + far * own_ref[0], near * other_small_ref[0] + far * own_small_ref[0]
        )
    else:
        me = lax.axis_index("gx")
        members = table.shape[0]
        for side in range(2):
            plane, small = 0.0, 0.0
            for m in range(members):
                for end in range(2):
                    weight = pick(table[:, side, 2 * m + end], me)
                    plane += weight * other_ref[m, end]
                    small += weight * other_small_ref[m, end]
            sides_ref[side] = widened(plane, small)
    last = sides_ref.shape[0] - 1

    def send(t):
        block = pl.ds(pl.multiple_of(t * tile, tile), tile)
        return pltpu.make_async_copy(out_ref.at[:, block], out_hbm.at[:, block], sems.at[t])

    def body(t, _):
        block = pl.ds(pl.multiple_of(t * tile, tile), tile)
        value = sides_ref[last, block]
        columns = columns_ref[block]
        first_spike, last_spike = north_spikes_ref[0, block], north_spikes_ref[1, block]
        for i in reversed(range(east)):
            value = sweep_ref[0, i] * (swept_ref[i, block] + value)
            if not pair:
                value += sweep_ref[2, i] * sides_ref[0, block]
            added = (
                columns[:, i : i + 1] * upward_spikes_ref[0:1, :]
                + columns[:, east + i : east + i + 1] * upward_spikes_ref[1:2, :]
            )
            added += first_spike * rows_ref[0, i : i + 1, :] + last_spike * rows_ref[1, i : i + 1, :]
            x = place(i)
            out_ref[x, block] = warmth_ref[x + 1, block] + value + added
        send(t).start()
        return 0

    lax.fori_loop(0, north // tile, body, 0)
    for t in range(north // tile):
        send(t).wait()


def spread_out(messages, axis):
    members = lax.axis_size(axis)
    taken = [
        lax.ppermute(messages[d], axis, [(k, peers(k, members, d + 1)[0]) for k in range(members)])
        for d in reversed(range(len(messages)))
    ]
    return taken[::-1]


def local(initial_warmth, heat_supply):
    shape = east, north, upward = initial_warmth.shape
    members = [lax.axis_size(axis) for axis in ("gx", "gy", "gz")]
    factors = [float((n * m) ** 2 // 4) for n, m in zip(shape, members)]
    lines = [line_tables(n, factor) for n, factor in zip(shape, factors)]
    sweep = sweep_table(east, factors[0])
    ratio, weights = sweep[:2]
    sweep = sweep.astype(np.float32)
    exchanges = [exchange_tables(line[1], line[2], m) for line, m in zip(lines, members)]
    upward_high, upward_low = split(lines[2][0], 0)
    north_high, north_low = split(lines[1][0] / (0.5 * factors[0]), 1)
    north_stack = np.block([[north_high, north_high], [north_low, np.zeros_like(north_low)]])
    tables = np.concatenate([
        np.concatenate([upward_high, upward_low]).astype(np.float32),
        np.pad(north_stack.astype(np.float32), ((0, 0), (0, max(upward - 2 * north, 0)))),
        np.repeat(np.concatenate([[0.0], ratio[:-1], weights, ratio[-1:], np.zeros(7)])[:, None], upward, axis=1).astype(np.float32),
    ])
    east_inverse = lines[0][0].astype(np.float32)
    north_inverse = lines[1][0].astype(np.float32)
    east_twice = np.kron(np.eye(2), lines[0][0]).astype(np.float32)
    upward_spikes = np.stack(lines[2][1:]).astype(np.float32)
    spread = np.repeat(upward_spikes, east, axis=0)
    north_spikes = np.broadcast_to(np.stack(lines[1][1:])[:, :, None], (2, north, upward)).astype(np.float32)

    pair = members[0] == 2
    count = 1 if pair else 2
    height = east + 8
    to_up, to_north = members[2] - 1, members[1] - 1
    vmem = pl.BlockSpec(memory_space=pltpu.VMEM)
    smem = pl.BlockSpec(memory_space=pltpu.SMEM)
    hbm = pl.BlockSpec(memory_space=pltpu.HBM)

    def kept(*sizes):
        return jax.ShapeDtypeStruct(sizes, F32)

    group = 4
    folded = kept(north // 2 + 8, 2 * east)
    swept, warmth, upward_ends, north_ends, own, *messages = pl.pallas_call(
        functools.partial(local_kernel, pair, group, factors, exchanges[2][0]),
        in_specs=[hbm] * 3,
        out_specs=[vmem] * (5 + to_up),
        out_shape=[
            pltpu.VMEM(shape, F32),
            pltpu.VMEM((east + 2, north, upward), F32),
            kept(2, *folded.shape),
            kept(2, height, upward),
            kept(count, north, upward),
        ]
        + [folded] * to_up,
        scratch_shapes=[
            pltpu.VMEM(shape, F32),
            pltpu.VMEM((2, north, 2 * east), F32),
            pltpu.VMEM((2 * east, upward), F32),
            pltpu.VMEM(tables.shape, F32),
            pltpu.VMEM((2 * upward, upward), BF16),
            pltpu.VMEM((2 * north, 2 * north), BF16),
            pltpu.VMEM((group * north, upward), F32),
            pltpu.VMEM((group * north, upward), F32),
            pltpu.SemaphoreType.DMA((2, east // group + 1)),
        ],
        compiler_params=pltpu.CompilerParams(vmem_limit_bytes=32 * MIB),
    )(pltpu.with_memory_space_constraint(jnp.asarray(tables), pltpu.HBM), initial_warmth, heat_supply)

    messages = spread_out(messages, "gz")
    if pair:
        other = lax.ppermute(own, "gx", [(0, 1), (1, 0)])
    else:
        other = lax.all_gather(own, "gx")
    columns, north_ends, planes, *messages = pl.pallas_call(
        functools.partial(upward_kernel, count, exchanges[2][1], exchanges[1][0]),
        in_specs=[vmem] * (5 + to_up),
        out_specs=[vmem] * (3 + to_north),
        out_shape=[kept(north, 2 * east), kept(2, height, upward), kept(count, 8, north)]
        + [kept(height, upward)] * to_north,
        compiler_params=pltpu.CompilerParams(vmem_limit_bytes=6 * MIB),
    )(upward_ends, north_ends, north_inverse, east_twice, spread, *messages)

    messages = spread_out(messages, "gy")
    rows, own_small = pl.pallas_call(
        functools.partial(north_kernel, count, exchanges[1][1]),
        in_specs=[vmem] * (3 + to_north),
        out_specs=[vmem] * 2,
        out_shape=[kept(2, east, upward), kept(count, 8, upward)],
        compiler_params=pltpu.CompilerParams(vmem_limit_bytes=6 * MIB),
    )(north_ends, planes, east_inverse, *messages)

    if pair:
        other_small = lax.ppermute(own_small, "gx", [(0, 1), (1, 0)])
        near = lines[0][1][0]
        table = np.array([1.0, near]) / (1.0 - near**2)
    else:
        other_small = lax.all_gather(own_small, "gx")
        table = interface_table(lines[0][1], lines[0][2], members[0])
    swept = pltpu.with_memory_space_constraint(swept, pltpu.VMEM)
    warmth = pltpu.with_memory_space_constraint(warmth, pltpu.VMEM)
    tile = 32
    return pl.pallas_call(
        functools.partial(final_kernel, pair, table, tile),
        in_specs=[smem] + [vmem] * 10,
        out_specs=hbm,
        out_shape=kept(*shape),
        scratch_shapes=[
            pltpu.VMEM(shape, F32),
            pltpu.VMEM((count, north, upward), F32),
            pltpu.SemaphoreType.DMA((north // tile,)),
        ],
        compiler_params=pltpu.CompilerParams(vmem_limit_bytes=16 * MIB),
    )(sweep, own, other, own_small, other_small, swept, warmth, columns, rows, upward_spikes, north_spikes)


def solution(mesh):
    return jax.shard_map(
        local,
        mesh=mesh,
        in_specs=(P("gx", "gy", "gz"), P("gx", "gy", "gz")),
        out_specs=P("gx", "gy", "gz"),
        check_vma=False,
    )
```

```python
import functools

import jax
import jax.numpy as jnp
import numpy as np
from jax import lax
from jax.experimental import pallas as pl
from jax.experimental.pallas import tpu as pltpu
from jax.sharding import PartitionSpec as P

F32 = jnp.float32
BF16 = jnp.bfloat16
MIB = 1 << 20


def line_tables(length, factor):
    matrix = (1.0 + factor) * np.eye(length)
    matrix -= 0.5 * factor * (np.eye(length, k=1) + np.eye(length, k=-1))
    inverse = np.linalg.inv(matrix)
    inverse = 0.5 * (inverse + inverse.T)
    return inverse, 0.5 * factor * inverse[:, 0], 0.5 * factor * inverse[:, -1]


def chain_system(near, far, members):
    system = np.eye(2 * members)
    for m in range(members):
        if m > 0:
            system[2 * m, 2 * m - 1] -= near
            system[2 * m + 1, 2 * m - 1] -= far
        if m < members - 1:
            system[2 * m, 2 * m + 2] -= far
            system[2 * m + 1, 2 * m + 2] -= near
    return np.linalg.inv(system)


def interface_table(before, after, members):
    solved = chain_system(before[0], before[-1], members)
    rows = np.zeros((members, 2, 2 * members))
    for m in range(members):
        if m > 0:
            rows[m, 0] = solved[2 * m - 1]
        if m < members - 1:
            rows[m, 1] = solved[2 * m + 2]
    return rows


def peers(member, members, distance):
    if members & (members - 1) == 0:
        return member ^ distance, member ^ distance
    return (member + distance) % members, (member - distance) % members


def exchange_tables(before, after, members):
    near, far = before[0], before[-1]
    sending = np.zeros((members, 2 * (members - 1)))
    taking = np.zeros((members, 8 + 2 * (members - 1)))
    for m in range(members):
        right = chain_system(near, far, members - 1 - m)
        left = chain_system(near, far, m)
        for d in range(1, members):
            k = peers(m, members, d)[1]
            if k > m:
                sending[k, 2 * d - 2 : 2 * d] = right[0, 2 * (k - m - 1) : 2 * (k - m)]
                taking[m, 8 + 2 * d - 1] = 1.0
            else:
                sending[k, 2 * d - 2 : 2 * d] = left[-1, 2 * k : 2 * k + 2]
                taking[m, 8 + 2 * d - 2] = 1.0
        pull_left = answer(near, far, m)
        pull_right = answer(near, far, members - 1 - m)
        system = np.array([
            [1.0, 0.0, -pull_left, 0.0],
            [0.0, 1.0, 0.0, -pull_right],
            [-near, -far, 1.0, 0.0],
            [-far, -near, 0.0, 1.0],
        ])
        taking[m, :8] = np.linalg.inv(system)[:2].reshape(8)
    return sending, taking


def answer(near, far, members):
    if members == 0:
        return 0.0
    push = np.zeros(2 * members)
    push[0], push[1] = near, far
    return chain_system(near, far, members)[0] @ push


def sweep_table(length, factor):
    half = 0.5 * factor
    ratio = np.zeros(length)
    last = 0.0
    for i in range(length):
        ratio[i] = last = half / (1.0 + factor - half * last)
    decay = np.cumprod(ratio)
    return np.stack([ratio, decay, decay])


def split(table, axis):
    rows = np.moveaxis(np.asarray(table, np.float64), axis, 0)
    high = np.zeros(rows.shape, BF16)
    carried = np.zeros(rows.shape[1:])
    for k, row in enumerate(rows):
        high[k] = (row + carried).astype(np.float32).astype(BF16)
        carried = carried + row - high[k].astype(np.float64)
    low = (rows - high.astype(np.float64)).astype(np.float32).astype(BF16)
    return np.moveaxis(high, 0, axis), np.moveaxis(low, 0, axis)


def parts(values):
    high = values.astype(BF16)
    return high, (values - high.astype(F32)).astype(BF16)


def dot(a, b):
    return jnp.dot(a, b, preferred_element_type=F32)


def exact_dot(a, b):
    return jnp.dot(a, b, precision=lax.Precision.HIGHEST, preferred_element_type=F32)


def upward_dot(values, table_ref):
    high, low = parts(values)
    count, depth = values.shape
    both = dot(jnp.concatenate([high, low], axis=0), table_ref[:depth])
    return both[:count] + both[count:] + dot(high, table_ref[depth:])


def north_dot(table_ref, values):
    north = values.shape[0]
    solved = dot(table_ref[...], jnp.concatenate(parts(values), axis=0))
    return solved[:north] + solved[north:]


def pick(column, me):
    value = float(column[0])
    for k in range(1, len(column)):
        value = jnp.where(me == k, float(column[k]), value)
    return value


def send_all(ends, table, me, out_refs):
    for d, out_ref in enumerate(out_refs):
        out_ref[...] = pick(table[:, 2 * d], me) * ends[0] + pick(table[:, 2 * d + 1], me) * ends[1]


def take_all(ends, table, me, messages):
    left = right = 0.0
    for d, message in enumerate(messages):
        left += pick(table[:, 8 + 2 * d], me) * message
        right += pick(table[:, 9 + 2 * d], me) * message
    known = (left, right) + tuple(ends)
    return [sum(pick(table[:, 4 * side + k], me) * known[k] for k in range(4)) for side in range(2)]


def diagonal(size):
    return lax.broadcasted_iota(jnp.int32, (size, size), 0) == lax.broadcasted_iota(jnp.int32, (size, size), 1)


def as_row(column):
    return jnp.sum(jnp.where(diagonal(column.shape[0]), column, 0.0), axis=0, keepdims=True)


def as_column(row):
    return jnp.sum(jnp.where(diagonal(row.shape[1]), row, 0.0), axis=1, keepdims=True)


def stacked(rows, height):
    filler = jnp.zeros((height - sum(row.shape[0] for row in rows), rows[0].shape[1]), F32)
    return jnp.concatenate(list(rows) + [filler], axis=0)


def ordered(pair, east):
    if not pair:
        return lambda i: i
    flip = lax.axis_index("gx")
    return lambda i: jnp.where(flip == 0, i, east - 1 - i)


def end_places(count, east):
    if count == 1:
        return [(east - 1, 0)]
    return [(0, 0), (east - 1, 1)]


def local_kernel(
    pair, group, factors, sending,
    tables_hbm, warmth_hbm, supply_hbm,
    swept_ref, warmth_ref, upward_ends_ref, north_ends_ref, east_ends_ref, *rest,
):
    to_up = sending.shape[1] // 2
    up_refs = rest[:to_up]
    supply_ref, both_ref, edges_ref, tables_ref, up_ref, north_ref, even_ref, odd_ref, sems = rest[to_up:]
    east, north, upward = supply_ref.shape
    groups = east // group
    count = east_ends_ref.shape[0]
    place = ordered(pair, east)

    def fetch(which, g):
        start = jnp.minimum(place(g * group), place(g * group + group - 1))
        block = pl.ds(start, group)
        if which == 0:
            return pltpu.make_async_copy(warmth_hbm.at[block], warmth_ref.at[pl.ds(start + 1, group)], sems.at[0, g])
        return pltpu.make_async_copy(supply_hbm.at[block], supply_ref.at[block], sems.at[1, g])

    def begin(g):
        for which in range(2):
            fetch(which, g).start()

    ahead = 2
    tables = pltpu.make_async_copy(tables_hbm, tables_ref, sems.at[0, groups])
    tables.start()
    for g in range(min(ahead, groups)):
        begin(g)
    warmth_ref[0] = jnp.zeros((north, upward), F32)
    warmth_ref[east + 1] = jnp.zeros((north, upward), F32)
    both_ref[...] = jnp.zeros_like(both_ref)
    east_ends_ref[...] = jnp.zeros_like(east_ends_ref)
    lane = lax.broadcasted_iota(jnp.int32, (1, 2 * east), 1)
    line = lax.broadcasted_iota(jnp.int32, (8, 1), 0)
    half_factor = 0.5 * factors[0]
    tables.wait()
    up_ref[...] = tables_ref[: 2 * upward].astype(BF16)
    north_ref[...] = tables_ref[2 * upward : 2 * upward + 2 * north, : 2 * north].astype(BF16)
    sweep = 2 * upward + 2 * north
    fetch(0, 0).wait()

    def arrive(g):
        fetch(1, g).wait()

        @pl.when(g + 1 < groups)
        def _():
            fetch(0, g + 1).wait()

        @pl.when(g + ahead < groups)
        def _():
            begin(g + ahead)

    def shifted(values, step):
        turned = pltpu.roll(values, step % north, 0)
        if step > 0:
            return jnp.concatenate([jnp.where(line == 0, 0.0, turned[:8]), turned[8:]], axis=0)
        return jnp.concatenate([turned[:-8], jnp.where(line == 7, 0.0, turned[-8:])], axis=0)

    def upward_part(g, slot_ref):
        heat_list = []
        for k in range(group):
            i = g * group + k
            x = place(i)
            warm = warmth_ref[x + 1]
            bent = (warmth_ref[x] - warm) + (warmth_ref[x + 2] - warm)
            across = (shifted(warm, 1) - warm) + (shifted(warm, -1) - warm)
            heat_list.append((supply_ref[x] + 2.0 * warm) + (factors[0] * bent + factors[1] * across))
            edges_ref[pl.ds(i, 1)] = warm[:1]
            edges_ref[pl.ds(east + i, 1)] = warm[north - 1 :]
        slot_ref[...] = upward_dot(jnp.concatenate(heat_list, axis=0), up_ref)

    def north_part(g, slot_ref):
        for k in range(group):
            i = g * group + k
            first = slot_ref[k * north : (k + 1) * north]
            both = jnp.where(lane < east, first[:, : 2 * east], first[:, upward - 2 * east :])
            both = pltpu.roll(both, i, 1)
            both_ref[0] = jnp.where(lane == i, both, both_ref[0])
            both_ref[1] = jnp.where(lane == lax.rem(i + 2 * east - 1, 2 * east), both, both_ref[1])
            solved = north_dot(north_ref, first - 2.0 * warmth_ref[place(i) + 1])
            north_ends_ref[0, pl.ds(i, 1)] = half_factor * solved[:1]
            north_ends_ref[1, pl.ds(i, 1)] = half_factor * solved[north - 1 :]
            swept = solved + tables_ref[pl.ds(sweep + i, 1), :] * east_ends_ref[count - 1]
            swept_ref[i] = swept
            east_ends_ref[count - 1] = swept
            if not pair:
                east_ends_ref[0] += tables_ref[pl.ds(sweep + east + i, 1), :] * swept

    arrive(0)
    upward_part(0, even_ref)

    def body(j, _):
        g = 2 * j
        arrive(g + 1)
        upward_part(g + 1, odd_ref)
        north_part(g, even_ref)
        arrive(g + 2)
        upward_part(g + 2, even_ref)
        north_part(g + 1, odd_ref)
        return 0

    lax.fori_loop(0, groups // 2 - 1, body, 0)
    arrive(groups - 1)
    upward_part(groups - 1, odd_ref)
    north_part(groups - 2, even_ref)
    north_part(groups - 1, odd_ref)

    ends = end_places(count, east)
    planes = [warmth_ref[place(i) + 1] for i, _ in ends]
    solved_up = upward_dot(jnp.concatenate([edges_ref[...]] + planes, axis=0), up_ref)
    east_ends_ref[count - 1] = tables_ref[sweep + 2 * east : sweep + 2 * east + 1, :] * east_ends_ref[count - 1]
    height = north_ends_ref.shape[1]
    rows = [[], []]
    for p in range(count):
        solved = half_factor * north_dot(north_ref, solved_up[2 * east + p * north : 2 * east + (p + 1) * north])
        rows[0].append(solved[:1])
        rows[1].append(solved[north - 1 :])
        east_ends_ref[p] += 2.0 * solved
    for end in range(2):
        north_ends_ref[end, :east] += 2.0 * solved_up[end * east : (end + 1) * east]
        north_ends_ref[end, east:] = stacked(rows[end], height - east)

    half = north // 2
    folded = []
    for end in range(2):
        top, bottom = both_ref[end, :half], both_ref[end, half:]
        top, bottom = pltpu.roll(top, end, 1), pltpu.roll(bottom, east + end, 1)
        folded.append(jnp.where(lane < east, top, bottom))
    upward_ends = []
    for end, column in enumerate((slice(0, 1), slice(upward - 1, upward))):
        extra = [as_row(solved_up[k * north : (k + 1) * north, column]) for k in range(1 + count)]
        upward_ends.append(stacked([folded[end]] + extra, upward_ends_ref.shape[1]))
        upward_ends_ref[end] = upward_ends[end]
    send_all(upward_ends, sending, lax.axis_index("gz"), up_refs)


def upward_kernel(
    count, taking, sending,
    ends_ref, north_ends_ref, north_inverse_ref, east_twice_ref, spread_ref, *rest,
):
    taken = (taking.shape[1] - 8) // 2
    message_refs = rest[:taken]
    columns_ref, north_out_ref, plane_ref, *out_refs = rest[taken:]
    north, lanes = columns_ref.shape
    east, half = lanes // 2, north // 2
    lane = lax.broadcasted_iota(jnp.int32, (1, lanes), 1)
    before, after = take_all(
        (ends_ref[0], ends_ref[1]), taking, lax.axis_index("gz"), [ref[...] for ref in message_refs]
    )

    def paired(end, rows):
        if end == 0:
            return jnp.where(lane < east, before[rows], pltpu.roll(after[rows], east, 1))
        return jnp.where(lane < east, pltpu.roll(before[rows], east, 1), after[rows])

    solved = exact_dot(north_inverse_ref[...], jnp.concatenate([paired(0, slice(0, half)), paired(1, slice(0, half))], axis=0))
    columns = exact_dot(solved, east_twice_ref[...])
    columns_ref[...] = columns
    planes = []
    for p in range(count):
        row = slice(half + 1 + p, half + 2 + p)
        planes.append([
            jnp.sum(north_inverse_ref[...] * side[row], axis=1, keepdims=True) for side in (before, after)
        ])
    height = north_ends_ref.shape[1]
    shape = (height, lanes)
    row = lax.broadcasted_iota(jnp.int32, shape, 0)
    short = lax.broadcasted_iota(jnp.int32, shape, 1) % east
    own = (row < east) & (short == row)
    behind = (row >= east) & (row < east + count) & (short == row - east)
    picked = []
    for end, y in enumerate((0, north - 1)):
        first = solved[y : y + 1] + 2.0 * paired(end, slice(half, half + 1))
        second = jnp.zeros((1, lanes), F32)
        for _, k in end_places(count, east):
            for side in range(2):
                second = jnp.where(lane == side * east + k, planes[k][side][y : y + 1], second)
        picked.append(jnp.where(own, first, 0.0) + jnp.where(behind, second, 0.0))
    added = exact_dot(jnp.concatenate(picked, axis=0), spread_ref[...])
    ends = []
    for end in range(2):
        ends.append(north_ends_ref[end] + added[end * height : (end + 1) * height])
        north_out_ref[end] = ends[end]
    send_all(ends, sending, lax.axis_index("gy"), out_refs)
    for i, k in end_places(count, east):
        rows = []
        for side in range(2):
            rows.append(as_row(columns[:, side * east + i : side * east + i + 1] + 2.0 * planes[k][side]))
        plane_ref[k] = stacked(rows, 8)


def north_kernel(
    count, taking,
    ends_ref, plane_ref, east_inverse_ref, *rest,
):
    taken = (taking.shape[1] - 8) // 2
    message_refs = rest[:taken]
    rows_ref, small_ref = rest[taken:]
    _, east, upward = rows_ref.shape
    sides = take_all((ends_ref[0], ends_ref[1]), taking, lax.axis_index("gy"), [ref[...] for ref in message_refs])
    swept = [exact_dot(east_inverse_ref[...], side[:east]) for side in sides]
    for n in range(2):
        rows_ref[n] = swept[n]
    for i, k in end_places(count, east):
        rows = [swept[n][i : i + 1] + 2.0 * sides[n][east + k : east + k + 1] for n in range(2)]
        wide = jnp.concatenate([plane_ref[k], jnp.zeros((8, upward - plane_ref.shape[2]), F32)], axis=1)
        small_ref[k] = stacked(rows + [wide[:2]], 8)


def final_kernel(
    pair, table, tile,
    sweep_ref, own_ref, other_ref, own_small_ref, other_small_ref,
    swept_ref, warmth_ref, columns_ref, rows_ref, upward_spikes_ref, north_spikes_ref,
    out_hbm,
    out_ref, sides_ref, sems,
):
    east, north, upward = out_ref.shape
    place = ordered(pair, east)

    def widened(plane, small):
        for side in range(2):
            plane += north_spikes_ref[side] * small[side : side + 1]
            plane += as_column(small[2 + side : 3 + side, :north]) * upward_spikes_ref[side : side + 1, :]
        return plane

    if pair:
        near, far = float(table[0]), float(table[1])
        sides_ref[0] = widened(
            near * other_ref[0] + far * own_ref[0], near * other_small_ref[0] + far * own_small_ref[0]
        )
    else:
        me = lax.axis_index("gx")
        members = table.shape[0]
        for side in range(2):
            plane, small = 0.0, 0.0
            for m in range(members):
                for end in range(2):
                    weight = pick(table[:, side, 2 * m + end], me)
                    plane += weight * other_ref[m, end]
                    small += weight * other_small_ref[m, end]
            sides_ref[side] = widened(plane, small)
    last = sides_ref.shape[0] - 1

    def send(t):
        block = pl.ds(pl.multiple_of(t * tile, tile), tile)
        return pltpu.make_async_copy(out_ref.at[:, block], out_hbm.at[:, block], sems.at[t])

    def body(t, _):
        block = pl.ds(pl.multiple_of(t * tile, tile), tile)
        value = sides_ref[last, block]
        columns = columns_ref[block]
        first_spike, last_spike = north_spikes_ref[0, block], north_spikes_ref[1, block]
        for i in reversed(range(east)):
            value = sweep_ref[0, i] * (swept_ref[i, block] + value)
            if not pair:
                value += sweep_ref[2, i] * sides_ref[0, block]
            added = (
                columns[:, i : i + 1] * upward_spikes_ref[0:1, :]
                + columns[:, east + i : east + i + 1] * upward_spikes_ref[1:2, :]
            )
            added += first_spike * rows_ref[0, i : i + 1, :] + last_spike * rows_ref[1, i : i + 1, :]
            x = place(i)
            out_ref[x, block] = warmth_ref[x + 1, block] + value + added
        send(t).start()
        return 0

    lax.fori_loop(0, north // tile, body, 0)
    for t in range(north // tile):
        send(t).wait()


def spread_out(messages, axis):
    members = lax.axis_size(axis)
    taken = [
        lax.ppermute(messages[d], axis, [(k, peers(k, members, d + 1)[0]) for k in range(members)])
        for d in reversed(range(len(messages)))
    ]
    return taken[::-1]


def local(initial_warmth, heat_supply):
    shape = east, north, upward = initial_warmth.shape
    members = [lax.axis_size(axis) for axis in ("gx", "gy", "gz")]
    factors = [float((n * m) ** 2 // 4) for n, m in zip(shape, members)]
    lines = [line_tables(n, factor) for n, factor in zip(shape, factors)]
    sweep = sweep_table(east, factors[0])
    ratio, weights = sweep[:2]
    sweep = sweep.astype(np.float32)
    exchanges = [exchange_tables(line[1], line[2], m) for line, m in zip(lines, members)]
    upward_high, upward_low = split(lines[2][0], 0)
    north_high, north_low = split(lines[1][0] / (0.5 * factors[0]), 1)
    north_stack = np.block([[north_high, north_high], [north_low, np.zeros_like(north_low)]])
    tables = np.concatenate([
        np.concatenate([upward_high, upward_low]).astype(np.float32),
        np.pad(north_stack.astype(np.float32), ((0, 0), (0, max(upward - 2 * north, 0)))),
        np.repeat(np.concatenate([[0.0], ratio[:-1], weights, ratio[-1:], np.zeros(7)])[:, None], upward, axis=1).astype(np.float32),
    ])
    east_inverse = lines[0][0].astype(np.float32)
    north_inverse = lines[1][0].astype(np.float32)
    east_twice = np.kron(np.eye(2), lines[0][0]).astype(np.float32)
    upward_spikes = np.stack(lines[2][1:]).astype(np.float32)
    spread = np.repeat(upward_spikes, east, axis=0)
    north_spikes = np.broadcast_to(np.stack(lines[1][1:])[:, :, None], (2, north, upward)).astype(np.float32)

    pair = members[0] == 2
    count = 1 if pair else 2
    height = east + 8
    to_up, to_north = members[2] - 1, members[1] - 1
    vmem = pl.BlockSpec(memory_space=pltpu.VMEM)
    smem = pl.BlockSpec(memory_space=pltpu.SMEM)
    hbm = pl.BlockSpec(memory_space=pltpu.HBM)

    def kept(*sizes):
        return jax.ShapeDtypeStruct(sizes, F32)

    group = 8
    folded = kept(north // 2 + 8, 2 * east)
    swept, warmth, upward_ends, north_ends, own, *messages = pl.pallas_call(
        functools.partial(local_kernel, pair, group, factors, exchanges[2][0]),
        in_specs=[hbm] * 3,
        out_specs=[vmem] * (5 + to_up),
        out_shape=[
            pltpu.VMEM(shape, F32),
            pltpu.VMEM((east + 2, north, upward), F32),
            kept(2, *folded.shape),
            kept(2, height, upward),
            kept(count, north, upward),
        ]
        + [folded] * to_up,
        scratch_shapes=[
            pltpu.VMEM(shape, F32),
            pltpu.VMEM((2, north, 2 * east), F32),
            pltpu.VMEM((2 * east, upward), F32),
            pltpu.VMEM(tables.shape, F32),
            pltpu.VMEM((2 * upward, upward), BF16),
            pltpu.VMEM((2 * north, 2 * north), BF16),
            pltpu.VMEM((group * north, upward), F32),
            pltpu.VMEM((group * north, upward), F32),
            pltpu.SemaphoreType.DMA((2, east // group + 1)),
        ],
        compiler_params=pltpu.CompilerParams(vmem_limit_bytes=32 * MIB),
    )(pltpu.with_memory_space_constraint(jnp.asarray(tables), pltpu.HBM), initial_warmth, heat_supply)

    messages = spread_out(messages, "gz")
    if pair:
        other = lax.ppermute(own, "gx", [(0, 1), (1, 0)])
    else:
        other = lax.all_gather(own, "gx")
    columns, north_ends, planes, *messages = pl.pallas_call(
        functools.partial(upward_kernel, count, exchanges[2][1], exchanges[1][0]),
        in_specs=[vmem] * (5 + to_up),
        out_specs=[vmem] * (3 + to_north),
        out_shape=[kept(north, 2 * east), kept(2, height, upward), kept(count, 8, north)]
        + [kept(height, upward)] * to_north,
        compiler_params=pltpu.CompilerParams(vmem_limit_bytes=6 * MIB),
    )(upward_ends, north_ends, north_inverse, east_twice, spread, *messages)

    messages = spread_out(messages, "gy")
    rows, own_small = pl.pallas_call(
        functools.partial(north_kernel, count, exchanges[1][1]),
        in_specs=[vmem] * (3 + to_north),
        out_specs=[vmem] * 2,
        out_shape=[kept(2, east, upward), kept(count, 8, upward)],
        compiler_params=pltpu.CompilerParams(vmem_limit_bytes=6 * MIB),
    )(north_ends, planes, east_inverse, *messages)

    if pair:
        other_small = lax.ppermute(own_small, "gx", [(0, 1), (1, 0)])
        near = lines[0][1][0]
        table = np.array([1.0, near]) / (1.0 - near**2)
    else:
        other_small = lax.all_gather(own_small, "gx")
        table = interface_table(lines[0][1], lines[0][2], members[0])
    swept = pltpu.with_memory_space_constraint(swept, pltpu.VMEM)
    warmth = pltpu.with_memory_space_constraint(warmth, pltpu.VMEM)
    tile = 32
    return pl.pallas_call(
        functools.partial(final_kernel, pair, table, tile),
        in_specs=[smem] + [vmem] * 10,
        out_specs=hbm,
        out_shape=kept(*shape),
        scratch_shapes=[
            pltpu.VMEM(shape, F32),
            pltpu.VMEM((count, north, upward), F32),
            pltpu.SemaphoreType.DMA((north // tile,)),
        ],
        compiler_params=pltpu.CompilerParams(vmem_limit_bytes=16 * MIB),
    )(sweep, own, other, own_small, other_small, swept, warmth, columns, rows, upward_spikes, north_spikes)


def solution(mesh):
    return jax.shard_map(
        local,
        mesh=mesh,
        in_specs=(P("gx", "gy", "gz"), P("gx", "gy", "gz")),
        out_specs=P("gx", "gy", "gz"),
        check_vma=False,
    )
```

```python
import functools

import jax
import jax.numpy as jnp
import numpy as np
from jax import lax
from jax.experimental import pallas as pl
from jax.experimental.pallas import tpu as pltpu
from jax.sharding import PartitionSpec as P

F32 = jnp.float32
BF16 = jnp.bfloat16
MIB = 1 << 20


def line_tables(length, factor):
    matrix = (1.0 + factor) * np.eye(length)
    matrix -= 0.5 * factor * (np.eye(length, k=1) + np.eye(length, k=-1))
    inverse = np.linalg.inv(matrix)
    inverse = 0.5 * (inverse + inverse.T)
    return inverse, 0.5 * factor * inverse[:, 0], 0.5 * factor * inverse[:, -1]


def chain_system(near, far, members):
    system = np.eye(2 * members)
    for m in range(members):
        if m > 0:
            system[2 * m, 2 * m - 1] -= near
            system[2 * m + 1, 2 * m - 1] -= far
        if m < members - 1:
            system[2 * m, 2 * m + 2] -= far
            system[2 * m + 1, 2 * m + 2] -= near
    return np.linalg.inv(system)


def interface_table(before, after, members):
    solved = chain_system(before[0], before[-1], members)
    rows = np.zeros((members, 2, 2 * members))
    for m in range(members):
        if m > 0:
            rows[m, 0] = solved[2 * m - 1]
        if m < members - 1:
            rows[m, 1] = solved[2 * m + 2]
    return rows


def peers(member, members, distance):
    if members & (members - 1) == 0:
        return member ^ distance, member ^ distance
    return (member + distance) % members, (member - distance) % members


def exchange_tables(before, after, members):
    near, far = before[0], before[-1]
    sending = np.zeros((members, 2 * (members - 1)))
    taking = np.zeros((members, 8 + 2 * (members - 1)))
    for m in range(members):
        right = chain_system(near, far, members - 1 - m)
        left = chain_system(near, far, m)
        for d in range(1, members):
            k = peers(m, members, d)[1]
            if k > m:
                sending[k, 2 * d - 2 : 2 * d] = right[0, 2 * (k - m - 1) : 2 * (k - m)]
                taking[m, 8 + 2 * d - 1] = 1.0
            else:
                sending[k, 2 * d - 2 : 2 * d] = left[-1, 2 * k : 2 * k + 2]
                taking[m, 8 + 2 * d - 2] = 1.0
        pull_left = answer(near, far, m)
        pull_right = answer(near, far, members - 1 - m)
        system = np.array([
            [1.0, 0.0, -pull_left, 0.0],
            [0.0, 1.0, 0.0, -pull_right],
            [-near, -far, 1.0, 0.0],
            [-far, -near, 0.0, 1.0],
        ])
        taking[m, :8] = np.linalg.inv(system)[:2].reshape(8)
    return sending, taking


def answer(near, far, members):
    if members == 0:
        return 0.0
    push = np.zeros(2 * members)
    push[0], push[1] = near, far
    return chain_system(near, far, members)[0] @ push


def sweep_table(length, factor):
    half = 0.5 * factor
    ratio = np.zeros(length)
    last = 0.0
    for i in range(length):
        ratio[i] = last = half / (1.0 + factor - half * last)
    decay = np.cumprod(ratio)
    return np.stack([ratio, decay, decay])


def split(table, axis):
    rows = np.moveaxis(np.asarray(table, np.float64), axis, 0)
    high = np.zeros(rows.shape, BF16)
    carried = np.zeros(rows.shape[1:])
    for k, row in enumerate(rows):
        high[k] = (row + carried).astype(np.float32).astype(BF16)
        carried = carried + row - high[k].astype(np.float64)
    low = (rows - high.astype(np.float64)).astype(np.float32).astype(BF16)
    return np.moveaxis(high, 0, axis), np.moveaxis(low, 0, axis)


def parts(values):
    high = values.astype(BF16)
    return high, (values - high.astype(F32)).astype(BF16)


def dot(a, b):
    return jnp.dot(a, b, preferred_element_type=F32)


def exact_dot(a, b):
    return jnp.dot(a, b, precision=lax.Precision.HIGHEST, preferred_element_type=F32)


def upward_dot(values, table_ref):
    high, low = parts(values)
    count, depth = values.shape
    both = dot(jnp.concatenate([high, low], axis=0), table_ref[:depth])
    return both[:count] + both[count:] + dot(high, table_ref[depth:])


def north_dot(table_ref, values):
    north = values.shape[0]
    solved = dot(table_ref[...], jnp.concatenate(parts(values), axis=0))
    return solved[:north] + solved[north:]


def pick(column, me):
    value = float(column[0])
    for k in range(1, len(column)):
        value = jnp.where(me == k, float(column[k]), value)
    return value


def send_all(ends, table, me, out_refs):
    for d, out_ref in enumerate(out_refs):
        out_ref[...] = pick(table[:, 2 * d], me) * ends[0] + pick(table[:, 2 * d + 1], me) * ends[1]


def take_all(ends, table, me, messages):
    left = right = 0.0
    for d, message in enumerate(messages):
        left += pick(table[:, 8 + 2 * d], me) * message
        right += pick(table[:, 9 + 2 * d], me) * message
    known = (left, right) + tuple(ends)
    return [sum(pick(table[:, 4 * side + k], me) * known[k] for k in range(4)) for side in range(2)]


def diagonal(size):
    return lax.broadcasted_iota(jnp.int32, (size, size), 0) == lax.broadcasted_iota(jnp.int32, (size, size), 1)


def as_row(column):
    return jnp.sum(jnp.where(diagonal(column.shape[0]), column, 0.0), axis=0, keepdims=True)


def as_column(row):
    return jnp.sum(jnp.where(diagonal(row.shape[1]), row, 0.0), axis=1, keepdims=True)


def stacked(rows, height):
    filler = jnp.zeros((height - sum(row.shape[0] for row in rows), rows[0].shape[1]), F32)
    return jnp.concatenate(list(rows) + [filler], axis=0)


def ordered(pair, east):
    if not pair:
        return lambda i: i
    flip = lax.axis_index("gx")
    return lambda i: jnp.where(flip == 0, i, east - 1 - i)


def end_places(count, east):
    if count == 1:
        return [(east - 1, 0)]
    return [(0, 0), (east - 1, 1)]


def local_kernel(
    pair, group, piece, factors, sending,
    tables_hbm, warmth_hbm, supply_hbm,
    swept_ref, warmth_ref, upward_ends_ref, north_ends_ref, east_ends_ref, *rest,
):
    to_up = sending.shape[1] // 2
    up_refs = rest[:to_up]
    supply_ref, both_ref, edges_ref, tables_ref, up_ref, north_ref, even_ref, odd_ref, sems = rest[to_up:]
    east, north, upward = supply_ref.shape
    groups = east // group
    count = east_ends_ref.shape[0]
    place = ordered(pair, east)

    def fetch(which, b):
        start = jnp.minimum(place(b * piece), place(b * piece + piece - 1))
        block = pl.ds(start, piece)
        if which == 0:
            return pltpu.make_async_copy(warmth_hbm.at[block], warmth_ref.at[pl.ds(start + 1, piece)], sems.at[0, b])
        return pltpu.make_async_copy(supply_hbm.at[block], supply_ref.at[block], sems.at[1, b])

    blocks = east // piece
    tables = pltpu.make_async_copy(tables_hbm, tables_ref, sems.at[0, blocks])
    for b in range(blocks):
        for which in range(2):
            fetch(which, b).start()
        if b == 1:
            tables.start()
    warmth_ref[0] = jnp.zeros((north, upward), F32)
    warmth_ref[east + 1] = jnp.zeros((north, upward), F32)
    both_ref[...] = jnp.zeros_like(both_ref)
    east_ends_ref[...] = jnp.zeros_like(east_ends_ref)
    lane = lax.broadcasted_iota(jnp.int32, (1, 2 * east), 1)
    line = lax.broadcasted_iota(jnp.int32, (8, 1), 0)
    half_factor = 0.5 * factors[0]
    def settle_tables():
        tables.wait()
        up_ref[...] = tables_ref[: 2 * upward].astype(BF16)
        north_ref[...] = tables_ref[2 * upward : 2 * upward + 2 * north, : 2 * north].astype(BF16)
    sweep = 2 * upward + 2 * north
    fetch(0, 0).wait()

    def arrive_block(b):
        fetch(1, b).wait()

        @pl.when(b + 1 < blocks)
        def _():
            fetch(0, b + 1).wait()

    def arrive(g):
        for c in range(group // piece):
            arrive_block(g * (group // piece) + c)

    def shifted(values, step):
        turned = pltpu.roll(values, step % north, 0)
        if step > 0:
            return jnp.concatenate([jnp.where(line == 0, 0.0, turned[:8]), turned[8:]], axis=0)
        return jnp.concatenate([turned[:-8], jnp.where(line == 7, 0.0, turned[-8:])], axis=0)

    def upward_part(g, slot_ref, first=False):
        heat_list = []
        for k in range(group):
            if first and k % piece == 0:
                arrive_block(k // piece)
            i = g * group + k
            x = place(i)
            warm = warmth_ref[x + 1]
            bent = (warmth_ref[x] - warm) + (warmth_ref[x + 2] - warm)
            across = (shifted(warm, 1) - warm) + (shifted(warm, -1) - warm)
            heat_list.append((supply_ref[x] + 2.0 * warm) + (factors[0] * bent + factors[1] * across))
            edges_ref[pl.ds(i, 1)] = warm[:1]
            edges_ref[pl.ds(east + i, 1)] = warm[north - 1 :]
        if first:
            settle_tables()
        slot_ref[...] = upward_dot(jnp.concatenate(heat_list, axis=0), up_ref)

    def north_part(g, slot_ref):
        for k in range(group):
            i = g * group + k
            first = slot_ref[k * north : (k + 1) * north]
            both = jnp.where(lane < east, first[:, : 2 * east], first[:, upward - 2 * east :])
            both = pltpu.roll(both, i, 1)
            both_ref[0] = jnp.where(lane == i, both, both_ref[0])
            both_ref[1] = jnp.where(lane == lax.rem(i + 2 * east - 1, 2 * east), both, both_ref[1])
            solved = north_dot(north_ref, first - 2.0 * warmth_ref[place(i) + 1])
            north_ends_ref[0, pl.ds(i, 1)] = half_factor * solved[:1]
            north_ends_ref[1, pl.ds(i, 1)] = half_factor * solved[north - 1 :]
            swept = solved + tables_ref[pl.ds(sweep + i, 1), :] * east_ends_ref[count - 1]
            swept_ref[i] = swept
            east_ends_ref[count - 1] = swept
            if not pair:
                east_ends_ref[0] += tables_ref[pl.ds(sweep + east + i, 1), :] * swept

    upward_part(0, even_ref, first=True)

    def body(j, _):
        g = 2 * j
        arrive(g + 1)
        upward_part(g + 1, odd_ref)
        north_part(g, even_ref)
        arrive(g + 2)
        upward_part(g + 2, even_ref)
        north_part(g + 1, odd_ref)
        return 0

    lax.fori_loop(0, groups // 2 - 1, body, 0)
    arrive(groups - 1)
    upward_part(groups - 1, odd_ref)
    north_part(groups - 2, even_ref)
    north_part(groups - 1, odd_ref)

    ends = end_places(count, east)
    planes = [warmth_ref[place(i) + 1] for i, _ in ends]
    solved_up = upward_dot(jnp.concatenate([edges_ref[...]] + planes, axis=0), up_ref)
    east_ends_ref[count - 1] = tables_ref[sweep + 2 * east : sweep + 2 * east + 1, :] * east_ends_ref[count - 1]
    height = north_ends_ref.shape[1]
    rows = [[], []]
    for p in range(count):
        solved = half_factor * north_dot(north_ref, solved_up[2 * east + p * north : 2 * east + (p + 1) * north])
        rows[0].append(solved[:1])
        rows[1].append(solved[north - 1 :])
        east_ends_ref[p] += 2.0 * solved
    for end in range(2):
        north_ends_ref[end, :east] += 2.0 * solved_up[end * east : (end + 1) * east]
        north_ends_ref[end, east:] = stacked(rows[end], height - east)

    half = north // 2
    folded = []
    for end in range(2):
        top, bottom = both_ref[end, :half], both_ref[end, half:]
        top, bottom = pltpu.roll(top, end, 1), pltpu.roll(bottom, east + end, 1)
        folded.append(jnp.where(lane < east, top, bottom))
    upward_ends = []
    for end, column in enumerate((slice(0, 1), slice(upward - 1, upward))):
        extra = [as_row(solved_up[k * north : (k + 1) * north, column]) for k in range(1 + count)]
        upward_ends.append(stacked([folded[end]] + extra, upward_ends_ref.shape[1]))
        upward_ends_ref[end] = upward_ends[end]
    send_all(upward_ends, sending, lax.axis_index("gz"), up_refs)


def upward_kernel(
    count, taking, sending,
    ends_ref, north_ends_ref, north_inverse_ref, east_twice_ref, spread_ref, *rest,
):
    taken = (taking.shape[1] - 8) // 2
    message_refs = rest[:taken]
    columns_ref, north_out_ref, plane_ref, *out_refs = rest[taken:]
    north, lanes = columns_ref.shape
    east, half = lanes // 2, north // 2
    lane = lax.broadcasted_iota(jnp.int32, (1, lanes), 1)
    before, after = take_all(
        (ends_ref[0], ends_ref[1]), taking, lax.axis_index("gz"), [ref[...] for ref in message_refs]
    )

    def paired(end, rows):
        if end == 0:
            return jnp.where(lane < east, before[rows], pltpu.roll(after[rows], east, 1))
        return jnp.where(lane < east, pltpu.roll(before[rows], east, 1), after[rows])

    solved = exact_dot(north_inverse_ref[...], jnp.concatenate([paired(0, slice(0, half)), paired(1, slice(0, half))], axis=0))
    columns = exact_dot(solved, east_twice_ref[...])
    columns_ref[...] = columns
    planes = []
    for p in range(count):
        row = slice(half + 1 + p, half + 2 + p)
        planes.append([
            jnp.sum(north_inverse_ref[...] * side[row], axis=1, keepdims=True) for side in (before, after)
        ])
    height = north_ends_ref.shape[1]
    shape = (height, lanes)
    row = lax.broadcasted_iota(jnp.int32, shape, 0)
    short = lax.broadcasted_iota(jnp.int32, shape, 1) % east
    own = (row < east) & (short == row)
    behind = (row >= east) & (row < east + count) & (short == row - east)
    picked = []
    for end, y in enumerate((0, north - 1)):
        first = solved[y : y + 1] + 2.0 * paired(end, slice(half, half + 1))
        second = jnp.zeros((1, lanes), F32)
        for _, k in end_places(count, east):
            for side in range(2):
                second = jnp.where(lane == side * east + k, planes[k][side][y : y + 1], second)
        picked.append(jnp.where(own, first, 0.0) + jnp.where(behind, second, 0.0))
    added = exact_dot(jnp.concatenate(picked, axis=0), spread_ref[...])
    ends = []
    for end in range(2):
        ends.append(north_ends_ref[end] + added[end * height : (end + 1) * height])
        north_out_ref[end] = ends[end]
    send_all(ends, sending, lax.axis_index("gy"), out_refs)
    for i, k in end_places(count, east):
        rows = []
        for side in range(2):
            rows.append(as_row(columns[:, side * east + i : side * east + i + 1] + 2.0 * planes[k][side]))
        plane_ref[k] = stacked(rows, 8)


def north_kernel(
    count, taking,
    ends_ref, plane_ref, east_inverse_ref, *rest,
):
    taken = (taking.shape[1] - 8) // 2
    message_refs = rest[:taken]
    rows_ref, small_ref = rest[taken:]
    _, east, upward = rows_ref.shape
    sides = take_all((ends_ref[0], ends_ref[1]), taking, lax.axis_index("gy"), [ref[...] for ref in message_refs])
    swept = [exact_dot(east_inverse_ref[...], side[:east]) for side in sides]
    for n in range(2):
        rows_ref[n] = swept[n]
    for i, k in end_places(count, east):
        rows = [swept[n][i : i + 1] + 2.0 * sides[n][east + k : east + k + 1] for n in range(2)]
        wide = jnp.concatenate([plane_ref[k], jnp.zeros((8, upward - plane_ref.shape[2]), F32)], axis=1)
        small_ref[k] = stacked(rows + [wide[:2]], 8)


def final_kernel(
    pair, table, tile,
    sweep_ref, own_ref, other_ref, own_small_ref, other_small_ref,
    swept_ref, warmth_ref, columns_ref, rows_ref, upward_spikes_ref, north_spikes_ref,
    out_hbm,
    out_ref, sides_ref, sems,
):
    east, north, upward = out_ref.shape
    place = ordered(pair, east)

    def widened(plane, small):
        for side in range(2):
            plane += north_spikes_ref[side] * small[side : side + 1]
            plane += as_column(small[2 + side : 3 + side, :north]) * upward_spikes_ref[side : side + 1, :]
        return plane

    if pair:
        near, far = float(table[0]), float(table[1])
        sides_ref[0] = widened(
            near * other_ref[0] + far * own_ref[0], near * other_small_ref[0] + far * own_small_ref[0]
        )
    else:
        me = lax.axis_index("gx")
        members = table.shape[0]
        for side in range(2):
            plane, small = 0.0, 0.0
            for m in range(members):
                for end in range(2):
                    weight = pick(table[:, side, 2 * m + end], me)
                    plane += weight * other_ref[m, end]
                    small += weight * other_small_ref[m, end]
            sides_ref[side] = widened(plane, small)
    last = sides_ref.shape[0] - 1

    def send(t):
        block = pl.ds(pl.multiple_of(t * tile, tile), tile)
        return pltpu.make_async_copy(out_ref.at[:, block], out_hbm.at[:, block], sems.at[t])

    def body(t, _):
        block = pl.ds(pl.multiple_of(t * tile, tile), tile)
        value = sides_ref[last, block]
        columns = columns_ref[block]
        first_spike, last_spike = north_spikes_ref[0, block], north_spikes_ref[1, block]
        for i in reversed(range(east)):
            value = sweep_ref[0, i] * (swept_ref[i, block] + value)
            if not pair:
                value += sweep_ref[2, i] * sides_ref[0, block]
            added = (
                columns[:, i : i + 1] * upward_spikes_ref[0:1, :]
                + columns[:, east + i : east + i + 1] * upward_spikes_ref[1:2, :]
            )
            added += first_spike * rows_ref[0, i : i + 1, :] + last_spike * rows_ref[1, i : i + 1, :]
            x = place(i)
            out_ref[x, block] = warmth_ref[x + 1, block] + value + added
        send(t).start()
        return 0

    lax.fori_loop(0, north // tile, body, 0)
    for t in range(north // tile):
        send(t).wait()


def spread_out(messages, axis):
    members = lax.axis_size(axis)
    taken = [
        lax.ppermute(messages[d], axis, [(k, peers(k, members, d + 1)[0]) for k in range(members)])
        for d in reversed(range(len(messages)))
    ]
    return taken[::-1]


def local(initial_warmth, heat_supply):
    shape = east, north, upward = initial_warmth.shape
    members = [lax.axis_size(axis) for axis in ("gx", "gy", "gz")]
    factors = [float((n * m) ** 2 // 4) for n, m in zip(shape, members)]
    lines = [line_tables(n, factor) for n, factor in zip(shape, factors)]
    sweep = sweep_table(east, factors[0])
    ratio, weights = sweep[:2]
    sweep = sweep.astype(np.float32)
    exchanges = [exchange_tables(line[1], line[2], m) for line, m in zip(lines, members)]
    upward_high, upward_low = split(lines[2][0], 0)
    north_high, north_low = split(lines[1][0] / (0.5 * factors[0]), 1)
    north_stack = np.block([[north_high, north_high], [north_low, np.zeros_like(north_low)]])
    tables = np.concatenate([
        np.concatenate([upward_high, upward_low]).astype(np.float32),
        np.pad(north_stack.astype(np.float32), ((0, 0), (0, max(upward - 2 * north, 0)))),
        np.repeat(np.concatenate([[0.0], ratio[:-1], weights, ratio[-1:], np.zeros(7)])[:, None], upward, axis=1).astype(np.float32),
    ])
    east_inverse = lines[0][0].astype(np.float32)
    north_inverse = lines[1][0].astype(np.float32)
    east_twice = np.kron(np.eye(2), lines[0][0]).astype(np.float32)
    upward_spikes = np.stack(lines[2][1:]).astype(np.float32)
    spread = np.repeat(upward_spikes, east, axis=0)
    north_spikes = np.broadcast_to(np.stack(lines[1][1:])[:, :, None], (2, north, upward)).astype(np.float32)

    pair = members[0] == 2
    count = 1 if pair else 2
    height = east + 8
    to_up, to_north = members[2] - 1, members[1] - 1
    vmem = pl.BlockSpec(memory_space=pltpu.VMEM)
    smem = pl.BlockSpec(memory_space=pltpu.SMEM)
    hbm = pl.BlockSpec(memory_space=pltpu.HBM)

    def kept(*sizes):
        return jax.ShapeDtypeStruct(sizes, F32)

    group, piece = 8, 4
    folded = kept(north // 2 + 8, 2 * east)
    swept, warmth, upward_ends, north_ends, own, *messages = pl.pallas_call(
        functools.partial(local_kernel, pair, group, piece, factors, exchanges[2][0]),
        in_specs=[hbm] * 3,
        out_specs=[vmem] * (5 + to_up),
        out_shape=[
            pltpu.VMEM(shape, F32),
            pltpu.VMEM((east + 2, north, upward), F32),
            kept(2, *folded.shape),
            kept(2, height, upward),
            kept(count, north, upward),
        ]
        + [folded] * to_up,
        scratch_shapes=[
            pltpu.VMEM(shape, F32),
            pltpu.VMEM((2, north, 2 * east), F32),
            pltpu.VMEM((2 * east, upward), F32),
            pltpu.VMEM(tables.shape, F32),
            pltpu.VMEM((2 * upward, upward), BF16),
            pltpu.VMEM((2 * north, 2 * north), BF16),
            pltpu.VMEM((group * north, upward), F32),
            pltpu.VMEM((group * north, upward), F32),
            pltpu.SemaphoreType.DMA((2, east // piece + 1)),
        ],
        compiler_params=pltpu.CompilerParams(vmem_limit_bytes=32 * MIB),
    )(pltpu.with_memory_space_constraint(jnp.asarray(tables), pltpu.HBM), initial_warmth, heat_supply)

    messages = spread_out(messages, "gz")
    if pair:
        other = lax.ppermute(own, "gx", [(0, 1), (1, 0)])
    else:
        other = lax.all_gather(own, "gx")
    columns, north_ends, planes, *messages = pl.pallas_call(
        functools.partial(upward_kernel, count, exchanges[2][1], exchanges[1][0]),
        in_specs=[vmem] * (5 + to_up),
        out_specs=[vmem] * (3 + to_north),
        out_shape=[kept(north, 2 * east), kept(2, height, upward), kept(count, 8, north)]
        + [kept(height, upward)] * to_north,
        compiler_params=pltpu.CompilerParams(vmem_limit_bytes=6 * MIB),
    )(upward_ends, north_ends, north_inverse, east_twice, spread, *messages)

    messages = spread_out(messages, "gy")
    rows, own_small = pl.pallas_call(
        functools.partial(north_kernel, count, exchanges[1][1]),
        in_specs=[vmem] * (3 + to_north),
        out_specs=[vmem] * 2,
        out_shape=[kept(2, east, upward), kept(count, 8, upward)],
        compiler_params=pltpu.CompilerParams(vmem_limit_bytes=6 * MIB),
    )(north_ends, planes, east_inverse, *messages)

    if pair:
        other_small = lax.ppermute(own_small, "gx", [(0, 1), (1, 0)])
        near = lines[0][1][0]
        table = np.array([1.0, near]) / (1.0 - near**2)
    else:
        other_small = lax.all_gather(own_small, "gx")
        table = interface_table(lines[0][1], lines[0][2], members[0])
    swept = pltpu.with_memory_space_constraint(swept, pltpu.VMEM)
    warmth = pltpu.with_memory_space_constraint(warmth, pltpu.VMEM)
    tile = 32
    return pl.pallas_call(
        functools.partial(final_kernel, pair, table, tile),
        in_specs=[smem] + [vmem] * 10,
        out_specs=hbm,
        out_shape=kept(*shape),
        scratch_shapes=[
            pltpu.VMEM(shape, F32),
            pltpu.VMEM((count, north, upward), F32),
            pltpu.SemaphoreType.DMA((north // tile,)),
        ],
        compiler_params=pltpu.CompilerParams(vmem_limit_bytes=16 * MIB),
    )(sweep, own, other, own_small, other_small, swept, warmth, columns, rows, upward_spikes, north_spikes)


def solution(mesh):
    return jax.shard_map(
        local,
        mesh=mesh,
        in_specs=(P("gx", "gy", "gz"), P("gx", "gy", "gz")),
        out_specs=P("gx", "gy", "gz"),
        check_vma=False,
    )
```
